32 devices in a mesh: rep: 2 (over y), shard: 16 (over z, x, core).
Axes of the slice: x: 2, y: 2, z: 4, core: 2. Of those that a mesh axis runs over, the one named last changes fastest.
Arguments:
- tokens: bfloat16 [16384, 960], P(('rep', 'shard')), may hold values from -6 to 6
- segment_ids: int32 [32, 512], P(('rep', 'shard')), may hold values from 0 to 1, as said below
- positions: int32 [32, 512], P(('rep', 'shard')), may hold values from 0 to 1534, as said below
- norm_attn: bfloat16 [960], P('shard'), may hold values from 0.099609375 to 1.8984375
- w_qkv: bfloat16 [960, 1600], P('shard')
- w_out: bfloat16 [960, 960], P('shard'), may hold values from -0.5 to 0.5
- norm_mlp: bfloat16 [960], P('shard'), may hold values from 0.099609375 to 1.8984375
- w_gate_up: bfloat16 [960, 5120], P('shard'), may hold values from -0.1875 to 0.1875
- w_down: bfloat16 [2560, 960], P('shard'), may hold values from -0.25 to 0.25
- cotangent: bfloat16 [16384, 960], P(('rep', 'shard')), may hold values from -6 to 6
Outputs:
- output: bfloat16 [16384, 960], P(('rep', 'shard'))
- input_grad: float32 [16384, 960], P(('rep', 'shard'))
- grad_norm_attn: float32 [960], P('shard')
- grad_qkv: float32 [960, 1600], P('shard')
- grad_out: float32 [960, 960], P('shard')
- grad_norm_mlp: float32 [960], P('shard')
- grad_gate_up: float32 [960, 5120], P('shard')
- grad_down: float32 [2560, 960], P('shard')
The draws below stay inside these ranges and needn't reach their ends.
Inputs may be any that keep to these rules, and one draw needn't show every extreme that they name: `segment_ids`: segment ids start at 0 in each sequence and rise by one at each new document; each sequence holds exactly 2 documents of one token or more. `positions`: a token's position within its document; the first document of a sequence starts at a position of 0 to 1024, every other document at 0.
All inputs are finite; a program needn't handle non-finite values.
Results may differ from the reference program's by a relative error of at most 0.015.
Values may be sent and summed in bfloat16 or wider, within the bound.
No kernel may reach another device: no remote copies, remote signals or barrier semaphores. Data moves between devices by JAX's collectives and lax.ppermute only.
A program may use at most 128 MiB of HBM per device.

```python
import math
import jax
import jax.numpy as jnp
from jax import lax

D = 960
HEADS = 15
KV_HEADS = 5
HD = 64
FF = 2560
LEN = 512
POS_OFF = 1024
DOCS = 2
SEQS = 32
TOKENS = 16384


def doc_layout(key):
    inner_key = jax.random.fold_in(key, 11)
    noise = jax.random.randint(jax.random.fold_in(inner_key, 1), (SEQS, LEN - 1), 0, 1 << 20)
    spots = jnp.arange(LEN - 1, dtype=jnp.int32)
    ranked = noise * LEN + spots[None, :]
    first_row = (LEN - 2 - spots)[None, :]
    row_ids = jnp.arange(SEQS, dtype=jnp.int32)[:, None]
    ranked = jnp.where(row_ids == 0, first_row, ranked)
    chosen_vals, chosen_idx = lax.top_k(-ranked, DOCS - 1)
    cut_points = chosen_idx.astype(jnp.int32) + 1
    places = jnp.arange(LEN, dtype=jnp.int32)
    passed = cut_points[:, None, :] <= places[None, :, None]
    seg_rows = jnp.sum(passed.astype(jnp.int32), -1)
    doc_start = jnp.max(jnp.where(passed, cut_points[:, None, :], 0), -1)
    first_offset = jax.random.randint(jax.random.fold_in(inner_key, 2), (SEQS, 1), 0, POS_OFF + 1)
    first_offset = jnp.where(row_ids == 0, POS_OFF, first_offset)
    pos_rows = places[None, :] - doc_start + jnp.where(seg_rows == 0, first_offset, 0)
    return (seg_rows.astype(jnp.int32), pos_rows.astype(jnp.int32))


def draw_segment_ids(key, part):
    return doc_layout(key)[0]


def draw_positions(key, part):
    return doc_layout(key)[1]


def draw_w_qkv(key, part):
    kv_width = KV_HEADS * HD
    base = jax.random.normal(jax.random.fold_in(key, 3), (D, D + 2 * kv_width), jnp.float32) * D ** (-0.5)
    return base.astype(jnp.bfloat16)


def block_levels(rng, extent, cuts, low, largest):
    level = 1.0
    for position, blocks in cuts:
        heights = jax.random.uniform(jax.random.fold_in(jax.random.fold_in(rng, 6), position), (blocks,), jnp.float32, low / len(cuts), largest / len(cuts))
        level = level * jnp.repeat(jnp.exp(heights), extent[position] // blocks).reshape((-1,) + (1,) * (len(extent) - 1 - position))
    return level


def centred(key, extent, spread, most, shards=(), kind=jnp.bfloat16):
    array = jax.random.normal(key, extent, jnp.float32) * spread
    if len(shards) > 0:
        array = block_levels(key, extent, shards, -0.22, 0.18) * array
    return jnp.clip(array, min=-most, max=most).astype(kind)


def setup_inputs(seed: int = 0) -> dict:
    splits = jax.random.split(jax.random.key(seed), 11)
    return {
        "tokens": centred(splits[0], (TOKENS, D), 1.0, 6.0, ((0, 32),)),
        "segment_ids": draw_segment_ids(jax.random.fold_in(splits[10], 71), 0),
        "positions": draw_positions(jax.random.fold_in(splits[10], 71), 0),
        "norm_attn": jnp.clip(1.0 + 0.18 * jax.random.normal(splits[3], (D,), jnp.float32), 0.099609375, 1.8984375).astype(jnp.bfloat16),
        "w_qkv": draw_w_qkv(jax.random.fold_in(splits[10], 71), 0),
        "w_out": centred(splits[5], (D, D), (D // 8) ** -0.5, 0.5, ((0, 16),)),
        "norm_mlp": jnp.clip(1.0 + 0.18 * jax.random.normal(splits[6], (D,), jnp.float32), 0.099609375, 1.8984375).astype(jnp.bfloat16),
        "w_gate_up": centred(splits[7], (D, 2 * FF), D ** -0.5, 0.1875, ((0, 16),)),
        "w_down": centred(splits[8], (FF, D), (FF // 4) ** -0.5, 0.25, ((0, 16),)),
        "cotangent": centred(splits[9], (TOKENS, D), 1.0, 6.0, ((0, 32),)),
    }


@jax.custom_vjp
def low(v):
    return lax.optimization_barrier(v.astype(jnp.bfloat16)).astype(jnp.float32)

@jax.custom_vjp
def low_back(v):
    return v

def low_keep(v):
    return (low(v), None)

def low_pass(kept, grad):
    return (grad,)

def back_keep(v):
    return (v, None)

def back_low(kept, grad):
    return (low(grad),)
low.defvjp(low_keep, low_pass)
low_back.defvjp(back_keep, back_low)
EPSILON = 1e-05
ROPE_BASE = 100000.0
NEG_FILL = -1e+30
HIGHEST = lax.Precision.HIGHEST

def rope_tables(places):
    half_dim = HD // 2
    freqs = ROPE_BASE ** (-2.0 * jnp.arange(half_dim, dtype=jnp.float32) / HD)
    angles = places.astype(jnp.float32)[..., None] * freqs
    return (jnp.cos(angles), jnp.sin(angles))

def rotate(values, cosine, sine):
    half_dim = values.shape[-1] // 2
    cosine = cosine[..., None, :]
    sine = sine[..., None, :]
    first_half = values[..., :half_dim]
    second_half = values[..., half_dim:]
    return jnp.concatenate([first_half * cosine - second_half * sine, second_half * cosine + first_half * sine], -1)

def rms_norm(values, gain):
    scale = lax.rsqrt(lax.optimization_barrier(jnp.mean(values * values, -1, keepdims=True)) + EPSILON)
    return values * scale * gain

def forward(hidden_in, gain_a, qkv_w, out_w, gain_m, gate_up_w, down_w, seg_rows, pos_rows):
    num_seqs, seq_len, model_width = hidden_in.shape
    kv_width = KV_HEADS * HD
    group_size = HEADS // KV_HEADS
    normed = low(rms_norm(hidden_in, gain_a))
    project = low_back(jnp.einsum('bld,de->ble', normed, qkv_w, precision=HIGHEST))
    queries = project[..., :model_width].reshape(num_seqs, seq_len, HEADS, HD)
    key_raw = project[..., model_width:model_width + kv_width].reshape(num_seqs, seq_len, KV_HEADS, HD)
    value_low = low(project[..., model_width + kv_width:].reshape(num_seqs, seq_len, KV_HEADS, HD))
    cosine, sine = rope_tables(pos_rows)
    query_rot = low(rotate(queries, cosine, sine))
    key_rot = low(rotate(key_raw, cosine, sine))
    key_all = jnp.repeat(key_rot, group_size, axis=2)
    value_all = jnp.repeat(value_low, group_size, axis=2)
    scores = low_back(jnp.einsum('blhe,bmhe->bhlm', query_rot, key_all, precision=HIGHEST) * 0.125)
    places = jnp.arange(seq_len)
    allowed = (seg_rows[:, :, None] == seg_rows[:, None, :]) & (places[None, None, :] <= places[None, :, None])
    scores = jnp.where(allowed[:, None], scores, NEG_FILL)
    attn_prob = jax.nn.softmax(scores, axis=-1)
    mixed = jnp.einsum('bhlm,bmhe->blhe', low(attn_prob), value_all, precision=HIGHEST).reshape(num_seqs, seq_len, model_width)
    mixed = low_back(low(mixed))
    branch = low_back(jnp.einsum('bld,de->ble', mixed, out_w, precision=HIGHEST))
    after_attn = hidden_in + branch
    normed_mlp = low(rms_norm(after_attn, gain_m))
    gate_up = low_back(jnp.einsum('bld,df->blf', normed_mlp, gate_up_w, precision=HIGHEST))
    inner = low(jax.nn.silu(gate_up[..., :FF]) * gate_up[..., FF:])
    mlp_branch = low_back(jnp.einsum('blf,fd->bld', inner, down_w, precision=HIGHEST))
    return after_attn + mlp_branch

def reference(tokens, segment_ids, positions, norm_attn, w_qkv, w_out, norm_mlp, w_gate_up, w_down, cotangent):
    group = math.gcd(SEQS, max(1, 2048 // LEN))
    rounds = SEQS // group
    inputs = tokens.astype(jnp.float32).reshape(rounds, group, LEN, D)
    cotan_all = cotangent.astype(jnp.float32).reshape(rounds, group, LEN, D)
    seg_all = segment_ids.reshape(rounds, group, LEN)
    pos_all = positions.reshape(rounds, group, LEN)
    params = tuple((weight.astype(jnp.float32) for weight in (norm_attn, w_qkv, w_out, norm_mlp, w_gate_up, w_down)))

    def one_round(totals, items):
        block_in, block_cot, block_seg, block_pos = items

        def apply(hidden_in, gain_a, qkv_w, out_w, gain_m, gate_up_w, down_w):
            return forward(hidden_in, gain_a, qkv_w, out_w, gain_m, gate_up_w, down_w, block_seg, block_pos)
        result, pull_back = jax.vjp(apply, block_in, params[0], params[1], params[2], params[3], params[4], params[5])
        gradients = pull_back(block_cot)
        totals = tuple((running + gradient for running, gradient in zip(totals, gradients[1:])))
        return (totals, (result.astype(jnp.bfloat16), gradients[0]))
    start_totals = tuple((jnp.zeros_like(weight) for weight in params))
    totals, (results, input_grads) = lax.scan(one_round, start_totals, (inputs, cotan_all, seg_all, pos_all))
    return (results.reshape(TOKENS, D), input_grads.reshape(TOKENS, D), totals[0], totals[1], totals[2], totals[3], totals[4], totals[5])
```

```python
import functools

import jax
import jax.numpy as jnp
from jax import lax
from jax.sharding import PartitionSpec as P

HEADS = 15
KV_HEADS = 5
HD = 64


EPSILON = 1e-05
ROPE_BASE = 100000.0
NEG_FILL = -1e30


def rope_tables(places):
    half_dim = HD // 2
    freqs = ROPE_BASE ** (-2.0 * jnp.arange(half_dim, dtype=jnp.float32) / HD)
    angles = places.astype(jnp.float32)[..., None] * freqs
    return (jnp.cos(angles), jnp.sin(angles))


def rotate(values, cosine, sine):
    half_dim = values.shape[-1] // 2
    cosine = cosine[..., None, :]
    sine = sine[..., None, :]
    first_half = values[..., :half_dim]
    second_half = values[..., half_dim:]
    return jnp.concatenate(
        [first_half * cosine - second_half * sine, second_half * cosine + first_half * sine], -1
    )


def unrotate(grads, cosine, sine):
    half_dim = grads.shape[-1] // 2
    cosine = cosine[..., None, :]
    sine = sine[..., None, :]
    first_half = grads[..., :half_dim]
    second_half = grads[..., half_dim:]
    return jnp.concatenate(
        [first_half * cosine + second_half * sine, second_half * cosine - first_half * sine], -1
    )


def norm_forward(values, gain):
    scale = lax.rsqrt(jnp.mean(values * values, -1, keepdims=True) + EPSILON)
    return (values * scale * gain, scale)


def norm_backward(values, scale, gain, grads):
    weighted = grads * gain
    values_grad = scale * weighted - values * (scale * scale * scale) * jnp.mean(
        weighted * values, -1, keepdims=True
    )
    gain_grad = jnp.sum(grads * values * scale, 0)
    return (values_grad, gain_grad)


def block_mask(seg_row, start, block_rows):
    seq_len = seg_row.shape[0]
    rows = start + jnp.arange(block_rows, dtype=jnp.int32)
    places = jnp.arange(seq_len, dtype=jnp.int32)
    return (seg_row[:, None] == seg_row[None, :]) & (places[None, :] <= rows[:, None])


def block_scores(query_block, key_low, allowed):
    scores = (
        jnp.einsum("bkge,mke->kgbm", query_block, key_low, preferred_element_type=jnp.float32)
        * 0.125
    )
    return jnp.where(allowed[None, None], scores, NEG_FILL)


AXES = ("rep", "shard")


def hop(values, shards, move):
    pairs = []
    for rep in range(2):
        for outer in range(shards // 4):
            for mid in range(2):
                for core in range(2):
                    to = move(rep, outer, mid, core)
                    pairs.append(
                        (
                            rep * shards + outer * 4 + mid * 2 + core,
                            to[0] * shards + to[1] * 4 + to[2] * 2 + to[3],
                        )
                    )
    return lax.ppermute(values, AXES, pairs)


def core_move(rep, outer, mid, core):
    return (rep, outer, mid, 1 - core)


def rep_move(rep, outer, mid, core):
    return (1 - rep, outer, mid, core)


def first_move(rep, outer, mid, core):
    return (rep, outer, 1 - mid, core) if core == 0 else (1 - rep, outer, mid, core)


def second_move(rep, outer, mid, core):
    return (1 - rep, outer, mid, core) if core == 0 else (rep, outer, 1 - mid, core)


def outer_move(step, count):
    return lambda rep, outer, mid, core: (rep, (outer + step) % count, mid, core)


def pick(array, index):
    return lax.dynamic_index_in_dim(array, index, 0, keepdims=False)


def place():
    shard = lax.axis_index("shard")
    return lax.axis_index("rep"), shard // 4, (shard // 2) % 2, shard % 2


def gather_rows(block, shards):
    rep, outer, mid, core = place()
    count = shards // 4
    rows, width = block.shape
    part = width // 4
    other = hop(
        lax.dynamic_slice(block, (0, ((1 - core) * 2 + rep) * part), (rows, part)), shards, core_move
    )
    mine = lax.dynamic_slice(block, (0, (core * 2 + rep) * part), (rows, part))
    both = jnp.stack([mine, other])
    chip = jnp.concatenate([pick(both, core), pick(both, 1 - core)], 0)
    held = jnp.stack([chip] + [hop(chip, shards, outer_move(k, count)) for k in range(1, count)])
    held = jnp.stack([held, hop(held, shards, second_move)])
    held = jnp.stack([held, hop(held, shards, first_move)])
    swap = hop(held, shards, core_move)
    halves = jnp.stack([held, swap])
    columns = []
    order = (outer - jnp.arange(count)) % count
    for want_core in range(2):
        half = pick(halves, core ^ want_core)
        for want_rep in range(2):
            pieces = []
            for want_mid in range(2):
                by_rep, by_mid = rep ^ want_rep, mid ^ want_mid
                second = by_mid if want_core == 0 else by_rep
                first = by_rep if want_core == 0 else by_mid
                pieces.append(pick(half.reshape((4,) + half.shape[2:]), second * 2 + first))
            quarter = jnp.stack(pieces, 1)
            columns.append(jnp.concatenate([pick(quarter, order[k])[None] for k in range(count)], 0))
    return jnp.concatenate([c.reshape(shards * rows, part) for c in columns], 1)


def add_low(*terms):
    total = terms[0].astype(jnp.float32)
    for term in terms[1:]:
        total = total + term.astype(jnp.float32)
    return total.astype(jnp.bfloat16)


def reduce_pieces(send_half, keep_half, piece, shards):
    rep, outer, mid, core = place()
    count = shards // 4
    came = hop(send_half, shards, core_move)
    first = core == 0
    away = [(1 - mid, 0), (1 - mid, 1)], [(0, 1 - rep), (1, 1 - rep)]
    stay = [(mid, 0), (mid, 1)], [(0, rep), (1, rep)]

    def chosen(table, k):
        return tuple(jnp.where(first, table[0][k][d], table[1][k][d]) for d in range(2))

    def both(where):
        return add_low(piece(keep_half, *where), piece(came, *where))

    sent = jnp.stack([both(chosen(away, 0)), both(chosen(away, 1))])
    got = hop(sent, shards, first_move)
    last = jnp.where(first, rep, mid)

    def held(k):
        where = jnp.where(first, mid, k), jnp.where(first, k, rep)
        return add_low(piece(keep_half, *where), piece(came, *where), pick(got, k))

    got_last = hop(held(1 - last), shards, second_move)
    where = (mid, rep)
    mine = add_low(piece(keep_half, *where), piece(came, *where), pick(got, last), got_last)
    total = pick(mine, outer).astype(jnp.float32)
    for k in range(1, count):
        total = total + hop(
            pick(mine, (outer + k) % count), shards, outer_move(k, count)
        ).astype(jnp.float32)
    return total.astype(jnp.bfloat16)


def reduce_columns(grad, shards):
    core = place()[3]
    rows, width = grad.shape
    half, part = width // 2, width // 4
    count = shards // 4

    def piece(array, mid, rep):
        array = array.reshape(count, 2, rows // (2 * count), half)
        out = lax.dynamic_slice(
            array, (0, mid, 0, rep * part), (count, 1, rows // (2 * count), part)
        )
        return out[:, 0]

    return reduce_pieces(
        lax.dynamic_slice(grad, (0, (1 - core) * half), (rows, half)),
        lax.dynamic_slice(grad, (0, core * half), (rows, half)),
        piece,
        shards,
    )


def reduce_rows(grad, shards):
    core = place()[3]
    rows, width = grad.shape
    count = shards // 4
    part = rows // (2 * shards)
    blocks = grad.reshape(count, 2, 2, 2, part, width)

    def half(which):
        return lax.dynamic_slice(
            blocks, (0, 0, which, 0, 0, 0), (count, 2, 1, 2, part, width)
        )[:, :, 0]

    def piece(array, mid, rep):
        return lax.dynamic_slice(array, (0, mid, rep, 0, 0), (count, 1, 1, part, width))[:, 0, 0]

    return reduce_pieces(half(1 - core), half(core), piece, shards)


def share_columns(total, shards):
    rep, outer, mid, core = place()
    rows = total.shape[0] // 2

    def rows_of(which):
        return lax.dynamic_slice(total, (which * rows, 0), (rows, total.shape[1]))

    parts = [
        rows_of(core),
        hop(rows_of(core), shards, rep_move),
        hop(rows_of(1 - core), shards, core_move),
        hop(rows_of(1 - core), shards, lambda r, o, m, c: (1 - r, o, m, 1 - c)),
    ]
    stack = jnp.stack(parts)
    return [pick(stack, q ^ (core * 2 + rep)) for q in range(4)]


def share_rows(total, shards):
    rep = place()[0]
    stack = jnp.stack([total, hop(total, shards, rep_move)])
    return jnp.concatenate([pick(stack, rep), pick(stack, 1 - rep)], 0)


def spread(features, shards):
    rows = features // shards
    padded = -(-rows // 8) * 8
    at = jnp.arange(features)
    target = at // rows * padded + at % rows
    return (target[:, None] == jnp.arange(padded * shards)[None, :]).astype(jnp.bfloat16)


def per_device(
    shards, tokens, segment_ids, positions, norm_attn, w_qkv, w_out, norm_mlp, w_gate_up, w_down, cotangent
):
    seq_len, model_width = tokens.shape
    hidden_units = w_gate_up.shape[1] // 2
    kv_width = KV_HEADS * HD
    group_size = HEADS // KV_HEADS
    block_rows = min(512, seq_len)
    num_blocks = seq_len // block_rows
    inputs = tokens.astype(jnp.float32)
    tail = (-(w_qkv.shape[1] - kv_width * 2)) % 128
    edge = model_width - tail
    head = model_width + tail
    mixed_block = jnp.concatenate(
        [w_qkv[:, :model_width], w_out[:, edge:], w_qkv[:, model_width:], w_out[:, :edge]], 1
    )
    mixed_full = gather_rows(mixed_block, shards)
    qkv_full = jnp.concatenate(
        [mixed_full[:, :model_width], mixed_full[:, head : head + 2 * kv_width]], 1
    )
    out_full = jnp.concatenate(
        [mixed_full[:, head + 2 * kv_width :], mixed_full[:, model_width:head]], 1
    )
    pad_rows = (-w_gate_up.shape[0]) % 8
    gate_up_full = lax.all_gather(
        jnp.pad(w_gate_up, ((0, pad_rows), (0, 0))), "shard", axis=0, tiled=True
    )
    down_full = lax.all_gather(w_down, "shard", axis=0, tiled=True)
    spreader = spread(model_width, shards)
    gains = lax.all_gather(jnp.stack([norm_attn, norm_mlp]), "shard", axis=1, tiled=True)
    gain_attn, gain_mlp = gains[0], gains[1]
    gain_attn = gain_attn.astype(jnp.float32)
    gain_mlp = gain_mlp.astype(jnp.float32)
    normed, scale_attn = norm_forward(inputs, gain_attn)
    normed_low = normed.astype(jnp.bfloat16)
    project = jnp.dot(normed_low, qkv_full, preferred_element_type=jnp.float32)
    cosine, sine = rope_tables(positions[0])
    query_low = rotate(project[:, :model_width].reshape(seq_len, HEADS, HD), cosine, sine).astype(
        jnp.bfloat16
    )
    key_low = rotate(
        project[:, model_width : model_width + kv_width].reshape(seq_len, KV_HEADS, HD),
        cosine,
        sine,
    ).astype(jnp.bfloat16)
    value_low = (
        project[:, model_width + kv_width :].reshape(seq_len, KV_HEADS, HD).astype(jnp.bfloat16)
    )
    seg_row = segment_ids[0]
    query_blocks = query_low.reshape(num_blocks, block_rows, KV_HEADS, group_size, HD)
    starts = jnp.arange(num_blocks, dtype=jnp.int32) * block_rows

    def attend(items):
        query_block, start = items
        allowed = block_mask(seg_row, start, block_rows)
        scores = block_scores(query_block, key_low, allowed)
        top_score = jnp.max(scores, -1, keepdims=True)
        expo = jnp.exp(scores - top_score)
        total_exp = jnp.sum(expo, -1, keepdims=True)
        log_total = top_score + jnp.log(total_exp)
        attn_prob = (expo / total_exp).astype(jnp.bfloat16)
        mixed = jnp.einsum(
            "kgbm,mke->bkge", attn_prob, value_low, preferred_element_type=jnp.float32
        )
        return (mixed.reshape(block_rows, model_width).astype(jnp.bfloat16), log_total)

    mixed_blocks, lse_blocks = lax.map(attend, (query_blocks, starts))
    mixed_low = mixed_blocks.reshape(seq_len, model_width)
    branch = jnp.dot(mixed_low, out_full, preferred_element_type=jnp.float32)
    after_attn = inputs + branch
    normed_mlp, scale_mlp = norm_forward(after_attn, gain_mlp)
    mlp_low = normed_mlp.astype(jnp.bfloat16)
    columns = mlp_low
    mlp_spread = jnp.dot(mlp_low, spreader, preferred_element_type=jnp.float32).astype(jnp.bfloat16)
    gate_up = jnp.dot(
        mlp_spread,
        gate_up_full,
        preferred_element_type=jnp.float32,
    )
    gate = gate_up[:, :hidden_units]
    up_part = gate_up[:, hidden_units:]
    sigma = jax.nn.sigmoid(gate)
    activ = gate * sigma
    inner_low = (activ * up_part).astype(jnp.bfloat16)
    columns = inner_low
    mlp_branch = jnp.dot(
        columns,
        down_full,
        preferred_element_type=jnp.float32,
    )
    output = (after_attn + mlp_branch).astype(jnp.bfloat16)
    cot_full = cotangent.astype(jnp.float32)
    inner_grad = jnp.einsum(
        "td,fd->tf",
        cotangent,
        down_full,
        preferred_element_type=jnp.float32,
    )
    columns = inner_low
    grad_down = jnp.einsum(
        "tf,td->fd", columns, cotangent, preferred_element_type=jnp.float32
    ).astype(jnp.bfloat16)
    grad_down = reduce_rows(grad_down, shards)
    gate_grad = inner_grad * up_part * sigma * (1.0 + gate * (1.0 - sigma))
    up_grad = inner_grad * activ
    gate_up_grad = jnp.concatenate([gate_grad, up_grad], 1).astype(jnp.bfloat16)
    columns = mlp_low
    grad_gate_up = jnp.einsum(
        "td,tf->df", columns, gate_up_grad, preferred_element_type=jnp.float32
    ).astype(jnp.bfloat16)
    grad_gate_up = reduce_columns(grad_gate_up, shards)
    spread_grad = jnp.einsum(
        "tf,df->td", gate_up_grad, gate_up_full, preferred_element_type=jnp.float32
    )
    grad_high = spread_grad.astype(jnp.bfloat16)
    grad_rest = (spread_grad - grad_high.astype(jnp.float32)).astype(jnp.bfloat16)
    normed_mlp_grad = jnp.einsum(
        "tp,dp->td", grad_high, spreader, preferred_element_type=jnp.float32
    ) + jnp.einsum("tp,dp->td", grad_rest, spreader, preferred_element_type=jnp.float32)
    after_grad_norm, grad_gain_mlp = norm_backward(after_attn, scale_mlp, gain_mlp, normed_mlp_grad)
    after_grad = cot_full + after_grad_norm
    branch_grad = after_grad.astype(jnp.bfloat16)
    grad_out = jnp.einsum("ti,td->id", mixed_low, branch_grad, preferred_element_type=jnp.float32)
    mixed_grad = jnp.einsum(
        "td,id->ti", branch_grad, out_full, preferred_element_type=jnp.float32
    ).astype(jnp.bfloat16)
    grad_blocks = mixed_grad.reshape(num_blocks, block_rows, KV_HEADS, group_size, HD)

    def attend_back(carry, items):
        key_acc, value_acc = carry
        query_block, grad_block, lse_block, start = items
        allowed = block_mask(seg_row, start, block_rows)
        scores = block_scores(query_block, key_low, allowed)
        prob = jnp.exp(scores - lse_block)
        value_acc = value_acc + jnp.einsum(
            "kgbm,bkge->mke",
            prob.astype(jnp.bfloat16),
            grad_block,
            preferred_element_type=jnp.float32,
        )
        prob_grad = jnp.einsum(
            "bkge,mke->kgbm", grad_block, value_low, preferred_element_type=jnp.float32
        )
        row_dot = jnp.sum(prob * prob_grad, -1, keepdims=True)
        score_grad = (prob * (prob_grad - row_dot)).astype(jnp.bfloat16)
        query_part = (
            jnp.einsum("kgbm,mke->bkge", score_grad, key_low, preferred_element_type=jnp.float32)
            * 0.125
        )
        key_acc = (
            key_acc
            + jnp.einsum(
                "kgbm,bkge->mke", score_grad, query_block, preferred_element_type=jnp.float32
            )
            * 0.125
        )
        return ((key_acc, value_acc), query_part)

    empty_kv = jnp.zeros((seq_len, KV_HEADS, HD), jnp.float32)
    (key_grad, value_grad), query_parts = lax.scan(
        attend_back, (empty_kv, empty_kv), (query_blocks, grad_blocks, lse_blocks, starts)
    )
    query_grad = query_parts.reshape(seq_len, HEADS, HD)
    project_grad = jnp.concatenate(
        [
            unrotate(query_grad, cosine, sine).reshape(seq_len, model_width),
            unrotate(key_grad, cosine, sine).reshape(seq_len, kv_width),
            value_grad.reshape(seq_len, kv_width),
        ],
        1,
    ).astype(jnp.bfloat16)
    grad_qkv = jnp.einsum("ti,tj->ij", normed_low, project_grad, preferred_element_type=jnp.float32)
    normed_grad = jnp.einsum(
        "tj,ij->ti", project_grad, qkv_full, preferred_element_type=jnp.float32
    )
    input_grad_norm, grad_gain_attn = norm_backward(inputs, scale_attn, gain_attn, normed_grad)
    input_grad = after_grad + input_grad_norm
    grad_mixed = jnp.concatenate(
        [
            grad_qkv[:, :model_width],
            grad_out[:, edge:],
            grad_qkv[:, model_width:],
            grad_out[:, :edge],
        ],
        1,
    ).astype(jnp.bfloat16)
    grad_mixed = reduce_columns(grad_mixed, shards)
    part = grad_mixed.shape[1]
    quarters = share_columns(jnp.concatenate([grad_mixed, grad_gate_up], 1), shards)
    whole_mixed = jnp.concatenate([q[:, :part] for q in quarters], 1).astype(jnp.float32)
    whole_gate_up = jnp.concatenate([q[:, part:] for q in quarters], 1).astype(jnp.float32)
    whole_qkv = jnp.concatenate(
        [whole_mixed[:, :model_width], whole_mixed[:, head : head + 2 * kv_width]], 1
    )
    whole_out = jnp.concatenate(
        [whole_mixed[:, head + 2 * kv_width :], whole_mixed[:, model_width:head]], 1
    )
    whole_down = share_rows(grad_down, shards).astype(jnp.float32)
    gain_grads = lax.psum(jnp.stack([grad_gain_attn, grad_gain_mlp]), AXES)
    rows = model_width // shards
    gain_grads = lax.dynamic_slice(gain_grads, (0, lax.axis_index("shard") * rows), (2, rows))
    return (
        output,
        input_grad,
        gain_grads[0],
        whole_qkv,
        whole_out,
        gain_grads[1],
        whole_gate_up,
        whole_down,
    )


def solution(mesh):
    in_specs = (
        P(("rep", "shard"), None),
        P(("rep", "shard"), None),
        P(("rep", "shard"), None),
        P("shard"),
        P("shard", None),
        P("shard", None),
        P("shard"),
        P("shard", None),
        P("shard", None),
        P(("rep", "shard"), None),
    )
    out_specs = (
        P(("rep", "shard"), None),
        P(("rep", "shard"), None),
        P("shard"),
        P("shard", None),
        P("shard", None),
        P("shard"),
        P("shard", None),
        P("shard", None),
    )
    return jax.shard_map(
        functools.partial(per_device, mesh.shape["shard"]), mesh=mesh, in_specs=in_specs, out_specs=out_specs, check_vma=False
    )
```

```python
import functools

import jax
import jax.numpy as jnp
from jax import lax
from jax.experimental import pallas as pl
from jax.experimental.pallas import tpu as pltpu
from jax.sharding import PartitionSpec as P

HEADS = 15
KV_HEADS = 5
HD = 64
GROUP = HEADS // KV_HEADS

EPSILON = 1e-05
ROPE_BASE = 100000.0
NEG_FILL = -1e30

AXES = ("rep", "shard")
F32 = jnp.float32
BF16 = jnp.bfloat16
LANES = 128
MIB = 1024 * 1024


def hop(values, shards, move):
    pairs = []
    for rep in range(2):
        for outer in range(shards // 4):
            for mid in range(2):
                for core in range(2):
                    to = move(rep, outer, mid, core)
                    pairs.append(
                        (
                            rep * shards + outer * 4 + mid * 2 + core,
                            to[0] * shards + to[1] * 4 + to[2] * 2 + to[3],
                        )
                    )
    return lax.ppermute(values, AXES, pairs)


def core_move(rep, outer, mid, core):
    return (rep, outer, mid, 1 - core)


def rep_move(rep, outer, mid, core):
    return (1 - rep, outer, mid, core)


def cross_move(rep, outer, mid, core):
    return (1 - rep, outer, mid, 1 - core)


def first_move(rep, outer, mid, core):
    return (rep, outer, 1 - mid, core) if core == 0 else (1 - rep, outer, mid, core)


def second_move(rep, outer, mid, core):
    return (1 - rep, outer, mid, core) if core == 0 else (rep, outer, 1 - mid, core)


def outer_move(step, count):
    return lambda rep, outer, mid, core: (rep, (outer + step) % count, mid, core)


class Order:
    def __init__(self):
        self.done = None

    def after(self, *values):
        if self.done is not None:
            values = lax.optimization_barrier(tuple(values) + (self.done,))[:-1]
        return values if len(values) > 1 else values[0]

    def mark(self, value):
        self.done = value
        return value


def pick(array, index):
    return lax.dynamic_index_in_dim(array, index, 0, keepdims=False)


def place():
    shard = lax.axis_index("shard")
    return lax.axis_index("rep"), shard // 4, (shard // 2) % 2, shard % 2


def settle_kernel(by_rows, where_ref, held_ref, came_ref, out_ref, sem):
    rep, mid, core = where_ref[0], where_ref[2], where_ref[3]
    for second, source in enumerate((held_ref, came_ref)):
        for first in range(2):
            to_mid = jnp.where(core == 0, mid ^ second, mid ^ first)
            to_rep = jnp.where(core == 0, rep ^ first, rep ^ second)
            for step in range(held_ref.shape[1]):
                to = out_ref.at[step, to_mid, to_rep] if by_rows else out_ref.at[to_rep, step, to_mid]
                pltpu.make_async_copy(source.at[first, step], to, sem).start()
    for source in (held_ref, came_ref):
        pltpu.make_async_copy(source, source, sem).wait()


def settle(held, came, where, by_rows):
    _, count, rows, width = held.shape
    shape = (count, 2, 2) if by_rows else (2, count, 2)
    any_space = pl.BlockSpec(memory_space=pl.ANY)
    out = pl.pallas_call(
        functools.partial(settle_kernel, by_rows),
        out_shape=jax.ShapeDtypeStruct(shape + (rows, width), held.dtype),
        in_specs=[pl.BlockSpec(memory_space=pltpu.SMEM), any_space, any_space],
        out_specs=pl.BlockSpec(memory_space=pltpu.VMEM),
        scratch_shapes=[pltpu.SemaphoreType.DMA],
        compiler_params=pltpu.CompilerParams(vmem_limit_bytes=8 * MIB),
        cost_estimate=SHORT,
        name="settle",
    )(where, held, came)
    return out.reshape(shape[:2] + (2 * rows, width))


def roll_steps(array, axis):
    count = array.shape[axis]
    outer = place()[1]
    parts = [
        lax.dynamic_index_in_dim(array, (outer - k) % count, axis, keepdims=True)
        for k in range(count)
    ]
    return jnp.concatenate(parts, axis)


def assemble_kernel(where_ref, own_ref, came_ref, out_ref, sem):
    outer, core = where_ref[1], where_ref[3]
    _, count, rows, width = own_ref.shape
    for source, half in ((own_ref, core), (came_ref, 1 - core)):
        for rep in range(2):
            column = pl.multiple_of((half * 2 + rep) * width, LANES)
            for step in range(count):
                row = pl.multiple_of(lax.rem(outer + count - step, count) * rows, 16)
                pltpu.make_async_copy(
                    source.at[rep, step],
                    out_ref.at[pl.ds(row, rows), pl.ds(column, width)],
                    sem,
                ).start()
    pltpu.make_async_copy(out_ref, out_ref, sem).wait()


def assemble(own, came, where):
    _, count, rows, width = own.shape
    core = where[3]
    shape = (count * rows, 4 * width)
    if rows % 16 or width % LANES:
        halves = roll_steps(jnp.stack([own, came]), 2)
        halves = jnp.stack([pick(halves, core), pick(halves, 1 - core)])
        return halves.transpose(2, 3, 0, 1, 4).reshape(shape)
    return pl.pallas_call(
        assemble_kernel,
        out_shape=jax.ShapeDtypeStruct(shape, own.dtype),
        in_specs=[
            pl.BlockSpec(memory_space=pltpu.SMEM),
            pl.BlockSpec(memory_space=pl.ANY),
            pl.BlockSpec(memory_space=pl.ANY),
        ],
        out_specs=pl.BlockSpec(memory_space=pltpu.VMEM),
        scratch_shapes=[pltpu.SemaphoreType.DMA],
        compiler_params=pltpu.CompilerParams(vmem_limit_bytes=16 * MIB),
        cost_estimate=LONG,
        name="assemble",
    )(where, own, came)


def add_low(*terms):
    total = terms[0].astype(F32)
    for term in terms[1:]:
        total = total + term.astype(F32)
    return total.astype(BF16)


class Reduction:
    def __init__(self, terms, piece, shards):
        self.terms, self.piece, self.shards = terms, piece, shards

    def parts(self, where):
        return [self.piece(term, *where) for term in self.terms]

    def first(self, order, *way):
        rep, _, mid, core = place()
        got = order.after(*self.terms, *way)
        self.terms = got if isinstance(got, tuple) else (got,)
        away = [(1 - mid, 0), (1 - mid, 1)], [(0, 1 - rep), (1, 1 - rep)]
        sums = []
        for k in range(2):
            where = tuple(jnp.where(core == 0, away[0][k][d], away[1][k][d]) for d in range(2))
            sums.append(add_low(*self.parts(where)))
        self.way = hop(order.mark(jnp.stack(sums)), self.shards, first_move)

    def second(self, order):
        rep, _, mid, core = place()
        self.got = order.after(self.way)
        self.last = jnp.where(core == 0, rep, mid)
        k = 1 - self.last
        where = jnp.where(core == 0, mid, k), jnp.where(core == 0, k, rep)
        out = order.mark(add_low(*self.parts(where), pick(self.got, k)))
        self.way = hop(out, self.shards, second_move)

    def third(self, order):
        rep, _, mid, _ = place()
        came = order.after(self.way)
        return order.mark(add_low(*self.parts((mid, rep)), pick(self.got, self.last), came))


def send_outer(mine, shards):
    outer = place()[1]
    count = shards // 4
    return [pick(mine, outer)] + [
        hop(pick(mine, (outer + k) % count), shards, outer_move(k, count)) for k in range(1, count)
    ]


def send_down(mine, shards):
    rep, outer, mid, core = place()
    count = shards // 4
    half = count // 2

    def move(step):
        pairs = []
        for r in range(2):
            for o in range(count):
                for m in range(2):
                    for c in range(2):
                        to = (o + step) % count
                        if to // half == c:
                            base = r * shards + m * 2 + c
                            pairs.append((base + o * 4, base + to * 4))
        return pairs

    return [pick(mine, outer % half)] + [
        lax.ppermute(pick(mine, (outer + k) % count % half), AXES, move(k))
        for k in range(1, count)
    ]


def share_down(total, shards):
    rep, outer, mid, core = place()
    came = hop(pick(total, 1 - core), shards, core_move)
    mine = jnp.where(outer // (shards // 8) == core, pick(total, core), came)
    stack = jnp.stack([mine, hop(mine, shards, rep_move)])
    return jnp.concatenate([pick(stack, rep), pick(stack, 1 - rep)], 0)


def share_columns(total, shards):
    rep, _, _, core = place()
    rows = total.shape[0] // 2
    halves = total.reshape(2, rows, total.shape[1])
    mine, other = pick(halves, core), pick(halves, 1 - core)
    stack = jnp.stack(
        [
            mine,
            hop(mine, shards, rep_move),
            hop(other, shards, core_move),
            hop(other, shards, cross_move),
        ]
    )
    return [pick(stack, q ^ (core * 2 + rep)) for q in range(4)]


LONG = pl.CostEstimate(flops=200 * 10**9, bytes_accessed=0, transcendentals=0)
SHORT = pl.CostEstimate(flops=10**6, bytes_accessed=0, transcendentals=0)


def dot(left, right, left_dim, right_dim):
    return lax.dot_general(
        left, right, (((left_dim,), (right_dim,)), ((), ())), preferred_element_type=F32
    )


def project_kernel(normed_ref, weight_ref, cos_ref, sin_ref, out_ref):
    half = HD // 2
    turned = (HEADS + KV_HEADS) * HD
    cosine, sine = cos_ref[...], sin_ref[...]
    normed = normed_ref[...]
    for start in range(0, turned, 2 * LANES):
        raw = dot(weight_ref[:, start : start + 2 * LANES], normed, 0, 0)
        for at in range(0, 2 * LANES, HD):
            row = start + at
            scale = 0.125 if row < HEADS * HD else 1.0
            upper, lower = raw[at : at + half], raw[at + half : at + HD]
            out_ref[row : row + half] = ((upper * cosine - lower * sine) * scale).astype(BF16)
            out_ref[row + half : row + HD] = ((lower * cosine + upper * sine) * scale).astype(BF16)
    out_ref[turned:] = dot(
        weight_ref[:, turned : turned + KV_HEADS * HD], normed, 0, 0
    ).astype(BF16)


def project(normed_t, weight, cosine, sine):
    return pl.pallas_call(
        project_kernel,
        out_shape=jax.ShapeDtypeStruct(((HEADS + 2 * KV_HEADS) * HD, normed_t.shape[1]), BF16),
        compiler_params=pltpu.CompilerParams(vmem_limit_bytes=24 * MIB),
        cost_estimate=SHORT,
        name="project",
    )(normed_t, weight, cosine, sine)


def split_tokens(tokens):
    block = 256 if tokens % 256 == 0 else tokens
    return [(start, start + block) for start in range(0, tokens, block)]


def attend_kernel(seg_row_ref, seg_col_ref, q_ref, k_ref, v_ref, prob_ref, mixed_ref, bias_ref):
    tokens = q_ref.shape[1]

    @pl.when(pl.program_id(0) == 0)
    def _():
        keys = lax.broadcasted_iota(jnp.int32, (tokens, tokens), 0)
        queries = lax.broadcasted_iota(jnp.int32, (tokens, tokens), 1)
        allowed = (seg_col_ref[...] == seg_row_ref[...]) & (keys <= queries)
        bias_ref[...] = jnp.where(allowed, 0.0, NEG_FILL)

    for head in range(GROUP):
        rows = slice(head * HD, (head + 1) * HD)
        for start, stop in split_tokens(tokens):
            scores = dot(k_ref[:, :stop], q_ref[rows, start:stop], 0, 0)
            scores = scores + bias_ref[:stop, start:stop]
            expo = jnp.exp(scores - jnp.max(scores, 0, keepdims=True))
            prob = (expo * (1.0 / jnp.sum(expo, 0, keepdims=True))).astype(BF16)
            prob_ref[head, :stop, start:stop] = prob
            mixed_ref[rows, start:stop] = dot(v_ref[:, :stop], prob, 1, 0).astype(BF16)


def attend(qkv, seg_row):
    tokens = qkv.shape[1]
    return pl.pallas_call(
        attend_kernel,
        grid=(KV_HEADS,),
        out_shape=(
            jax.ShapeDtypeStruct((HEADS, tokens, tokens), BF16),
            jax.ShapeDtypeStruct((HEADS * HD, tokens), BF16),
        ),
        in_specs=[
            pl.BlockSpec((1, tokens), lambda i: (0, 0)),
            pl.BlockSpec((tokens, 1), lambda i: (0, 0)),
            pl.BlockSpec((GROUP * HD, tokens), lambda i: (i, 0)),
            pl.BlockSpec((HD, tokens), lambda i: (HEADS + i, 0)),
            pl.BlockSpec((HD, tokens), lambda i: (HEADS + KV_HEADS + i, 0)),
        ],
        out_specs=(
            pl.BlockSpec((GROUP, tokens, tokens), lambda i: (i, 0, 0)),
            pl.BlockSpec((GROUP * HD, tokens), lambda i: (i, 0)),
        ),
        scratch_shapes=[pltpu.VMEM((tokens, tokens), F32)],
        compiler_params=pltpu.CompilerParams(vmem_limit_bytes=32 * MIB),
        cost_estimate=LONG,
        name="attend",
    )(seg_row.reshape(1, tokens), seg_row.reshape(tokens, 1), qkv, qkv, qkv)


def out_columns(width):
    kept = (HEADS + 2 * KV_HEADS) * HD
    tail = -kept % LANES
    return kept + tail - LANES, LANES - tail, kept + tail


def branch_kernel(mixed_ref, weight_ref, tokens_ref, after_ref, scale_ref, normed_ref):
    mixed = mixed_ref[...]
    tile, skip, rest = out_columns(weight_ref.shape[1])
    wide = weight_ref.shape[1] - rest
    last = dot(weight_ref[:, tile : tile + LANES], mixed, 0, 0)
    after_ref[:wide] = tokens_ref[:wide].astype(F32) + dot(weight_ref[:, rest:], mixed, 0, 0)
    after_ref[wide:] = tokens_ref[wide:].astype(F32) + last[skip:]
    after = after_ref[...]
    scale = lax.rsqrt(jnp.mean(after * after, 0, keepdims=True) + EPSILON)
    scale_ref[...] = scale
    normed_ref[...] = (after * scale).astype(BF16)


def branch(mixed, weight, tokens):
    width, count = tokens.shape
    return pl.pallas_call(
        branch_kernel,
        out_shape=(
            jax.ShapeDtypeStruct((width, count), F32),
            jax.ShapeDtypeStruct((1, count), F32),
            jax.ShapeDtypeStruct((width, count), BF16),
        ),
        compiler_params=pltpu.CompilerParams(vmem_limit_bytes=24 * MIB),
        cost_estimate=LONG,
        name="branch",
    )(mixed, weight, tokens)


def feed_kernel(
    ordered,
    offset,
    where_ref,
    normed_refs,
    cot_refs,
    pieces_ref,
    down_refs,
    down_grad_in_ref,
    sum_refs,
    back_refs,
    grad_ref,
    down_grad_ref,
    normed,
    cot,
    weight,
    down_all,
    down,
    inner,
    pull,
    grad,
    down_grad,
    results,
    results_low,
    sems,
    out_sems,
):
    outer, core = where_ref[1], where_ref[3]
    tokens = normed_refs[0].shape[1]
    units = down.shape[0]
    size = units // 2
    quarter = down_all.shape[0] // 2

    def load(index, copies):
        for source, to in copies:
            pltpu.make_async_copy(source, to, sems.at[index]).start()

    def ready(index, ref):
        pltpu.make_async_copy(ref, ref, sems.at[index]).wait()

    load(0, [(normed_refs[k], normed.at[:, pl.ds(k * tokens, tokens)]) for k in range(2)])
    if ordered:
        steps, rows = 1, pieces_ref.shape[2]
    else:
        steps, rows = pieces_ref.shape[1:3]
    for kind in range(2):
        load(
            1 + kind,
            [
                (
                    pieces_ref.at[rep, step, :, pl.ds(kind * size, size)],
                    weight.at[
                        pl.ds(pl.multiple_of(lax.rem(outer + steps - step, steps) * rows, 16), rows)
                        if steps > 1
                        else pl.ds(0, rows),
                        pl.ds(kind * units + rep * size, size),
                    ],
                )
                for rep in range(2)
                for step in range(steps)
            ],
        )
    load(3, [(cot_refs[k], cot.at[:, pl.ds(k * tokens, tokens)]) for k in range(2)])
    if ordered:
        load(4, [(down_refs[0], down_all)])
    else:
        half = steps // 2
        block = down_refs[0].shape[2]
        for source, owner in ((down_refs[0], core), (down_refs[1], 1 - core)):
            for at in range(half):
                step = lax.rem(outer + steps - (core * half + at), steps)
                for mid in range(2):
                    row = pl.multiple_of(((at * 2 + mid) * 2 + owner) * block, 16)
                    load(4, [(source.at[step, mid], down_all.at[pl.ds(row, block)])])
    ready(0, normed)
    ready(1, weight.at[:, pl.ds(0, units)])
    tile = 2 * LANES if units % (2 * LANES) == 0 else LANES
    for start in range(0, units, tile):
        at = pl.ds(start, tile)
        gate = dot(weight[:, at], normed[...], 0, 0)
        if start == 0:
            ready(2, weight.at[:, pl.ds(units, units)])
        up = dot(weight[:, pl.ds(units + start, tile)], normed[...], 0, 0)
        if start == 0:
            ready(3, cot)
            ready(4, down_all)
            down[:size] = down_all[offset : offset + size]
            down[size:] = down_all[quarter + offset : quarter + offset + size]
        inner_grad = dot(down[at], cot[...], 1, 0)
        sigma = 1.0 / (1.0 + jnp.exp(-gate))
        activ = gate * sigma
        inner[at] = (activ * up).astype(BF16)
        pull[at] = (inner_grad * up * (sigma + activ * (1.0 - sigma))).astype(BF16)
        pull[pl.ds(units + start, tile)] = (inner_grad * activ).astype(BF16)
        down_grad[at] = dot(inner[at], cot[...], 1, 1).astype(BF16)
    for rep in range(2):
        pltpu.make_async_copy(
            down_grad.at[pl.ds(rep * size, size)],
            down_grad_ref.at[rep, pl.ds(offset, size)],
            out_sems.at[0],
        ).start()
    for kind in range(2):
        for start in range(0, units, tile):
            at = pl.ds(kind * units + start, tile)
            grad[:, at] = dot(normed[...], pull[at], 1, 1).astype(BF16)
        for rep in range(2):
            pltpu.make_async_copy(
                grad.at[:, pl.ds(kind * units + rep * size, size)],
                grad_ref.at[rep, :, pl.ds(kind * size, size)],
                out_sems.at[1],
            ).start()
    for index, (out_refs, left, right, dim) in enumerate(
        ((back_refs, weight, pull, 1), (sum_refs, down, inner, 0))
    ):
        low = dot(left[...], right[:, pl.ds(tokens, tokens)], dim, 0)
        results_low[index] = low.astype(BF16)
        pltpu.make_async_copy(results_low.at[index], out_refs[1], out_sems.at[2 + index]).start()
        results[index] = dot(left[...], right[:, pl.ds(0, tokens)], dim, 0)
        pltpu.make_async_copy(results.at[index], out_refs[0], out_sems.at[4 + index]).start()
    pltpu.make_async_copy(down_grad, down_grad, out_sems.at[0]).wait()
    pltpu.make_async_copy(grad, grad, out_sems.at[1]).wait()
    for index in range(2):
        pltpu.make_async_copy(
            results_low.at[index], results_low.at[index], out_sems.at[2 + index]
        ).wait()
        pltpu.make_async_copy(results.at[index], results.at[index], out_sems.at[4 + index]).wait()


def feed(where, offset, normed, cot, pieces, down, down_grad):
    width, tokens = normed[0].shape
    size = pieces.shape[-1] // 2
    units = 2 * size
    count, _, block = down[0].shape[:3]
    half_units = count * 2 * block
    ordered = pieces.shape[2] % 16 != 0 or block % 16 != 0
    if ordered:
        pieces = roll_steps(pieces, 1).reshape(2, 1, width, units)
        core = where[3]
        rows = roll_steps(jnp.stack(down), 1)
        rows = jnp.stack([pick(rows, core), pick(rows, 1 - core)], 2)
        rows = rows.reshape(2, half_units, width)
        down = (pick(rows, core),)
    first_call = down_grad is None
    operands = [*normed, *cot, pieces, *down] + ([] if first_call else [down_grad])
    split = len(down)

    def body(where_ref, *refs):
        refs = list(refs)
        take = lambda count: [refs.pop(0) for _ in range(count)]
        ins = take(2), take(2), take(1)[0], take(split)
        down_grad_in = None if first_call else take(1)[0]
        feed_kernel(
            ordered, offset, where_ref, *ins, down_grad_in, take(2), take(2), *refs
        )

    wide = jax.ShapeDtypeStruct((width, tokens), F32)
    low = jax.ShapeDtypeStruct((width, tokens), BF16)
    out_shape = (
        wide,
        low,
        wide,
        low,
        jax.ShapeDtypeStruct((2, width, units), BF16),
        jax.ShapeDtypeStruct((2, half_units // 2, width), BF16),
    )
    any_space = pl.BlockSpec(memory_space=pl.ANY)
    return pl.pallas_call(
        body,
        in_specs=[pl.BlockSpec(memory_space=pltpu.SMEM)] + [any_space] * len(operands),
        out_specs=(any_space,) * len(out_shape),
        out_shape=out_shape,
        scratch_shapes=[
            pltpu.VMEM((width, 2 * tokens), BF16),
            pltpu.VMEM((width, 2 * tokens), BF16),
            pltpu.VMEM((width, 2 * units), BF16),
            pltpu.VMEM((half_units, width), BF16),
            pltpu.VMEM((units, width), BF16),
            pltpu.VMEM((units, 2 * tokens), BF16),
            pltpu.VMEM((2 * units, 2 * tokens), BF16),
            pltpu.VMEM((width, 2 * units), BF16),
            pltpu.VMEM((units, width), BF16),
            pltpu.VMEM((2, width, tokens), F32),
            pltpu.VMEM((2, width, tokens), BF16),
            pltpu.SemaphoreType.DMA((6,)),
            pltpu.SemaphoreType.DMA((6,)),
        ],
        input_output_aliases={} if first_call else {len(operands): 5},
        compiler_params=pltpu.CompilerParams(vmem_limit_bytes=52 * MIB),
        cost_estimate=LONG,
        name="feed",
    )(where, *operands)


def return_kernel(
    back_refs, after_ref, scale_ref, cot_ref, mixed_ref, weight_ref, grad_ref, mixed_grad_ref, out_grad_ref
):
    back = back_refs[0][...]
    for ref in back_refs[1:]:
        back = back + ref[...].astype(F32)
    after, scale = after_ref[...], scale_ref[...]
    mean = jnp.mean(back * after, 0, keepdims=True)
    grad = cot_ref[...].astype(F32) + scale * back - after * (scale * scale * scale * mean)
    grad_ref[...] = grad
    low = grad.astype(BF16)
    tile, skip, rest = out_columns(weight_ref.shape[1])
    wide = weight_ref.shape[1] - rest
    last = low[wide:]
    mixed_grad_ref[...] = (
        dot(weight_ref[:, rest:], low[:wide], 1, 0)
        + dot(weight_ref[:, tile + skip : rest], last, 1, 0)
    ).astype(BF16)
    mixed = mixed_ref[...]
    out_grad_ref[:, : LANES - skip] = dot(mixed, last, 1, 1).astype(BF16)
    out_grad_ref[:, LANES - skip :] = dot(mixed, low[:wide], 1, 1).astype(BF16)


def return_branch(backs, after, scale, cot, mixed, weight):
    width, count = after.shape

    def body(*refs):
        return_kernel(refs[: len(backs)], *refs[len(backs) :])

    return pl.pallas_call(
        body,
        out_shape=(
            jax.ShapeDtypeStruct((width, count), F32),
            jax.ShapeDtypeStruct((width, count), BF16),
            jax.ShapeDtypeStruct((width, width), BF16),
        ),
        compiler_params=pltpu.CompilerParams(vmem_limit_bytes=32 * MIB),
        cost_estimate=LONG,
        name="return_branch",
    )(*backs, after, scale, cot, mixed, weight)


def attend_back_kernel(
    prob_ref, mixed_ref, grad_ref, q_ref, k_ref, v_ref, cos_ref, sin_ref, dq_ref, dk_ref, dv_ref
):
    half = HD // 2
    tokens = q_ref.shape[1]
    cosine, sine = cos_ref[...], sin_ref[...]
    key_grad = [None] * len(split_tokens(tokens))
    value_grad = [None] * len(split_tokens(tokens))

    def unturn(to_ref, row, grads, columns):
        upper, lower = grads[:half], grads[half:]
        c, s = cosine[:, columns], sine[:, columns]
        to_ref[row : row + half, columns] = (upper * c + lower * s).astype(BF16)
        to_ref[row + half : row + HD, columns] = (lower * c - upper * s).astype(BF16)

    for head in range(GROUP):
        rows = slice(head * HD, (head + 1) * HD)
        for block, (start, stop) in enumerate(split_tokens(tokens)):
            grad = grad_ref[rows, start:stop]
            mixed = mixed_ref[rows, start:stop]
            row_dot = jnp.sum(grad.astype(F32) * mixed.astype(F32), 0, keepdims=True)
            prob = prob_ref[head, :stop, start:stop]
            prob_grad = dot(v_ref[:, :stop], grad, 0, 0)
            score_grad = (prob.astype(F32) * (prob_grad - row_dot)).astype(BF16)
            unturn(
                dq_ref,
                head * HD,
                dot(k_ref[:, :stop], score_grad, 1, 0) * 0.125,
                slice(start, stop),
            )
            dk = dot(q_ref[rows, start:stop], score_grad, 1, 1)
            dv = dot(grad, prob, 1, 1)
            for part in range(block + 1):
                a, b = split_tokens(tokens)[part]
                if key_grad[part] is None:
                    key_grad[part], value_grad[part] = dk[:, a:b], dv[:, a:b]
                else:
                    key_grad[part] = key_grad[part] + dk[:, a:b]
                    value_grad[part] = value_grad[part] + dv[:, a:b]
    for part, (a, b) in enumerate(split_tokens(tokens)):
        unturn(dk_ref, 0, key_grad[part], slice(a, b))
        dv_ref[:, a:b] = value_grad[part].astype(BF16)


def attend_back(prob, mixed, grad, qkv, cosine, sine):
    tokens = qkv.shape[1]
    heads = pl.BlockSpec((GROUP * HD, tokens), lambda i: (i, 0))
    one = pl.BlockSpec((HD, tokens), lambda i: (i, 0))
    table = pl.BlockSpec((HD // 2, tokens), lambda i: (0, 0))
    return pl.pallas_call(
        attend_back_kernel,
        grid=(KV_HEADS,),
        out_shape=(
            jax.ShapeDtypeStruct((HEADS * HD, tokens), BF16),
            jax.ShapeDtypeStruct((KV_HEADS * HD, tokens), BF16),
            jax.ShapeDtypeStruct((KV_HEADS * HD, tokens), BF16),
        ),
        in_specs=[
            pl.BlockSpec((GROUP, tokens, tokens), lambda i: (i, 0, 0)),
            heads,
            heads,
            heads,
            pl.BlockSpec((HD, tokens), lambda i: (HEADS + i, 0)),
            pl.BlockSpec((HD, tokens), lambda i: (HEADS + KV_HEADS + i, 0)),
            table,
            table,
        ],
        out_specs=(heads, one, one),
        compiler_params=pltpu.CompilerParams(vmem_limit_bytes=32 * MIB),
        cost_estimate=LONG,
        name="attend_back",
    )(prob, mixed, grad, qkv, qkv, qkv, cosine, sine)


def finish_grads_kernel(
    where_ref, normed_t_ref, dq_ref, dk_ref, dv_ref, out_grad_ref, keep_ref, send_ref, halves_ref
):
    normed_t = normed_t_ref[...]
    queries = dq_ref.shape[0]
    values = dv_ref.shape[0]
    halves_ref[0, :, :queries] = dot(normed_t, dq_ref[...], 1, 1).astype(BF16)
    halves_ref[0, :, queries:] = dot(normed_t, dk_ref[...], 1, 1).astype(BF16)
    halves_ref[1, :, :values] = dot(normed_t, dv_ref[...], 1, 1).astype(BF16)
    halves_ref[1, :, values:] = out_grad_ref[...]
    core = where_ref[3]
    keep_ref[...] = halves_ref[core]
    send_ref[...] = halves_ref[1 - core]


def finish_grads(where, normed_t, dq, dk, dv, out_grad):
    width = normed_t.shape[0]
    half = dq.shape[0] + dk.shape[0]
    shape = jax.ShapeDtypeStruct((width, half), BF16)
    vmem = pl.BlockSpec(memory_space=pltpu.VMEM)
    return pl.pallas_call(
        finish_grads_kernel,
        out_shape=(shape, shape),
        in_specs=[pl.BlockSpec(memory_space=pltpu.SMEM)] + [vmem] * 5,
        out_specs=(vmem, vmem),
        scratch_shapes=[pltpu.VMEM((2, width, half), BF16)],
        compiler_params=pltpu.CompilerParams(vmem_limit_bytes=24 * MIB),
        cost_estimate=LONG,
        name="finish_grads",
    )(where, normed_t, dq, dk, dv, out_grad)


def input_grad_kernel(dq_ref, dk_ref, dv_ref, weight_ref, tokens_ref, scale_ref, grad_ref, out_ref):
    queries, keys = dq_ref.shape[0], dk_ref.shape[0]
    end = queries + keys + dv_ref.shape[0]
    pull = dot(weight_ref[:, :queries], dq_ref[...], 1, 0)
    pull = pull + dot(weight_ref[:, queries : queries + keys], dk_ref[...], 1, 0)
    pull = pull + dot(weight_ref[:, queries + keys : end], dv_ref[...], 1, 0)
    values, scale = tokens_ref[...].astype(F32), scale_ref[...]
    mean = jnp.mean(pull * values, 0, keepdims=True)
    out_ref[...] = grad_ref[...] + scale * pull - values * (scale * scale * scale * mean)


def input_gradient(dq, dk, dv, weight, tokens, scale, grad):
    return pl.pallas_call(
        input_grad_kernel,
        out_shape=jax.ShapeDtypeStruct(grad.shape, F32),
        compiler_params=pltpu.CompilerParams(vmem_limit_bytes=24 * MIB),
        cost_estimate=SHORT,
        name="input_gradient",
    )(dq, dk, dv, weight, tokens, scale, grad)


def per_device(
    shards,
    tokens,
    segment_ids,
    positions,
    norm_attn,
    w_qkv,
    w_out,
    norm_mlp,
    w_gate_up,
    w_down,
    cotangent,
):
    rep, outer, mid, core = place()
    where = jnp.stack([rep, outer, mid, core]).astype(jnp.int32)
    count = shards // 4
    width = tokens.shape[1]
    rows = w_qkv.shape[0]
    kept = w_qkv.shape[1]
    units = w_gate_up.shape[1] // 8
    gain_attn, gain_mlp = norm_attn.astype(F32)[:, None], norm_mlp.astype(F32)[:, None]

    qkv_block = (w_qkv.astype(F32) * gain_attn).astype(BF16)
    tail = -kept % LANES
    attn_block = jnp.concatenate([qkv_block, w_out[:, width - tail :], w_out[:, : width - tail]], 1)
    feed_block = (w_gate_up.astype(F32) * gain_mlp).astype(BF16)
    part = attn_block.shape[1] // 4

    big = -(-units // (2 * LANES)) * LANES
    chunks = ((0, big), (big, units - big))

    def quarter(index):
        return jnp.concatenate(
            [lax.dynamic_slice(attn_block, (0, index * part), (rows, part))]
            + [
                lax.dynamic_slice(feed_block, (0, (kind * 4 + index) * units + start), (rows, size))
                for start, size in chunks
                for kind in range(2)
            ],
            1,
        )

    order = Order()
    mine = quarter(core * 2 + rep)
    other = hop(quarter((1 - core) * 2 + rep), shards, core_move)
    both = jnp.stack([mine, other])
    chip = jnp.concatenate([pick(both, core), pick(both, 1 - core)], 0)
    down_piece = pick(w_down.reshape(2, w_down.shape[0] // 2, width), rep)

    def outer_start(piece):
        return [piece] + [hop(piece, shards, outer_move(k, count)) for k in range(1, count)]

    def outer_stop(parts):
        return order.mark(jnp.stack(order.after(*parts)))

    def pair(held, came):
        return order.mark(jnp.stack(order.after(held, came)))

    def settled(held, came, by_rows=False):
        held, came = order.after(held, came)
        return order.mark(settle(held, came, where, by_rows))

    tokens_t, cot_t = tokens.T, cotangent.T

    attn_way = outer_start(order.mark(chip[:, :part]))
    cot_came = hop(cot_t, shards, core_move)
    half_dim = HD // 2
    freqs = ROPE_BASE ** (-2.0 * jnp.arange(half_dim, dtype=F32) / HD)
    angles = freqs[:, None] * positions[0].astype(F32)[None, :]
    cosine, sine = jnp.cos(angles), jnp.sin(angles)
    inputs = order.after(tokens_t).astype(F32)
    scale_attn = lax.rsqrt(jnp.mean(inputs * inputs, 0, keepdims=True) + EPSILON)
    normed_t = order.mark((inputs * scale_attn).astype(BF16))
    attn_own = outer_stop(attn_way)
    attn_way = hop(attn_own, shards, second_move)
    down_way = outer_start(order.after(down_piece))
    attn_own = pair(attn_own, attn_way)
    attn_way = hop(attn_own, shards, first_move)
    down_own = outer_stop(down_way)
    down_way = hop(down_own, shards, second_move)
    feed0_way = outer_start(order.after(chip[:, part : part + 2 * big]))
    attn_own = settled(attn_own, attn_way)
    attn_way = hop(attn_own, shards, core_move)
    down_own = pair(down_own, down_way)
    down_way = hop(down_own, shards, first_move)
    attn_own, attn_way = order.after(attn_own, attn_way)
    attn_full = order.mark(assemble(attn_own, attn_way, where))
    qkv = order.mark(project(order.after(normed_t), attn_full, cosine, sine))
    feed0_own = outer_stop(feed0_way)
    feed0_way = hop(feed0_own, shards, second_move)
    feed1_way = outer_start(order.after(chip[:, part + 2 * big :]))
    prob, mixed = attend(order.after(qkv), segment_ids[0])
    order.mark(mixed)
    down_own = settled(down_own, down_way, True)
    down_way = hop(down_own, shards, core_move)
    feed0_own = pair(feed0_own, feed0_way)
    feed0_way = hop(feed0_own, shards, first_move)
    feed1_own = outer_stop(feed1_way)
    feed1_way = hop(feed1_own, shards, second_move)
    after_attn, scale_mlp, mlp_low = branch(order.after(mixed), attn_full, tokens_t)
    order.mark(mlp_low)
    low_came = hop(mlp_low, shards, core_move)
    feed1_own = pair(feed1_own, feed1_way)
    feed1_way = hop(feed1_own, shards, first_move)
    feed0_full = settled(feed0_own, feed0_way)

    def run_feed(chunk, pieces, down_grad):
        pieces, low, cot, down = order.after(pieces, low_came, cot_came, down_way)
        return feed(
            where, chunks[chunk][0], (mlp_low, low), (cot_t, cot), pieces, (down_own, down), down_grad
        )

    sum0, sum0_other, back0, back0_other, feed0_grad, down_grad = run_feed(0, feed0_full, None)
    order.mark(feed0_grad)
    sum0_came = hop(sum0_other, shards, core_move)
    back0_came = hop(back0_other, shards, core_move)

    def feed_piece(array, to_mid, to_rep):
        array = array.reshape(2, count, 2, 2 * rows, array.shape[-1])
        return lax.dynamic_slice(
            array, (to_rep, 0, to_mid, 0, 0), (1, count, 1) + array.shape[3:]
        )[0, :, 0]

    feed0_sum = Reduction((feed0_grad,), feed_piece, shards)
    feed0_sum.first(order)
    feed1_full = settled(feed1_own, feed1_way)
    sum1, sum1_other, back1, back1_other, feed1_grad, down_grad = run_feed(1, feed1_full, down_grad)
    order.mark(feed1_grad)
    back1_came = hop(back1_other, shards, core_move)
    sum1_came = hop(sum1_other, shards, core_move)

    def down_piece_of(array, to_mid, to_rep):
        array = array.reshape(count // 2, 2, 2, 2, w_down.shape[0] // 2, width)
        return lax.dynamic_slice(
            array, (0, to_mid, 0, to_rep, 0, 0), (count // 2, 1, 2, 1) + array.shape[4:]
        )[:, 0, :, 0]

    feed1_sum = Reduction((feed1_grad,), feed_piece, shards)
    down_sum = Reduction((down_grad,), down_piece_of, shards)
    feed1_sum.first(order)
    backs = order.after(back0, back0_came, back1, back1_came)
    after_grad, mixed_grad, out_grad = return_branch(
        backs, after_attn, scale_mlp, cot_t, mixed, attn_full
    )
    order.mark(mixed_grad)
    feed0_sum.second(order)
    dq, dk, dv = attend_back(prob, mixed, order.after(mixed_grad), qkv, cosine, sine)
    order.mark(dq)
    feed1_sum.second(order)
    down_sum.first(order)
    feed0_total = feed0_sum.third(order)
    keep_attn, send_attn = finish_grads(where, normed_t, order.after(dq), dk, dv, out_grad)
    order.mark(keep_attn)

    def attn_piece(array, to_mid, to_rep):
        array = array.reshape(count, 2, 2 * rows, 2 * part)
        return lax.dynamic_slice(
            array, (0, to_mid, 0, to_rep * part), (count, 1, 2 * rows, part)
        )[:, 0]

    attn_came = hop(send_attn, shards, core_move)
    input_grad = input_gradient(order.after(dq), dk, dv, attn_full, tokens_t, scale_attn, after_grad)
    order.mark(input_grad)
    attn_sum = Reduction((keep_attn, attn_came), attn_piece, shards)
    attn_sum.first(order)
    down_sum.second(order)
    feed1_total = feed1_sum.third(order)
    feed_way = send_outer(
        order.mark(jnp.concatenate(order.after(feed0_total, feed1_total), -1)), shards
    )
    output = after_attn + (sum0 + sum1)
    output = (output + (sum0_came.astype(F32) + sum1_came.astype(F32))).astype(BF16)
    attn_sum.second(order)
    down_total = down_sum.third(order)
    down_way = send_down(down_total, shards)
    feed_total = order.mark(add_low(*order.after(*feed_way)))
    feed_quarters = share_columns(feed_total, shards)
    attn_total = attn_sum.third(order)
    attn_way = send_outer(attn_total, shards)
    down_total = order.mark(add_low(*order.after(*down_way)))
    grad_down = share_down(down_total, shards).astype(F32)
    attn_quarters = share_columns(add_low(*order.after(*attn_way)), shards)

    attn_rows = jnp.concatenate(attn_quarters, 1).astype(F32)
    feed_rows = jnp.concatenate(
        [
            q[:, 2 * start + kind * size : 2 * start + (kind + 1) * size]
            for kind in range(2)
            for q in feed_quarters
            for start, size in chunks
        ],
        1,
    ).astype(F32)
    qkv_rows = attn_rows[:, :kept]
    grad_norm_attn = jnp.sum(qkv_rows * w_qkv.astype(F32), 1)
    grad_norm_mlp = jnp.sum(feed_rows * w_gate_up.astype(F32), 1)
    grad_out = jnp.concatenate([attn_rows[:, kept + tail :], attn_rows[:, kept : kept + tail]], 1)
    return (
        output.T,
        input_grad.T,
        grad_norm_attn,
        qkv_rows * gain_attn,
        grad_out,
        grad_norm_mlp,
        feed_rows * gain_mlp,
        grad_down,
    )


def solution(mesh):
    in_specs = (
        P(("rep", "shard"), None),
        P(("rep", "shard"), None),
        P(("rep", "shard"), None),
        P("shard"),
        P("shard", None),
        P("shard", None),
        P("shard"),
        P("shard", None),
        P("shard", None),
        P(("rep", "shard"), None),
    )
    out_specs = (
        P(("rep", "shard"), None),
        P(("rep", "shard"), None),
        P("shard"),
        P("shard", None),
        P("shard", None),
        P("shard"),
        P("shard", None),
        P("shard", None),
    )
    return jax.shard_map(
        functools.partial(per_device, mesh.shape["shard"]),
        mesh=mesh,
        in_specs=in_specs,
        out_specs=out_specs,
        check_vma=False,
    )
```

```python
import functools

import jax
import jax.numpy as jnp
from jax import lax
from jax.experimental import pallas as pl
from jax.experimental.pallas import tpu as pltpu
from jax.sharding import PartitionSpec as P

HEADS = 15
KV_HEADS = 5
HD = 64
GROUP = HEADS // KV_HEADS

EPSILON = 1e-05
ROPE_BASE = 100000.0
NEG_FILL = -1e30

AXES = ("rep", "shard")
F32 = jnp.float32
BF16 = jnp.bfloat16
LANES = 128
MIB = 1024 * 1024


def hop(values, shards, move):
    pairs = []
    for rep in range(2):
        for outer in range(shards // 4):
            for mid in range(2):
                for core in range(2):
                    to = move(rep, outer, mid, core)
                    pairs.append(
                        (
                            rep * shards + outer * 4 + mid * 2 + core,
                            to[0] * shards + to[1] * 4 + to[2] * 2 + to[3],
                        )
                    )
    return lax.ppermute(values, AXES, pairs)


def core_move(rep, outer, mid, core):
    return (rep, outer, mid, 1 - core)


def rep_move(rep, outer, mid, core):
    return (1 - rep, outer, mid, core)


def cross_move(rep, outer, mid, core):
    return (1 - rep, outer, mid, 1 - core)


def first_move(rep, outer, mid, core):
    return (rep, outer, 1 - mid, core) if core == 0 else (1 - rep, outer, mid, core)


def second_move(rep, outer, mid, core):
    return (1 - rep, outer, mid, core) if core == 0 else (rep, outer, 1 - mid, core)


def outer_move(step, count):
    return lambda rep, outer, mid, core: (rep, (outer + step) % count, mid, core)


class Order:
    def __init__(self, tick):
        self.done = None
        self.tick = tick

    def after(self, *values):
        if self.done is not None:
            values = lax.optimization_barrier(tuple(values) + (self.done,))[:-1]
        return values if len(values) > 1 else values[0]

    def mark(self, value):
        self.done = value
        return value

    def pause(self):
        self.tick = self.mark(anchor(self.after(self.tick)))


def pick(array, index):
    return lax.dynamic_index_in_dim(array, index, 0, keepdims=False)


def place():
    shard = lax.axis_index("shard")
    return lax.axis_index("rep"), shard // 4, (shard // 2) % 2, shard % 2


def arrival(half, first, second, step, rep, outer, mid, count):
    to_mid = jnp.where(half == 0, mid ^ second, mid ^ first)
    to_rep = jnp.where(half == 0, rep ^ first, rep ^ second)
    return to_mid, to_rep, lax.rem(outer + count - step, count)


def in_order(held, half):
    rep, outer, mid, _ = place()
    count = held.shape[2]
    flat = held.reshape((4,) + held.shape[2:])
    reps = []
    for want_rep in range(2):
        mids = []
        for want_mid in range(2):
            by_rep, by_mid = rep ^ want_rep, mid ^ want_mid
            second = jnp.where(half == 0, by_mid, by_rep)
            first = jnp.where(half == 0, by_rep, by_mid)
            piece = pick(flat, second * 2 + first)
            mids.append(
                jnp.concatenate([pick(piece, (outer - k) % count)[None] for k in range(count)], 0)
            )
        reps.append(jnp.stack(mids, 1))
    return jnp.stack(reps)


def assemble_kernel(where_ref, own_ref, came_ref, out_ref, sem):
    rep, outer, mid, core = (where_ref[k] for k in range(4))
    count, _, width = own_ref.shape[2:]
    for source, half in ((own_ref, core), (came_ref, 1 - core)):
        for second in range(2):
            for first in range(2):
                for step in range(count):
                    to_mid, to_rep, to_outer = arrival(
                        half, first, second, step, rep, outer, mid, count
                    )
                    column = pl.multiple_of((half * 2 + to_rep) * width, LANES)
                    pltpu.make_async_copy(
                        source.at[second, first, step],
                        out_ref.at[to_outer * 2 + to_mid, :, pl.ds(column, width)],
                        sem,
                    ).start()
    pltpu.make_async_copy(out_ref, out_ref, sem).wait()


def assemble(own, came, where):
    count, rows, width = own.shape[2:]
    core = where[3]
    shape = (2 * count * rows, 4 * width)
    if rows % 8 or width % LANES:
        halves = jnp.stack([in_order(own, core), in_order(came, 1 - core)])
        halves = jnp.stack([pick(halves, core), pick(halves, 1 - core)])
        return halves.transpose(2, 3, 4, 0, 1, 5).reshape(shape)
    out = pl.pallas_call(
        assemble_kernel,
        out_shape=jax.ShapeDtypeStruct((2 * count, rows, 4 * width), own.dtype),
        in_specs=[
            pl.BlockSpec(memory_space=pltpu.SMEM),
            pl.BlockSpec(memory_space=pl.ANY),
            pl.BlockSpec(memory_space=pl.ANY),
        ],
        out_specs=pl.BlockSpec(memory_space=pltpu.VMEM),
        scratch_shapes=[pltpu.SemaphoreType.DMA],
        compiler_params=pltpu.CompilerParams(vmem_limit_bytes=16 * MIB),
        cost_estimate=LONG,
        name="assemble",
    )(where, own, came)
    return out.reshape(shape)


def add_low(*terms):
    total = terms[0].astype(F32)
    for term in terms[1:]:
        total = total + term.astype(F32)
    return total.astype(BF16)


class Reduction:
    def __init__(self, terms, piece, shards):
        self.terms, self.piece, self.shards = terms, piece, shards

    def parts(self, where):
        return [self.piece(term, *where) for term in self.terms]

    def first(self, order, *way):
        rep, _, mid, core = place()
        got = order.after(*self.terms, *way)
        self.terms = got if isinstance(got, tuple) else (got,)
        away = [(1 - mid, 0), (1 - mid, 1)], [(0, 1 - rep), (1, 1 - rep)]
        sums = []
        for k in range(2):
            where = tuple(jnp.where(core == 0, away[0][k][d], away[1][k][d]) for d in range(2))
            sums.append(add_low(*self.parts(where)))
        self.way = hop(order.mark(jnp.stack(sums)), self.shards, first_move)

    def second(self, order):
        rep, _, mid, core = place()
        self.got = order.after(self.way)
        self.last = jnp.where(core == 0, rep, mid)
        k = 1 - self.last
        where = jnp.where(core == 0, mid, k), jnp.where(core == 0, k, rep)
        out = order.mark(add_low(*self.parts(where), pick(self.got, k)))
        self.way = hop(out, self.shards, second_move)

    def third(self, order):
        rep, _, mid, _ = place()
        came = order.after(self.way)
        return order.mark(add_low(*self.parts((mid, rep)), pick(self.got, self.last), came))


class OuterReduction:
    def __init__(self, mine, shards):
        self.mine, self.shards, self.bit = mine, shards, 1

    def send(self):
        outer = place()[1]
        count = self.mine.shape[0]
        pairs = self.mine.reshape((count // 2, 2) + self.mine.shape[1:])
        side = (outer // self.bit) % 2
        split = lambda which: lax.dynamic_index_in_dim(pairs, which, 1, keepdims=False)
        self.keep = split(side)
        move = lambda rep, outer, mid, core: (rep, outer ^ self.bit, mid, core)
        self.way = hop(split(1 - side), self.shards, move)

    def receive(self, order):
        keep, way = order.after(self.keep, self.way)
        self.mine = order.mark(add_low(keep, way))
        self.bit *= 2

    def finish(self, order):
        while self.mine.shape[0] > 1:
            self.send()
            self.receive(order)
        return pick(self.mine, 0)


def give_down(mine, shards):
    count = shards // 4
    half = count // 2
    pairs = []
    for r in range(2):
        for o in range(count):
            for m in range(2):
                for c in range(2):
                    if o // half != c:
                        base = r * shards + m * 2 + c
                        pairs.append((base + o * 4, base + (o ^ half) * 4))
    return lax.ppermute(mine, AXES, pairs)


def share_columns(total, shards, rep, core):
    rows = total.shape[0] // 2
    halves = total.reshape(2, rows, total.shape[1])
    mine, other = pick(halves, core), pick(halves, 1 - core)
    stack = jnp.stack(
        [
            mine,
            hop(mine, shards, rep_move),
            hop(other, shards, core_move),
            hop(other, shards, cross_move),
        ]
    )
    return [pick(stack, q ^ (core * 2 + rep)) for q in range(4)]


LONG = pl.CostEstimate(flops=200 * 10**9, bytes_accessed=0, transcendentals=0)
SHORT = pl.CostEstimate(flops=10**6, bytes_accessed=0, transcendentals=0)


def dot(left, right, left_dim, right_dim):
    return lax.dot_general(
        left, right, (((left_dim,), (right_dim,)), ((), ())), preferred_element_type=F32
    )


def anchor_kernel(in_ref, out_ref):
    for k in range(4):
        out_ref[k] = in_ref[k]


def anchor(tick):
    return pl.pallas_call(
        anchor_kernel,
        out_shape=jax.ShapeDtypeStruct(tick.shape, tick.dtype),
        in_specs=[pl.BlockSpec(memory_space=pltpu.SMEM)],
        out_specs=pl.BlockSpec(memory_space=pltpu.SMEM),
        cost_estimate=LONG,
        name="anchor",
    )(tick)


def project_kernel(normed_ref, weight_ref, cos_ref, sin_ref, out_ref):
    half = HD // 2
    turned = (HEADS + KV_HEADS) * HD
    cosine, sine = cos_ref[...], sin_ref[...]
    normed = normed_ref[...]
    for start in range(0, turned, 2 * LANES):
        raw = dot(weight_ref[:, start : start + 2 * LANES], normed, 0, 0)
        for at in range(0, 2 * LANES, HD):
            row = start + at
            scale = 0.125 if row < HEADS * HD else 1.0
            upper, lower = raw[at : at + half], raw[at + half : at + HD]
            out_ref[row : row + half] = ((upper * cosine - lower * sine) * scale).astype(BF16)
            out_ref[row + half : row + HD] = ((lower * cosine + upper * sine) * scale).astype(BF16)
    out_ref[turned:] = dot(
        weight_ref[:, turned : turned + KV_HEADS * HD], normed, 0, 0
    ).astype(BF16)


def project(normed_t, weight, cosine, sine):
    return pl.pallas_call(
        project_kernel,
        out_shape=jax.ShapeDtypeStruct(((HEADS + 2 * KV_HEADS) * HD, normed_t.shape[1]), BF16),
        compiler_params=pltpu.CompilerParams(vmem_limit_bytes=24 * MIB),
        cost_estimate=SHORT,
        name="project",
    )(normed_t, weight, cosine, sine)


def split_tokens(tokens):
    block = 256 if tokens % 256 == 0 else tokens
    return [(start, start + block) for start in range(0, tokens, block)]


def attend_kernel(seg_row_ref, seg_col_ref, q_ref, k_ref, v_ref, prob_ref, mixed_ref, bias_ref):
    tokens = q_ref.shape[1]

    @pl.when(pl.program_id(0) == 0)
    def _():
        keys = lax.broadcasted_iota(jnp.int32, (tokens, tokens), 0)
        queries = lax.broadcasted_iota(jnp.int32, (tokens, tokens), 1)
        allowed = (seg_col_ref[...] == seg_row_ref[...]) & (keys <= queries)
        bias_ref[...] = jnp.where(allowed, 0.0, NEG_FILL)

    for head in range(GROUP):
        rows = slice(head * HD, (head + 1) * HD)
        for start, stop in split_tokens(tokens):
            scores = dot(k_ref[:, :stop], q_ref[rows, start:stop], 0, 0)
            scores = scores + bias_ref[:stop, start:stop]
            expo = jnp.exp(scores - jnp.max(scores, 0, keepdims=True))
            prob = (expo * (1.0 / jnp.sum(expo, 0, keepdims=True))).astype(BF16)
            prob_ref[head, :stop, start:stop] = prob
            mixed_ref[rows, start:stop] = dot(v_ref[:, :stop], prob, 1, 0).astype(BF16)


def attend(qkv, seg_row):
    tokens = qkv.shape[1]
    return pl.pallas_call(
        attend_kernel,
        grid=(KV_HEADS,),
        out_shape=(
            jax.ShapeDtypeStruct((HEADS, tokens, tokens), BF16),
            jax.ShapeDtypeStruct((HEADS * HD, tokens), BF16),
        ),
        in_specs=[
            pl.BlockSpec((1, tokens), lambda i: (0, 0)),
            pl.BlockSpec((tokens, 1), lambda i: (0, 0)),
            pl.BlockSpec((GROUP * HD, tokens), lambda i: (i, 0)),
            pl.BlockSpec((HD, tokens), lambda i: (HEADS + i, 0)),
            pl.BlockSpec((HD, tokens), lambda i: (HEADS + KV_HEADS + i, 0)),
        ],
        out_specs=(
            pl.BlockSpec((GROUP, tokens, tokens), lambda i: (i, 0, 0)),
            pl.BlockSpec((GROUP * HD, tokens), lambda i: (i, 0)),
        ),
        scratch_shapes=[pltpu.VMEM((tokens, tokens), F32)],
        compiler_params=pltpu.CompilerParams(vmem_limit_bytes=32 * MIB),
        cost_estimate=LONG,
        name="attend",
    )(seg_row.reshape(1, tokens), seg_row.reshape(tokens, 1), qkv, qkv, qkv)


def out_columns(width):
    kept = (HEADS + 2 * KV_HEADS) * HD
    tail = -kept % LANES
    return kept + tail - LANES, LANES - tail, kept + tail


def branch_kernel(mixed_ref, weight_ref, tokens_ref, after_ref, scale_ref, normed_ref):
    mixed = mixed_ref[...]
    tile, skip, rest = out_columns(weight_ref.shape[1])
    wide = weight_ref.shape[1] - rest
    last = dot(weight_ref[:, tile : tile + LANES], mixed, 0, 0)
    after_ref[:wide] = tokens_ref[:wide].astype(F32) + dot(weight_ref[:, rest:], mixed, 0, 0)
    after_ref[wide:] = tokens_ref[wide:].astype(F32) + last[skip:]
    after = after_ref[...]
    scale = lax.rsqrt(jnp.mean(after * after, 0, keepdims=True) + EPSILON)
    scale_ref[...] = scale
    normed_ref[...] = (after * scale).astype(BF16)


def branch(mixed, weight, tokens):
    width, count = tokens.shape
    return pl.pallas_call(
        branch_kernel,
        out_shape=(
            jax.ShapeDtypeStruct((width, count), F32),
            jax.ShapeDtypeStruct((1, count), F32),
            jax.ShapeDtypeStruct((width, count), BF16),
        ),
        compiler_params=pltpu.CompilerParams(vmem_limit_bytes=24 * MIB),
        cost_estimate=SHORT,
        name="branch",
    )(mixed, weight, tokens)


def feed_kernel(
    ordered,
    offset,
    where_ref,
    normed_refs,
    cot_refs,
    pieces_refs,
    down_refs,
    down_grad_in_ref,
    before_refs,
    sum_refs,
    back_refs,
    grad_ref,
    down_grad_ref,
    normed,
    cot,
    weight,
    down_all,
    down,
    inner,
    pull,
    grad,
    down_grad,
    results,
    results_low,
    sems,
    out_sems,
):
    rep, outer, mid, core = (where_ref[k] for k in range(4))
    tokens = normed_refs[0].shape[1]
    units = down.shape[0]
    size = units // 2
    quarter = down_all.shape[0] // 2

    def load(index, copies):
        for source, to in copies:
            pltpu.make_async_copy(source, to, sems.at[index]).start()

    def ready(index, ref):
        pltpu.make_async_copy(ref, ref, sems.at[index]).wait()

    load(0, [(normed_refs[k], normed.at[:, pl.ds(k * tokens, tokens)]) for k in range(2)])
    for kind in range(2):
        if ordered:
            load(
                1 + kind,
                [
                    (
                        pieces_refs[0].at[k, :, pl.ds(kind * size, size)],
                        weight.at[0, :, pl.ds(kind * units + k * size, size)],
                    )
                    for k in range(2)
                ],
            )
            continue
        for second, source in enumerate(pieces_refs):
            for first in range(2):
                steps = source.shape[1]
                for step in range(steps):
                    to_mid, to_rep, to_outer = arrival(
                        core, first, second, step, rep, outer, mid, steps
                    )
                    column = pl.multiple_of(kind * units + to_rep * size, LANES)
                    load(
                        1 + kind,
                        [
                            (
                                source.at[first, step, :, pl.ds(kind * size, size)],
                                weight.at[to_outer * 2 + to_mid, :, pl.ds(column, size)],
                            )
                        ],
                    )
    load(3, [(cot_refs[k], cot.at[:, pl.ds(k * tokens, tokens)]) for k in range(2)])
    if ordered:
        load(4, [(down_refs[0], down_all)])
    else:
        steps, block = down_refs[0].shape[2:4]
        half = steps // 2
        for source, owner in ((down_refs[0], core), (down_refs[1], 1 - core)):
            for at in range(half):
                step = lax.rem(outer + steps - (core * half + at), steps)
                for second in range(2):
                    for first in range(2):
                        to_mid, to_rep, _ = arrival(owner, first, second, 0, rep, outer, mid, steps)
                        row = (((at * 2 + to_mid) * 2 + owner) * 2 + to_rep) * block
                        to = down_all.at[pl.ds(pl.multiple_of(row, 16), block)]
                        load(4, [(source.at[second, first, step], to)])

    if before_refs:
        load(5, [(before_refs[2 - 2 * k], results.at[k]) for k in range(2)])
        load(6, [(before_refs[3 - 2 * k], results_low.at[k]) for k in range(2)])

    ready(0, normed)
    ready(1, weight.at[:, :, pl.ds(0, units)])
    tile = 2 * LANES if units % (2 * LANES) == 0 else LANES

    def columns(start, count=tile):
        return weight[:, :, pl.ds(start, count)].reshape(normed.shape[0], count)

    for start in range(0, units, tile):
        at = pl.ds(start, tile)
        gate = dot(columns(start), normed[...], 0, 0)
        if start == 0:
            ready(2, weight.at[:, :, pl.ds(units, units)])
        up = dot(columns(units + start), normed[...], 0, 0)
        if start == 0:
            ready(3, cot)
            ready(4, down_all)
            down[:size] = down_all[offset : offset + size]
            down[size:] = down_all[quarter + offset : quarter + offset + size]
        inner_grad = dot(down[at], cot[...], 1, 0)
        sigma = 1.0 / (1.0 + jnp.exp(-gate))
        activ = gate * sigma
        inner[at] = (activ * up).astype(BF16)
        pull[at] = (inner_grad * up * (sigma + activ * (1.0 - sigma))).astype(BF16)
        pull[pl.ds(units + start, tile)] = (inner_grad * activ).astype(BF16)
        down_grad[at] = dot(inner[at], cot[...], 1, 1).astype(BF16)
    for rep in range(2):
        pltpu.make_async_copy(
            down_grad.at[pl.ds(rep * size, size)],
            down_grad_ref.at[rep, pl.ds(offset, size)],
            out_sems.at[0],
        ).start()
    for kind in range(2):
        for start in range(0, units, tile):
            at = pl.ds(kind * units + start, tile)
            grad[:, at] = dot(normed[...], pull[at], 1, 1).astype(BF16)
        for rep in range(2):
            pltpu.make_async_copy(
                grad.at[:, pl.ds(kind * units + rep * size, size)],
                grad_ref.at[rep, :, pl.ds(kind * size, size)],
                out_sems.at[1],
            ).start()
    for index, (out_refs, left, right, dim) in enumerate(
        ((back_refs, columns(0, 2 * units), pull, 1), (sum_refs, down[...], inner, 0))
    ):
        if before_refs and index == 0:
            ready(5, results)
            ready(6, results_low)
        low = dot(left, right[:, pl.ds(tokens, tokens)], dim, 0)
        if before_refs:
            low = low + results_low[index].astype(F32)
        results_low[index] = low.astype(BF16)
        pltpu.make_async_copy(results_low.at[index], out_refs[1], out_sems.at[2 + index]).start()
        total = dot(left, right[:, pl.ds(0, tokens)], dim, 0)
        results[index] = total + results[index] if before_refs else total
        pltpu.make_async_copy(results.at[index], out_refs[0], out_sems.at[4 + index]).start()
    pltpu.make_async_copy(down_grad, down_grad, out_sems.at[0]).wait()
    pltpu.make_async_copy(grad, grad, out_sems.at[1]).wait()
    for index in range(2):
        pltpu.make_async_copy(
            results_low.at[index], results_low.at[index], out_sems.at[2 + index]
        ).wait()
        pltpu.make_async_copy(results.at[index], results.at[index], out_sems.at[4 + index]).wait()


def feed(where, offset, normed, cot, pieces, down, down_grad, before):
    width, tokens = normed[0].shape
    size = pieces[0].shape[-1] // 2
    units = 2 * size
    count, block = down[0].shape[2:4]
    half_units = count * 4 * block
    rows = pieces[0].shape[2]
    ordered = rows % 8 != 0 or block % 16 != 0
    if ordered:
        core = where[3]
        pieces = (in_order(jnp.stack(pieces), core).reshape(2, width, units),)
        blocks = [in_order(array, half) for array, half in zip(down, (core, 1 - core))]
        blocks = jnp.stack([jnp.where(core == k, *blocks) for k in range(2)])
        blocks = blocks.transpose(2, 3, 0, 1, 4, 5).reshape(2, half_units, width)
        down = (pick(blocks, core),)
        rows = width
    first_call = down_grad is None
    operands = [*normed, *cot, *pieces, *down] + ([] if first_call else [down_grad, *before])
    split_before = len(before)
    split = len(down)

    def body(where_ref, *refs):
        refs = list(refs)
        take = lambda count: [refs.pop(0) for _ in range(count)]
        ins = take(2), take(2), take(len(pieces)), take(split)
        down_grad_in = None if first_call else take(1)[0]
        feed_kernel(
            ordered, offset, where_ref, *ins, down_grad_in, take(split_before), take(2), take(2), *refs
        )

    wide = jax.ShapeDtypeStruct((width, tokens), F32)
    low = jax.ShapeDtypeStruct((width, tokens), BF16)
    out_shape = (
        wide,
        low,
        wide,
        low,
        jax.ShapeDtypeStruct((2, width, units), BF16),
        jax.ShapeDtypeStruct((2, half_units // 2, width), BF16),
    )
    any_space = pl.BlockSpec(memory_space=pl.ANY)
    return pl.pallas_call(
        body,
        in_specs=[pl.BlockSpec(memory_space=pltpu.SMEM)] + [any_space] * len(operands),
        out_specs=(any_space,) * len(out_shape),
        out_shape=out_shape,
        scratch_shapes=[
            pltpu.VMEM((width, 2 * tokens), BF16),
            pltpu.VMEM((width, 2 * tokens), BF16),
            pltpu.VMEM((width // rows, rows, 2 * units), BF16),
            pltpu.VMEM((half_units, width), BF16),
            pltpu.VMEM((units, width), BF16),
            pltpu.VMEM((units, 2 * tokens), BF16),
            pltpu.VMEM((2 * units, 2 * tokens), BF16),
            pltpu.VMEM((width, 2 * units), BF16),
            pltpu.VMEM((units, width), BF16),
            pltpu.VMEM((2, width, tokens), F32),
            pltpu.VMEM((2, width, tokens), BF16),
            pltpu.SemaphoreType.DMA((7,)),
            pltpu.SemaphoreType.DMA((6,)),
        ],
        input_output_aliases={} if first_call else {len(operands) - split_before: 5},
        compiler_params=pltpu.CompilerParams(vmem_limit_bytes=52 * MIB),
        cost_estimate=LONG,
        name="feed",
    )(where, *operands)


def return_kernel(
    back_refs, after_ref, scale_ref, cot_ref, mixed_ref, weight_ref, grad_ref, mixed_grad_ref, out_grad_ref
):
    back = back_refs[0][...]
    for ref in back_refs[1:]:
        back = back + ref[...].astype(F32)
    after, scale = after_ref[...], scale_ref[...]
    mean = jnp.mean(back * after, 0, keepdims=True)
    grad = cot_ref[...].astype(F32) + scale * back - after * (scale * scale * scale * mean)
    grad_ref[...] = grad
    low = grad.astype(BF16)
    tile, skip, rest = out_columns(weight_ref.shape[1])
    wide = weight_ref.shape[1] - rest
    last = low[wide:]
    mixed_grad_ref[...] = (
        dot(weight_ref[:, rest:], low[:wide], 1, 0)
        + dot(weight_ref[:, tile + skip : rest], last, 1, 0)
    ).astype(BF16)
    mixed = mixed_ref[...]
    out_grad_ref[:, : LANES - skip] = dot(mixed, last, 1, 1).astype(BF16)
    out_grad_ref[:, LANES - skip :] = dot(mixed, low[:wide], 1, 1).astype(BF16)


def return_branch(backs, after, scale, cot, mixed, weight):
    width, count = after.shape

    def body(*refs):
        return_kernel(refs[: len(backs)], *refs[len(backs) :])

    return pl.pallas_call(
        body,
        out_shape=(
            jax.ShapeDtypeStruct((width, count), F32),
            jax.ShapeDtypeStruct((width, count), BF16),
            jax.ShapeDtypeStruct((width, width), BF16),
        ),
        compiler_params=pltpu.CompilerParams(vmem_limit_bytes=32 * MIB),
        cost_estimate=SHORT,
        name="return_branch",
    )(*backs, after, scale, cot, mixed, weight)


def attend_back_kernel(
    prob_ref, mixed_ref, grad_ref, q_ref, k_ref, v_ref, cos_ref, sin_ref, dq_ref, dk_ref, dv_ref
):
    half = HD // 2
    tokens = q_ref.shape[1]
    cosine, sine = cos_ref[...], sin_ref[...]
    key_grad = [None] * len(split_tokens(tokens))
    value_grad = [None] * len(split_tokens(tokens))

    def unturn(to_ref, row, grads, columns):
        upper, lower = grads[:half], grads[half:]
        c, s = cosine[:, columns], sine[:, columns]
        to_ref[row : row + half, columns] = (upper * c + lower * s).astype(BF16)
        to_ref[row + half : row + HD, columns] = (lower * c - upper * s).astype(BF16)

    for head in range(GROUP):
        rows = slice(head * HD, (head + 1) * HD)
        for block, (start, stop) in enumerate(split_tokens(tokens)):
            grad = grad_ref[rows, start:stop]
            mixed = mixed_ref[rows, start:stop]
            row_dot = jnp.sum(grad.astype(F32) * mixed.astype(F32), 0, keepdims=True)
            prob = prob_ref[head, :stop, start:stop]
            prob_grad = dot(v_ref[:, :stop], grad, 0, 0)
            score_grad = (prob.astype(F32) * (prob_grad - row_dot)).astype(BF16)
            unturn(
                dq_ref,
                head * HD,
                dot(k_ref[:, :stop], score_grad, 1, 0) * 0.125,
                slice(start, stop),
            )
            dk = dot(q_ref[rows, start:stop], score_grad, 1, 1)
            dv = dot(grad, prob, 1, 1)
            for part in range(block + 1):
                a, b = split_tokens(tokens)[part]
                if key_grad[part] is None:
                    key_grad[part], value_grad[part] = dk[:, a:b], dv[:, a:b]
                else:
                    key_grad[part] = key_grad[part] + dk[:, a:b]
                    value_grad[part] = value_grad[part] + dv[:, a:b]
    for part, (a, b) in enumerate(split_tokens(tokens)):
        unturn(dk_ref, 0, key_grad[part], slice(a, b))
        dv_ref[:, a:b] = value_grad[part].astype(BF16)


def attend_back(prob, mixed, grad, qkv, cosine, sine):
    tokens = qkv.shape[1]
    heads = pl.BlockSpec((GROUP * HD, tokens), lambda i: (i, 0))
    one = pl.BlockSpec((HD, tokens), lambda i: (i, 0))
    table = pl.BlockSpec((HD // 2, tokens), lambda i: (0, 0))
    return pl.pallas_call(
        attend_back_kernel,
        grid=(KV_HEADS,),
        out_shape=(
            jax.ShapeDtypeStruct((HEADS * HD, tokens), BF16),
            jax.ShapeDtypeStruct((KV_HEADS * HD, tokens), BF16),
            jax.ShapeDtypeStruct((KV_HEADS * HD, tokens), BF16),
        ),
        in_specs=[
            pl.BlockSpec((GROUP, tokens, tokens), lambda i: (i, 0, 0)),
            heads,
            heads,
            heads,
            pl.BlockSpec((HD, tokens), lambda i: (HEADS + i, 0)),
            pl.BlockSpec((HD, tokens), lambda i: (HEADS + KV_HEADS + i, 0)),
            table,
            table,
        ],
        out_specs=(heads, one, one),
        compiler_params=pltpu.CompilerParams(vmem_limit_bytes=32 * MIB),
        cost_estimate=SHORT,
        name="attend_back",
    )(prob, mixed, grad, qkv, qkv, qkv, cosine, sine)


def finish_grads_kernel(
    where_ref, normed_t_ref, dq_ref, dk_ref, dv_ref, out_grad_ref, keep_ref, send_ref, halves_ref
):
    normed_t = normed_t_ref[...]
    queries = dq_ref.shape[0]
    values = dv_ref.shape[0]
    halves_ref[0, :, :queries] = dot(normed_t, dq_ref[...], 1, 1).astype(BF16)
    halves_ref[0, :, queries:] = dot(normed_t, dk_ref[...], 1, 1).astype(BF16)
    halves_ref[1, :, :values] = dot(normed_t, dv_ref[...], 1, 1).astype(BF16)
    halves_ref[1, :, values:] = out_grad_ref[...]
    core = where_ref[3]
    keep_ref[...] = halves_ref[core]
    send_ref[...] = halves_ref[1 - core]


def finish_grads(where, normed_t, dq, dk, dv, out_grad):
    width = normed_t.shape[0]
    half = dq.shape[0] + dk.shape[0]
    shape = jax.ShapeDtypeStruct((width, half), BF16)
    vmem = pl.BlockSpec(memory_space=pltpu.VMEM)
    return pl.pallas_call(
        finish_grads_kernel,
        out_shape=(shape, shape),
        in_specs=[pl.BlockSpec(memory_space=pltpu.SMEM)] + [vmem] * 5,
        out_specs=(vmem, vmem),
        scratch_shapes=[pltpu.VMEM((2, width, half), BF16)],
        compiler_params=pltpu.CompilerParams(vmem_limit_bytes=24 * MIB),
        cost_estimate=LONG,
        name="finish_grads",
    )(where, normed_t, dq, dk, dv, out_grad)


def input_grad_kernel(
    dq_ref, dk_ref, dv_ref, weight_ref, tokens_ref, scale_ref, grad_ref, after_ref, sum_ref, came_ref,
    out_ref, output_ref,
):
    output_ref[...] = (after_ref[...] + sum_ref[...] + came_ref[...].astype(F32)).astype(BF16)
    queries, keys = dq_ref.shape[0], dk_ref.shape[0]
    end = queries + keys + dv_ref.shape[0]
    pull = dot(weight_ref[:, :queries], dq_ref[...], 1, 0)
    pull = pull + dot(weight_ref[:, queries : queries + keys], dk_ref[...], 1, 0)
    pull = pull + dot(weight_ref[:, queries + keys : end], dv_ref[...], 1, 0)
    values, scale = tokens_ref[...].astype(F32), scale_ref[...]
    mean = jnp.mean(pull * values, 0, keepdims=True)
    out_ref[...] = grad_ref[...] + scale * pull - values * (scale * scale * scale * mean)


def input_gradient(dq, dk, dv, weight, tokens, scale, grad, after, own, came):
    return pl.pallas_call(
        input_grad_kernel,
        out_shape=(
            jax.ShapeDtypeStruct(grad.shape, F32),
            jax.ShapeDtypeStruct(grad.shape, BF16),
        ),
        compiler_params=pltpu.CompilerParams(vmem_limit_bytes=24 * MIB),
        cost_estimate=LONG,
        name="input_gradient",
    )(dq, dk, dv, weight, tokens, scale, grad, after, own, came)


def per_device(
    shards,
    tokens,
    segment_ids,
    positions,
    norm_attn,
    w_qkv,
    w_out,
    norm_mlp,
    w_gate_up,
    w_down,
    cotangent,
):
    rep, outer, mid, core = place()
    where = jnp.stack([rep, outer, mid, core]).astype(jnp.int32)
    count = shards // 4
    width = tokens.shape[1]
    rows = w_qkv.shape[0]
    kept = w_qkv.shape[1]
    units = w_gate_up.shape[1] // 8
    gain_attn, gain_mlp = norm_attn.astype(F32)[:, None], norm_mlp.astype(F32)[:, None]

    qkv_block = (w_qkv.astype(F32) * gain_attn).astype(BF16)
    tail = -kept % LANES
    attn_block = jnp.concatenate([qkv_block, w_out[:, width - tail :], w_out[:, : width - tail]], 1)
    part = attn_block.shape[1] // 4

    big = -(-units // (2 * LANES)) * LANES
    chunks = ((0, big), (big, units - big))

    def attn_quarter(index):
        return lax.dynamic_slice(attn_block, (0, index * part), (rows, part))

    def feed_quarter(index):
        return jnp.concatenate(
            [
                lax.dynamic_slice(feed_block, (0, (kind * 4 + index) * units + start), (rows, size))
                for start, size in chunks
                for kind in range(2)
            ],
            1,
        )

    def chip_rows(mine, other):
        mine, other = order.after(mine, other)
        return order.mark(
            jnp.concatenate(
                [jnp.where(core == 0, mine, other), jnp.where(core == 0, other, mine)], 0
            )
        )

    order = Order(where)
    attn_mine = attn_quarter(core * 2 + rep)
    attn_other = hop(attn_quarter((1 - core) * 2 + rep), shards, core_move)
    attn_chip = chip_rows(attn_mine, attn_other)
    down_piece = pick(w_down.reshape(2, w_down.shape[0] // 2, width), rep)

    def outer_start(piece):
        return [piece] + [hop(piece, shards, outer_move(k, count)) for k in range(1, count)]

    def outer_stop(parts):
        return order.mark(jnp.stack(order.after(*parts)))

    def pair(held, came):
        return order.mark(jnp.stack(order.after(held, came)))

    tokens_t, cot_t = tokens.T, cotangent.T

    attn_way = outer_start(attn_chip)
    feed_block = (order.after(w_gate_up).astype(F32) * gain_mlp).astype(BF16)
    feed_mine = feed_quarter(core * 2 + rep)
    feed_other = hop(feed_quarter((1 - core) * 2 + rep), shards, core_move)
    cot_came = hop(cot_t, shards, core_move)
    half_dim = HD // 2
    freqs = ROPE_BASE ** (-2.0 * jnp.arange(half_dim, dtype=F32) / HD)
    angles = freqs[:, None] * positions[0].astype(F32)[None, :]
    cosine, sine = jnp.cos(angles), jnp.sin(angles)
    inputs = order.after(tokens_t).astype(F32)
    scale_attn = lax.rsqrt(jnp.mean(inputs * inputs, 0, keepdims=True) + EPSILON)
    normed_t = order.mark((inputs * scale_attn).astype(BF16))
    order.pause()
    cot_came = order.mark(order.after(cot_came))
    feed_chip = chip_rows(feed_mine, feed_other)
    attn_own = outer_stop(attn_way)
    attn_way = hop(attn_own, shards, second_move)
    down_way = outer_start(order.after(down_piece))
    order.pause()
    attn_own = pair(attn_own, attn_way)
    attn_way = hop(attn_own, shards, first_move)
    down_own = outer_stop(down_way)
    down_way = hop(down_own, shards, second_move)
    feed_way = outer_start(order.after(feed_chip))
    order.pause()
    attn_own = pair(attn_own, attn_way)
    attn_way = hop(attn_own, shards, core_move)
    order.pause()
    down_own = pair(down_own, down_way)
    down_way = hop(down_own, shards, first_move)
    attn_own, attn_way = order.after(attn_own, attn_way)
    attn_full = order.mark(assemble(attn_own, attn_way, where))
    qkv = order.mark(project(order.after(normed_t), attn_full, cosine, sine))
    feed_own = outer_stop(feed_way)
    feed_way = hop(feed_own, shards, second_move)
    prob, mixed = attend(order.after(qkv), segment_ids[0])
    order.mark(mixed)
    feed_own, feed_way = order.after(feed_own, feed_way)
    feed0_own = order.mark(jnp.stack([feed_own[..., : 2 * big], feed_way[..., : 2 * big]]))
    feed0_way = hop(feed0_own, shards, first_move)
    after_attn, scale_mlp, mlp_low = branch(order.after(mixed), attn_full, tokens_t)
    order.mark(mlp_low)
    low_came = hop(mlp_low, shards, core_move)
    down_own = pair(down_own, down_way)
    down_way = hop(down_own, shards, core_move)
    feed1_own = jnp.stack(order.after(feed_own[..., 2 * big :], feed_way[..., 2 * big :]))
    feed1_way = hop(order.mark(feed1_own), shards, first_move)
    order.pause()

    def run_feed(chunk, pieces, down_grad, before):
        own, way, low, cot, down = order.after(*pieces, low_came, cot_came, down_way)
        return feed(
            where, chunks[chunk][0], (mlp_low, low), (cot_t, cot), (own, way), (down_own, down), down_grad, before
        )

    *before, feed0_grad, down_grad = run_feed(0, (feed0_own, feed0_way), None, ())
    order.mark(feed0_grad)

    def feed_piece(array, to_mid, to_rep):
        array = array.reshape(2, count, 2, 2 * rows, array.shape[-1])
        return lax.dynamic_slice(
            array, (to_rep, 0, to_mid, 0, 0), (1, count, 1) + array.shape[3:]
        )[0, :, 0]

    feed0_sum = Reduction((feed0_grad,), feed_piece, shards)
    feed0_sum.first(order)
    sums, sums_other, back, back_other, feed1_grad, down_grad = run_feed(
        1, (feed1_own, feed1_way), down_grad, before
    )
    order.mark(feed1_grad)
    back_came = hop(back_other, shards, core_move)
    sums_came = hop(sums_other, shards, core_move)

    def down_piece_of(array, to_mid, to_rep):
        array = array.reshape(count // 2, 2, 2, 2, w_down.shape[0] // 2, width)
        return lax.dynamic_slice(
            array, (0, to_mid, 0, to_rep, 0, 0), (count // 2, 1, 2, 1) + array.shape[4:]
        )[:, 0, :, 0]

    feed1_sum = Reduction((feed1_grad,), feed_piece, shards)
    down_sum = Reduction((down_grad,), down_piece_of, shards)
    feed1_sum.first(order)
    feed0_sum.second(order)
    down_sum.first(order)
    order.pause()
    sums_came, back_came = order.after(sums_came, back_came)
    backs = (back, back_came)
    after_grad, mixed_grad, out_grad = return_branch(
        backs, after_attn, scale_mlp, cot_t, mixed, attn_full
    )
    order.mark(mixed_grad)
    dq, dk, dv = attend_back(prob, mixed, order.after(mixed_grad), qkv, cosine, sine)
    order.mark(dq)
    feed1_sum.second(order)
    feed0_out = OuterReduction(feed0_sum.third(order), shards)
    feed0_out.send()
    down_sum.second(order)
    keep_attn, send_attn = finish_grads(where, normed_t, order.after(dq), dk, dv, out_grad)
    order.mark(keep_attn)

    def attn_piece(array, to_mid, to_rep):
        array = array.reshape(count, 2, 2 * rows, 2 * part)
        return lax.dynamic_slice(
            array, (0, to_mid, 0, to_rep * part), (count, 1, 2 * rows, part)
        )[:, 0]

    attn_came = hop(send_attn, shards, core_move)
    feed1_out = OuterReduction(feed1_sum.third(order), shards)
    feed1_out.send()
    feed0_out.receive(order)
    feed0_out.send()
    down_out = OuterReduction(down_sum.third(order), shards)
    down_out.send()
    order.pause()
    attn_sum = Reduction((keep_attn, attn_came), attn_piece, shards)
    attn_sum.first(order)
    input_grad, output = input_gradient(
        order.after(dq), dk, dv, attn_full, tokens_t, scale_attn, after_grad, after_attn, sums, sums_came
    )
    order.mark(output)
    feed0_out.receive(order)
    feed0_total = feed0_out.finish(order)
    feed1_out.receive(order)
    feed1_out.send()
    down_out.receive(order)
    down_mine = down_out.finish(order)
    down_way = give_down(down_mine, shards)
    order.pause()
    attn_sum.second(order)
    feed1_out.receive(order)
    feed1_total = feed1_out.finish(order)
    feed_total = order.mark(jnp.concatenate(order.after(feed0_total, feed1_total), -1))
    order.pause()
    attn_out = OuterReduction(attn_sum.third(order), shards)
    attn_out.send()
    down_total = order.mark(add_low(*order.after(down_mine, down_way)))
    down_way = hop(pick(down_total, 1 - core), shards, core_move)
    feed_quarters = share_columns(order.after(feed_total), shards, rep, core)
    order.pause()
    attn_out.receive(order)
    attn_out.send()
    mine, came = order.after(pick(down_total, core), down_way)
    down_rows = order.mark(jnp.where(outer // (count // 2) == core, mine, came))
    down_way = hop(down_rows, shards, rep_move)
    feed_quarters = order.after(*feed_quarters)
    order.mark(feed_quarters[3])
    order.pause()
    attn_out.receive(order)
    rep, core = order.tick[0], order.tick[3]
    down_rows = jnp.stack(order.after(down_rows, down_way))
    attn_quarters = share_columns(attn_out.finish(order), shards, rep, core)
    down_rows = jnp.concatenate([pick(down_rows, rep), pick(down_rows, 1 - rep)], 0)
    grad_down = down_rows.astype(F32)

    attn_rows = jnp.concatenate(attn_quarters, 1).astype(F32)
    feed_rows = jnp.concatenate(
        [
            q[:, 2 * start + kind * size : 2 * start + (kind + 1) * size]
            for kind in range(2)
            for q in feed_quarters
            for start, size in chunks
        ],
        1,
    ).astype(F32)
    qkv_rows = attn_rows[:, :kept]
    grad_norm_attn = jnp.sum(qkv_rows * w_qkv.astype(F32), 1)
    grad_norm_mlp = jnp.sum(feed_rows * w_gate_up.astype(F32), 1)
    grad_out = jnp.concatenate([attn_rows[:, kept + tail :], attn_rows[:, kept : kept + tail]], 1)
    return (
        output.T,
        input_grad.T,
        grad_norm_attn,
        qkv_rows * gain_attn,
        grad_out,
        grad_norm_mlp,
        feed_rows * gain_mlp,
        grad_down,
    )


def solution(mesh):
    in_specs = (
        P(("rep", "shard"), None),
        P(("rep", "shard"), None),
        P(("rep", "shard"), None),
        P("shard"),
        P("shard", None),
        P("shard", None),
        P("shard"),
        P("shard", None),
        P("shard", None),
        P(("rep", "shard"), None),
    )
    out_specs = (
        P(("rep", "shard"), None),
        P(("rep", "shard"), None),
        P("shard"),
        P("shard", None),
        P("shard", None),
        P("shard"),
        P("shard", None),
        P("shard", None),
    )
    return jax.shard_map(
        functools.partial(per_device, mesh.shape["shard"]),
        mesh=mesh,
        in_specs=in_specs,
        out_specs=out_specs,
        check_vma=False,
    )
```

```python
import functools

import jax
import jax.numpy as jnp
from jax import lax
from jax.experimental import pallas as pl
from jax.experimental.pallas import tpu as pltpu
from jax.sharding import PartitionSpec as P

HEADS = 15
KV_HEADS = 5
HD = 64
GROUP = HEADS // KV_HEADS

EPSILON = 1e-05
ROPE_BASE = 100000.0
NEG_FILL = -1e30

AXES = ("rep", "shard")
F32 = jnp.float32
BF16 = jnp.bfloat16
LANES = 128
MIB = 1024 * 1024


def hop(values, shards, move):
    pairs = []
    for rep in range(2):
        for outer in range(shards // 4):
            for mid in range(2):
                for core in range(2):
                    to = move(rep, outer, mid, core)
                    pairs.append(
                        (
                            rep * shards + outer * 4 + mid * 2 + core,
                            to[0] * shards + to[1] * 4 + to[2] * 2 + to[3],
                        )
                    )
    return lax.ppermute(values, AXES, pairs)


def core_move(rep, outer, mid, core):
    return (rep, outer, mid, 1 - core)


def rep_move(rep, outer, mid, core):
    return (1 - rep, outer, mid, core)


def cross_move(rep, outer, mid, core):
    return (1 - rep, outer, mid, 1 - core)


def first_move(rep, outer, mid, core):
    return (rep, outer, 1 - mid, core) if core == 0 else (1 - rep, outer, mid, core)


def second_move(rep, outer, mid, core):
    return (1 - rep, outer, mid, core) if core == 0 else (rep, outer, 1 - mid, core)


def outer_move(step, count):
    return lambda rep, outer, mid, core: (rep, (outer + step) % count, mid, core)


class Order:
    def __init__(self, tick):
        self.done = None
        self.tick = tick

    def after(self, *values):
        if self.done is not None:
            values = lax.optimization_barrier(tuple(values) + (self.done,))[:-1]
        return values if len(values) > 1 else values[0]

    def mark(self, value):
        self.done = value
        return value

    def pause(self):
        self.tick = self.mark(anchor(self.after(self.tick)))


def pick(array, index):
    return lax.dynamic_index_in_dim(array, index, 0, keepdims=False)


def place():
    shard = lax.axis_index("shard")
    return lax.axis_index("rep"), shard // 4, (shard // 2) % 2, shard % 2


def arrival(half, first, second, step, rep, outer, mid, count):
    to_mid = jnp.where(half == 0, mid ^ second, mid ^ first)
    to_rep = jnp.where(half == 0, rep ^ first, rep ^ second)
    return to_mid, to_rep, lax.rem(outer + count - step, count)


def in_order(held, half):
    rep, outer, mid, _ = place()
    count = held.shape[2]
    flat = held.reshape((4,) + held.shape[2:])
    reps = []
    for want_rep in range(2):
        mids = []
        for want_mid in range(2):
            by_rep, by_mid = rep ^ want_rep, mid ^ want_mid
            second = jnp.where(half == 0, by_mid, by_rep)
            first = jnp.where(half == 0, by_rep, by_mid)
            piece = pick(flat, second * 2 + first)
            mids.append(
                jnp.concatenate([pick(piece, (outer - k) % count)[None] for k in range(count)], 0)
            )
        reps.append(jnp.stack(mids, 1))
    return jnp.stack(reps)


def assemble_kernel(where_ref, own_ref, came_ref, out_ref, sem):
    rep, outer, mid, core = (where_ref[k] for k in range(4))
    count, _, width = own_ref.shape[2:]
    for source, half in ((own_ref, core), (came_ref, 1 - core)):
        for second in range(2):
            for first in range(2):
                for step in range(count):
                    to_mid, to_rep, to_outer = arrival(
                        half, first, second, step, rep, outer, mid, count
                    )
                    column = pl.multiple_of((half * 2 + to_rep) * width, LANES)
                    pltpu.make_async_copy(
                        source.at[second, first, step],
                        out_ref.at[to_outer * 2 + to_mid, :, pl.ds(column, width)],
                        sem,
                    ).start()
    pltpu.make_async_copy(out_ref, out_ref, sem).wait()


def assemble(own, came, where):
    count, rows, width = own.shape[2:]
    core = where[3]
    shape = (2 * count * rows, 4 * width)
    if rows % 8 or width % LANES:
        halves = jnp.stack([in_order(own, core), in_order(came, 1 - core)])
        halves = jnp.stack([pick(halves, core), pick(halves, 1 - core)])
        return halves.transpose(2, 3, 4, 0, 1, 5).reshape(shape)
    out = pl.pallas_call(
        assemble_kernel,
        out_shape=jax.ShapeDtypeStruct((2 * count, rows, 4 * width), own.dtype),
        in_specs=[
            pl.BlockSpec(memory_space=pltpu.SMEM),
            pl.BlockSpec(memory_space=pl.ANY),
            pl.BlockSpec(memory_space=pl.ANY),
        ],
        out_specs=pl.BlockSpec(memory_space=pltpu.VMEM),
        scratch_shapes=[pltpu.SemaphoreType.DMA],
        compiler_params=pltpu.CompilerParams(vmem_limit_bytes=16 * MIB),
        cost_estimate=LONG,
        name="assemble",
    )(where, own, came)
    return out.reshape(shape)


def add_low(*terms):
    total = terms[0].astype(F32)
    for term in terms[1:]:
        total = total + term.astype(F32)
    return total.astype(BF16)


class Reduction:
    def __init__(self, terms, piece, shards):
        self.terms, self.piece, self.shards = terms, piece, shards

    def parts(self, where):
        return [self.piece(term, *where) for term in self.terms]

    def first(self, order, *way):
        rep, _, mid, core = place()
        got = order.after(*self.terms, *way)
        self.terms = got if isinstance(got, tuple) else (got,)
        away = [(1 - mid, 0), (1 - mid, 1)], [(0, 1 - rep), (1, 1 - rep)]
        sums = []
        for k in range(2):
            where = tuple(jnp.where(core == 0, away[0][k][d], away[1][k][d]) for d in range(2))
            sums.append(add_low(*self.parts(where)))
        self.way = hop(order.mark(jnp.stack(sums)), self.shards, first_move)

    def second(self, order):
        rep, _, mid, core = place()
        self.got = order.after(self.way)
        self.last = jnp.where(core == 0, rep, mid)
        k = 1 - self.last
        where = jnp.where(core == 0, mid, k), jnp.where(core == 0, k, rep)
        out = order.mark(add_low(*self.parts(where), pick(self.got, k)))
        self.way = hop(out, self.shards, second_move)

    def third(self, order):
        rep, _, mid, _ = place()
        came = order.after(self.way)
        return order.mark(add_low(*self.parts((mid, rep)), pick(self.got, self.last), came))


class SlotReduction:
    def __init__(self, keep, send, shards):
        rep, _, mid, core = place()
        self.last = jnp.where(core == 0, rep, mid)
        self.keep, self.shards = keep, shards
        self.way = hop(send, shards, first_move)

    def second(self, order):
        self.got = order.after(self.way)
        k = 1 - self.last
        out = order.mark(add_low(pick(self.keep, k), pick(self.got, k)))
        self.way = hop(out, self.shards, second_move)

    def third(self, order):
        came = order.after(self.way)
        return order.mark(add_low(pick(self.keep, self.last), pick(self.got, self.last), came))


class OuterReduction:
    def __init__(self, mine, shards):
        self.mine, self.shards, self.bit = mine, shards, 1

    def send(self):
        outer = place()[1]
        count = self.mine.shape[0]
        pairs = self.mine.reshape((count // 2, 2) + self.mine.shape[1:])
        side = (outer // self.bit) % 2
        split = lambda which: lax.dynamic_index_in_dim(pairs, which, 1, keepdims=False)
        self.keep = split(side)
        move = lambda rep, outer, mid, core: (rep, outer ^ self.bit, mid, core)
        self.way = hop(split(1 - side), self.shards, move)

    def receive(self, order):
        keep, way = order.after(self.keep, self.way)
        self.mine = order.mark(add_low(keep, way))
        self.bit *= 2

    def finish(self, order):
        while self.mine.shape[0] > 1:
            self.send()
            self.receive(order)
        return pick(self.mine, 0)


def give_down(mine, shards):
    count = shards // 4
    half = count // 2
    pairs = []
    for r in range(2):
        for o in range(count):
            for m in range(2):
                for c in range(2):
                    if o // half != c:
                        base = r * shards + m * 2 + c
                        pairs.append((base + o * 4, base + (o ^ half) * 4))
    return lax.ppermute(mine, AXES, pairs)


def share_columns(total, shards, rep, core):
    rows = total.shape[0] // 2
    halves = total.reshape(2, rows, total.shape[1])
    mine, other = pick(halves, core), pick(halves, 1 - core)
    stack = jnp.stack(
        [
            mine,
            hop(mine, shards, rep_move),
            hop(other, shards, core_move),
            hop(other, shards, cross_move),
        ]
    )
    return [pick(stack, q ^ (core * 2 + rep)) for q in range(4)]


LONG = pl.CostEstimate(flops=200 * 10**9, bytes_accessed=0, transcendentals=0)
SHORT = pl.CostEstimate(flops=10**6, bytes_accessed=0, transcendentals=0)


def dot(left, right, left_dim, right_dim):
    return lax.dot_general(
        left, right, (((left_dim,), (right_dim,)), ((), ())), preferred_element_type=F32
    )


def anchor_kernel(in_ref, out_ref):
    if len(in_ref.shape) == 1:
        for k in range(4):
            out_ref[k] = in_ref[k]
    else:
        out_ref[...] = in_ref[...]


def anchor(tick):
    space = pl.BlockSpec(memory_space=pltpu.SMEM if tick.ndim == 1 else pltpu.VMEM)
    return pl.pallas_call(
        anchor_kernel,
        out_shape=jax.ShapeDtypeStruct(tick.shape, tick.dtype),
        in_specs=[space],
        out_specs=space,
        cost_estimate=LONG,
        name="anchor",
    )(tick)


def project_kernel(normed_ref, weight_ref, cos_ref, sin_ref, out_ref):
    half = HD // 2
    turned = (HEADS + KV_HEADS) * HD
    cosine, sine = cos_ref[...], sin_ref[...]
    normed = normed_ref[...]
    for start in range(0, turned, 2 * LANES):
        raw = dot(weight_ref[:, start : start + 2 * LANES], normed, 0, 0)
        for at in range(0, 2 * LANES, HD):
            row = start + at
            scale = 0.125 if row < HEADS * HD else 1.0
            upper, lower = raw[at : at + half], raw[at + half : at + HD]
            out_ref[row : row + half] = ((upper * cosine - lower * sine) * scale).astype(BF16)
            out_ref[row + half : row + HD] = ((lower * cosine + upper * sine) * scale).astype(BF16)
    out_ref[turned:] = dot(
        weight_ref[:, turned : turned + KV_HEADS * HD], normed, 0, 0
    ).astype(BF16)


def project(normed_t, weight, cosine, sine):
    return pl.pallas_call(
        project_kernel,
        out_shape=jax.ShapeDtypeStruct(((HEADS + 2 * KV_HEADS) * HD, normed_t.shape[1]), BF16),
        compiler_params=pltpu.CompilerParams(vmem_limit_bytes=24 * MIB),
        cost_estimate=SHORT,
        name="project",
    )(normed_t, weight, cosine, sine)


def split_tokens(tokens):
    block = 256 if tokens % 256 == 0 else tokens
    return [(start, start + block) for start in range(0, tokens, block)]


def attend_kernel(seg_row_ref, seg_col_ref, q_ref, k_ref, v_ref, prob_ref, mixed_ref, bias_ref):
    tokens = q_ref.shape[1]

    @pl.when(pl.program_id(0) == 0)
    def _():
        keys = lax.broadcasted_iota(jnp.int32, (tokens, tokens), 0)
        queries = lax.broadcasted_iota(jnp.int32, (tokens, tokens), 1)
        allowed = (seg_col_ref[...] == seg_row_ref[...]) & (keys <= queries)
        bias_ref[...] = jnp.where(allowed, 0.0, NEG_FILL)

    for head in range(GROUP):
        rows = slice(head * HD, (head + 1) * HD)
        for start, stop in split_tokens(tokens):
            scores = dot(k_ref[:, :stop], q_ref[rows, start:stop], 0, 0)
            scores = scores + bias_ref[:stop, start:stop]
            expo = jnp.exp(scores - jnp.max(scores, 0, keepdims=True))
            prob = (expo * (1.0 / jnp.sum(expo, 0, keepdims=True))).astype(BF16)
            prob_ref[head, :stop, start:stop] = prob
            mixed_ref[rows, start:stop] = dot(v_ref[:, :stop], prob, 1, 0).astype(BF16)


def attend(qkv, seg_row):
    tokens = qkv.shape[1]
    return pl.pallas_call(
        attend_kernel,
        grid=(KV_HEADS,),
        out_shape=(
            jax.ShapeDtypeStruct((HEADS, tokens, tokens), BF16),
            jax.ShapeDtypeStruct((HEADS * HD, tokens), BF16),
        ),
        in_specs=[
            pl.BlockSpec((1, tokens), lambda i: (0, 0)),
            pl.BlockSpec((tokens, 1), lambda i: (0, 0)),
            pl.BlockSpec((GROUP * HD, tokens), lambda i: (i, 0)),
            pl.BlockSpec((HD, tokens), lambda i: (HEADS + i, 0)),
            pl.BlockSpec((HD, tokens), lambda i: (HEADS + KV_HEADS + i, 0)),
        ],
        out_specs=(
            pl.BlockSpec((GROUP, tokens, tokens), lambda i: (i, 0, 0)),
            pl.BlockSpec((GROUP * HD, tokens), lambda i: (i, 0)),
        ),
        scratch_shapes=[pltpu.VMEM((tokens, tokens), F32)],
        compiler_params=pltpu.CompilerParams(vmem_limit_bytes=32 * MIB),
        cost_estimate=LONG,
        name="attend",
    )(seg_row.reshape(1, tokens), seg_row.reshape(tokens, 1), qkv, qkv, qkv)


def out_columns(width):
    kept = (HEADS + 2 * KV_HEADS) * HD
    tail = -kept % LANES
    return kept + tail - LANES, LANES - tail, kept + tail


def branch_kernel(mixed_ref, weight_ref, tokens_ref, after_ref, scale_ref, normed_ref):
    mixed = mixed_ref[...]
    tile, skip, rest = out_columns(weight_ref.shape[1])
    wide = weight_ref.shape[1] - rest
    last = dot(weight_ref[:, tile : tile + LANES], mixed, 0, 0)
    after_ref[:wide] = tokens_ref[:wide].astype(F32) + dot(weight_ref[:, rest:], mixed, 0, 0)
    after_ref[wide:] = tokens_ref[wide:].astype(F32) + last[skip:]
    after = after_ref[...]
    scale = lax.rsqrt(jnp.mean(after * after, 0, keepdims=True) + EPSILON)
    scale_ref[...] = scale
    normed_ref[...] = (after * scale).astype(BF16)


def branch(mixed, weight, tokens):
    width, count = tokens.shape
    return pl.pallas_call(
        branch_kernel,
        out_shape=(
            jax.ShapeDtypeStruct((width, count), F32),
            jax.ShapeDtypeStruct((1, count), F32),
            jax.ShapeDtypeStruct((width, count), BF16),
        ),
        compiler_params=pltpu.CompilerParams(vmem_limit_bytes=24 * MIB),
        cost_estimate=SHORT,
        name="branch",
    )(mixed, weight, tokens)


def feed_kernel(
    ordered,
    offset,
    where_ref,
    normed_refs,
    cot_refs,
    pieces_refs,
    down_refs,
    down_grad_in_ref,
    before_refs,
    sum_refs,
    back_refs,
    grad_refs,
    down_grad_ref,
    normed,
    cot,
    weight,
    down_all,
    down,
    inner,
    pull,
    grad,
    down_grad,
    results,
    results_low,
    sems,
    out_sems,
):
    rep, outer, mid, core = (where_ref[k] for k in range(4))
    tokens = normed_refs[0].shape[1]
    units = down.shape[0]
    size = units // 2
    quarter = down_all.shape[0] // 2

    def load(index, copies):
        for source, to in copies:
            pltpu.make_async_copy(source, to, sems.at[index]).start()

    def ready(index, ref):
        pltpu.make_async_copy(ref, ref, sems.at[index]).wait()

    load(0, [(normed_refs[k], normed.at[:, pl.ds(k * tokens, tokens)]) for k in range(2)])
    for kind in range(2):
        if ordered:
            load(
                1 + kind,
                [
                    (
                        pieces_refs[0].at[k, :, pl.ds(kind * size, size)],
                        weight.at[0, :, pl.ds(kind * units + k * size, size)],
                    )
                    for k in range(2)
                ],
            )
            continue
        for second, source in enumerate(pieces_refs):
            for first in range(2):
                steps = source.shape[1]
                for step in range(steps):
                    to_mid, to_rep, to_outer = arrival(
                        core, first, second, step, rep, outer, mid, steps
                    )
                    column = pl.multiple_of(kind * units + to_rep * size, LANES)
                    load(
                        1 + kind,
                        [
                            (
                                source.at[first, step, :, pl.ds(kind * size, size)],
                                weight.at[to_outer * 2 + to_mid, :, pl.ds(column, size)],
                            )
                        ],
                    )
    load(3, [(cot_refs[k], cot.at[:, pl.ds(k * tokens, tokens)]) for k in range(2)])
    if ordered:
        load(4, [(down_refs[0], down_all)])
    else:
        steps, block = down_refs[0].shape[2:4]
        half = steps // 2
        for source, owner in ((down_refs[0], core), (down_refs[1], 1 - core)):
            for at in range(half):
                step = lax.rem(outer + steps - (core * half + at), steps)
                for second in range(2):
                    for first in range(2):
                        to_mid, to_rep, _ = arrival(owner, first, second, 0, rep, outer, mid, steps)
                        row = (((at * 2 + to_mid) * 2 + owner) * 2 + to_rep) * block
                        to = down_all.at[pl.ds(pl.multiple_of(row, 16), block)]
                        load(4, [(source.at[second, first, step], to)])

    if before_refs:
        load(5, [(before_refs[2 - 2 * k], results.at[k]) for k in range(2)])
        load(6, [(before_refs[3 - 2 * k], results_low.at[k]) for k in range(2)])

    ready(0, normed)
    ready(1, weight.at[:, :, pl.ds(0, units)])
    tile = 2 * LANES if units % (2 * LANES) == 0 else LANES

    def columns(start, count=tile):
        return weight[:, :, pl.ds(start, count)].reshape(normed.shape[0], count)

    for start in range(0, units, tile):
        at = pl.ds(start, tile)
        gate = dot(columns(start), normed[...], 0, 0)
        if start == 0:
            ready(2, weight.at[:, :, pl.ds(units, units)])
        up = dot(columns(units + start), normed[...], 0, 0)
        if start == 0:
            ready(3, cot)
            ready(4, down_all)
            down[:size] = down_all[offset : offset + size]
            down[size:] = down_all[quarter + offset : quarter + offset + size]
        inner_grad = dot(down[at], cot[...], 1, 0)
        sigma = 1.0 / (1.0 + jnp.exp(-gate))
        activ = gate * sigma
        inner[at] = (activ * up).astype(BF16)
        pull[at] = (inner_grad * up * (sigma + activ * (1.0 - sigma))).astype(BF16)
        pull[pl.ds(units + start, tile)] = (inner_grad * activ).astype(BF16)
        down_grad[at] = dot(inner[at], cot[...], 1, 1).astype(BF16)
    for k in range(2):
        pltpu.make_async_copy(
            down_grad.at[pl.ds(k * size, size)],
            down_grad_ref.at[k, pl.ds(offset, size)],
            out_sems.at[0],
        ).start()
    for kind in range(2):
        for start in range(0, units, tile):
            at = pl.ds(kind * units + start, tile)
            part = dot(normed[...], pull[at], 1, 1)
            if ordered:
                grad[0, :, at] = part.astype(BF16)
            else:
                grad[:, :, at] = part.reshape(*grad.shape[:2], tile).astype(BF16)
        for to_rep in range(2):
            source_at = pl.ds(kind * units + to_rep * size, size)
            target_at = pl.ds(kind * size, size)
            if ordered:
                pltpu.make_async_copy(
                    grad.at[0, :, source_at], grad_refs[0].at[to_rep, :, target_at], out_sems.at[1]
                ).start()
                continue
            for at in range(grad.shape[0]):
                to_outer, to_mid = at // 2, at % 2
                for which in range(2):
                    slot, mine = (to_mid, rep == to_rep) if which else (to_rep, mid == to_mid)
                    for ref, wanted in zip(grad_refs, (mine, jnp.logical_not(mine))):

                        @pl.when(jnp.logical_and(core == which, wanted))
                        def _():
                            pltpu.make_async_copy(
                                grad.at[at, :, source_at],
                                ref.at[slot, to_outer, :, target_at],
                                out_sems.at[1],
                            ).start()
    for index, (out_refs, left, right, dim) in enumerate(
        ((back_refs, columns(0, 2 * units), pull, 1), (sum_refs, down[...], inner, 0))
    ):
        if before_refs and index == 0:
            ready(5, results)
            ready(6, results_low)
        low = dot(left, right[:, pl.ds(tokens, tokens)], dim, 0)
        if before_refs:
            low = low + results_low[index].astype(F32)
        results_low[index] = low.astype(BF16)
        pltpu.make_async_copy(results_low.at[index], out_refs[1], out_sems.at[2 + index]).start()
        total = dot(left, right[:, pl.ds(0, tokens)], dim, 0)
        results[index] = total + results[index] if before_refs else total
        pltpu.make_async_copy(results.at[index], out_refs[0], out_sems.at[4 + index]).start()
    pltpu.make_async_copy(down_grad, down_grad, out_sems.at[0]).wait()
    pltpu.make_async_copy(grad, grad, out_sems.at[1]).wait()
    for index in range(2):
        pltpu.make_async_copy(
            results_low.at[index], results_low.at[index], out_sems.at[2 + index]
        ).wait()
        pltpu.make_async_copy(results.at[index], results.at[index], out_sems.at[4 + index]).wait()


def feed(where, offset, normed, cot, pieces, down, down_grad, before):
    width, tokens = normed[0].shape
    size = pieces[0].shape[-1] // 2
    units = 2 * size
    count, block = down[0].shape[2:4]
    half_units = count * 4 * block
    rows = pieces[0].shape[2]
    ordered = rows % 8 != 0 or block % 16 != 0
    if ordered:
        core = where[3]
        pieces = (in_order(jnp.stack(pieces), core).reshape(2, width, units),)
        blocks = [in_order(array, half) for array, half in zip(down, (core, 1 - core))]
        blocks = jnp.stack([jnp.where(core == k, *blocks) for k in range(2)])
        blocks = blocks.transpose(2, 3, 0, 1, 4, 5).reshape(2, half_units, width)
        down = (pick(blocks, core),)
        rows = width
    first_call = down_grad is None
    operands = [*normed, *cot, *pieces, *down] + ([] if first_call else [down_grad, *before])
    split_before = len(before)
    split = len(down)

    def body(where_ref, *refs):
        refs = list(refs)
        take = lambda count: [refs.pop(0) for _ in range(count)]
        ins = take(2), take(2), take(len(pieces)), take(split)
        down_grad_in = None if first_call else take(1)[0]
        feed_kernel(
            ordered, offset, where_ref, *ins, down_grad_in, take(split_before), take(2), take(2), take(len(grads)), *refs
        )

    wide = jax.ShapeDtypeStruct((width, tokens), F32)
    low = jax.ShapeDtypeStruct((width, tokens), BF16)
    if ordered:
        grads = [jax.ShapeDtypeStruct((2, width, units), BF16)]
    else:
        grads = [jax.ShapeDtypeStruct((2, count, rows, units), BF16)] * 2
    out_shape = (
        wide,
        low,
        wide,
        low,
        *grads,
        jax.ShapeDtypeStruct((2, half_units // 2, width), BF16),
    )
    any_space = pl.BlockSpec(memory_space=pl.ANY)
    *sums, down_grad = pl.pallas_call(
        body,
        in_specs=[pl.BlockSpec(memory_space=pltpu.SMEM)] + [any_space] * len(operands),
        out_specs=(any_space,) * len(out_shape),
        out_shape=out_shape,
        scratch_shapes=[
            pltpu.VMEM((width, 2 * tokens), BF16),
            pltpu.VMEM((width, 2 * tokens), BF16),
            pltpu.VMEM((width // rows, rows, 2 * units), BF16),
            pltpu.VMEM((half_units, width), BF16),
            pltpu.VMEM((units, width), BF16),
            pltpu.VMEM((units, 2 * tokens), BF16),
            pltpu.VMEM((2 * units, 2 * tokens), BF16),
            pltpu.VMEM((width // rows, rows, 2 * units), BF16),
            pltpu.VMEM((units, width), BF16),
            pltpu.VMEM((2, width, tokens), F32),
            pltpu.VMEM((2, width, tokens), BF16),
            pltpu.SemaphoreType.DMA((7,)),
            pltpu.SemaphoreType.DMA((6,)),
        ],
        input_output_aliases={} if first_call else {len(operands) - split_before: 4 + len(grads)},
        compiler_params=pltpu.CompilerParams(vmem_limit_bytes=52 * MIB),
        cost_estimate=LONG,
        name="feed",
    )(where, *operands)
    if ordered:
        sums = (*sums[:4], *slots(sums[4], where, count))
    return (*sums, down_grad)


def slots(grad, where, count):
    rep, _, mid, core = (where[k] for k in range(4))
    blocks = grad.reshape(2, count, 2, -1, grad.shape[-1])

    def piece(to_mid, to_rep):
        return lax.dynamic_slice(
            blocks, (to_rep, 0, to_mid, 0, 0), (1, count, 1) + blocks.shape[3:]
        )[0, :, 0]

    keep = [piece(jnp.where(core == 0, mid, k), jnp.where(core == 0, k, rep)) for k in range(2)]
    send = [
        piece(jnp.where(core == 0, 1 - mid, k), jnp.where(core == 0, k, 1 - rep)) for k in range(2)
    ]
    return jnp.stack(keep), jnp.stack(send)


def return_kernel(
    back_refs, after_ref, scale_ref, cot_ref, mixed_ref, weight_ref, grad_ref, mixed_grad_ref, out_grad_ref
):
    back = back_refs[0][...]
    for ref in back_refs[1:]:
        back = back + ref[...].astype(F32)
    after, scale = after_ref[...], scale_ref[...]
    mean = jnp.mean(back * after, 0, keepdims=True)
    grad = cot_ref[...].astype(F32) + scale * back - after * (scale * scale * scale * mean)
    grad_ref[...] = grad
    low = grad.astype(BF16)
    tile, skip, rest = out_columns(weight_ref.shape[1])
    wide = weight_ref.shape[1] - rest
    last = low[wide:]
    mixed_grad_ref[...] = (
        dot(weight_ref[:, rest:], low[:wide], 1, 0)
        + dot(weight_ref[:, tile + skip : rest], last, 1, 0)
    ).astype(BF16)
    mixed = mixed_ref[...]
    out_grad_ref[:, : LANES - skip] = dot(mixed, last, 1, 1).astype(BF16)
    out_grad_ref[:, LANES - skip :] = dot(mixed, low[:wide], 1, 1).astype(BF16)


def return_branch(backs, after, scale, cot, mixed, weight):
    width, count = after.shape

    def body(*refs):
        return_kernel(refs[: len(backs)], *refs[len(backs) :])

    return pl.pallas_call(
        body,
        out_shape=(
            jax.ShapeDtypeStruct((width, count), F32),
            jax.ShapeDtypeStruct((width, count), BF16),
            jax.ShapeDtypeStruct((width, width), BF16),
        ),
        compiler_params=pltpu.CompilerParams(vmem_limit_bytes=32 * MIB),
        cost_estimate=SHORT,
        name="return_branch",
    )(*backs, after, scale, cot, mixed, weight)


def attend_back_kernel(
    prob_ref, mixed_ref, grad_ref, q_ref, k_ref, v_ref, cos_ref, sin_ref, dq_ref, dk_ref, dv_ref
):
    half = HD // 2
    tokens = q_ref.shape[1]
    cosine, sine = cos_ref[...], sin_ref[...]
    key_grad = [None] * len(split_tokens(tokens))
    value_grad = [None] * len(split_tokens(tokens))

    def unturn(to_ref, row, grads, columns):
        upper, lower = grads[:half], grads[half:]
        c, s = cosine[:, columns], sine[:, columns]
        to_ref[row : row + half, columns] = (upper * c + lower * s).astype(BF16)
        to_ref[row + half : row + HD, columns] = (lower * c - upper * s).astype(BF16)

    for head in range(GROUP):
        rows = slice(head * HD, (head + 1) * HD)
        for block, (start, stop) in enumerate(split_tokens(tokens)):
            grad = grad_ref[rows, start:stop]
            mixed = mixed_ref[rows, start:stop]
            row_dot = jnp.sum(grad.astype(F32) * mixed.astype(F32), 0, keepdims=True)
            prob = prob_ref[head, :stop, start:stop]
            prob_grad = dot(v_ref[:, :stop], grad, 0, 0)
            score_grad = (prob.astype(F32) * (prob_grad - row_dot)).astype(BF16)
            unturn(
                dq_ref,
                head * HD,
                dot(k_ref[:, :stop], score_grad, 1, 0) * 0.125,
                slice(start, stop),
            )
            dk = dot(q_ref[rows, start:stop], score_grad, 1, 1)
            dv = dot(grad, prob, 1, 1)
            for part in range(block + 1):
                a, b = split_tokens(tokens)[part]
                if key_grad[part] is None:
                    key_grad[part], value_grad[part] = dk[:, a:b], dv[:, a:b]
                else:
                    key_grad[part] = key_grad[part] + dk[:, a:b]
                    value_grad[part] = value_grad[part] + dv[:, a:b]
    for part, (a, b) in enumerate(split_tokens(tokens)):
        unturn(dk_ref, 0, key_grad[part], slice(a, b))
        dv_ref[:, a:b] = value_grad[part].astype(BF16)


def attend_back(prob, mixed, grad, qkv, cosine, sine):
    tokens = qkv.shape[1]
    heads = pl.BlockSpec((GROUP * HD, tokens), lambda i: (i, 0))
    one = pl.BlockSpec((HD, tokens), lambda i: (i, 0))
    table = pl.BlockSpec((HD // 2, tokens), lambda i: (0, 0))
    return pl.pallas_call(
        attend_back_kernel,
        grid=(KV_HEADS,),
        out_shape=(
            jax.ShapeDtypeStruct((HEADS * HD, tokens), BF16),
            jax.ShapeDtypeStruct((KV_HEADS * HD, tokens), BF16),
            jax.ShapeDtypeStruct((KV_HEADS * HD, tokens), BF16),
        ),
        in_specs=[
            pl.BlockSpec((GROUP, tokens, tokens), lambda i: (i, 0, 0)),
            heads,
            heads,
            heads,
            pl.BlockSpec((HD, tokens), lambda i: (HEADS + i, 0)),
            pl.BlockSpec((HD, tokens), lambda i: (HEADS + KV_HEADS + i, 0)),
            table,
            table,
        ],
        out_specs=(heads, one, one),
        compiler_params=pltpu.CompilerParams(vmem_limit_bytes=32 * MIB),
        cost_estimate=SHORT,
        name="attend_back",
    )(prob, mixed, grad, qkv, qkv, qkv, cosine, sine)


def finish_grads_kernel(
    where_ref, normed_t_ref, dq_ref, dk_ref, dv_ref, out_grad_ref, keep_ref, send_ref, halves_ref
):
    normed_t = normed_t_ref[...]
    queries = dq_ref.shape[0]
    values = dv_ref.shape[0]
    halves_ref[0, :, :queries] = dot(normed_t, dq_ref[...], 1, 1).astype(BF16)
    halves_ref[0, :, queries:] = dot(normed_t, dk_ref[...], 1, 1).astype(BF16)
    halves_ref[1, :, :values] = dot(normed_t, dv_ref[...], 1, 1).astype(BF16)
    halves_ref[1, :, values:] = out_grad_ref[...]
    core = where_ref[3]
    keep_ref[...] = halves_ref[core]
    send_ref[...] = halves_ref[1 - core]


def finish_grads(where, normed_t, dq, dk, dv, out_grad):
    width = normed_t.shape[0]
    half = dq.shape[0] + dk.shape[0]
    shape = jax.ShapeDtypeStruct((width, half), BF16)
    vmem = pl.BlockSpec(memory_space=pltpu.VMEM)
    return pl.pallas_call(
        finish_grads_kernel,
        out_shape=(shape, shape),
        in_specs=[pl.BlockSpec(memory_space=pltpu.SMEM)] + [vmem] * 5,
        out_specs=(vmem, vmem),
        scratch_shapes=[pltpu.VMEM((2, width, half), BF16)],
        compiler_params=pltpu.CompilerParams(vmem_limit_bytes=24 * MIB),
        cost_estimate=SHORT,
        name="finish_grads",
    )(where, normed_t, dq, dk, dv, out_grad)


def input_grad_kernel(
    dq_ref, dk_ref, dv_ref, weight_ref, tokens_ref, scale_ref, grad_ref, after_ref, sum_ref, came_ref,
    out_ref, output_ref,
):
    output_ref[...] = (after_ref[...] + sum_ref[...] + came_ref[...].astype(F32)).astype(BF16)
    queries, keys = dq_ref.shape[0], dk_ref.shape[0]
    end = queries + keys + dv_ref.shape[0]
    pull = dot(weight_ref[:, :queries], dq_ref[...], 1, 0)
    pull = pull + dot(weight_ref[:, queries : queries + keys], dk_ref[...], 1, 0)
    pull = pull + dot(weight_ref[:, queries + keys : end], dv_ref[...], 1, 0)
    values, scale = tokens_ref[...].astype(F32), scale_ref[...]
    mean = jnp.mean(pull * values, 0, keepdims=True)
    out_ref[...] = grad_ref[...] + scale * pull - values * (scale * scale * scale * mean)


def input_gradient(dq, dk, dv, weight, tokens, scale, grad, after, own, came):
    return pl.pallas_call(
        input_grad_kernel,
        out_shape=(
            jax.ShapeDtypeStruct(grad.shape, F32),
            jax.ShapeDtypeStruct(grad.shape, BF16),
        ),
        compiler_params=pltpu.CompilerParams(vmem_limit_bytes=24 * MIB),
        cost_estimate=LONG,
        name="input_gradient",
    )(dq, dk, dv, weight, tokens, scale, grad, after, own, came)


def per_device(
    shards,
    tokens,
    segment_ids,
    positions,
    norm_attn,
    w_qkv,
    w_out,
    norm_mlp,
    w_gate_up,
    w_down,
    cotangent,
):
    rep, outer, mid, core = place()
    where = jnp.stack([rep, outer, mid, core]).astype(jnp.int32)
    count = shards // 4
    width = tokens.shape[1]
    rows = w_qkv.shape[0]
    kept = w_qkv.shape[1]
    units = w_gate_up.shape[1] // 8
    gain_attn, gain_mlp = norm_attn.astype(F32)[:, None], norm_mlp.astype(F32)[:, None]

    qkv_block = (w_qkv.astype(F32) * gain_attn).astype(BF16)
    tail = -kept % LANES
    attn_block = jnp.concatenate([qkv_block, w_out[:, width - tail :], w_out[:, : width - tail]], 1)
    part = attn_block.shape[1] // 4

    big = -(-units // (2 * LANES)) * LANES
    chunks = ((0, big), (big, units - big))

    def attn_quarter(index):
        return lax.dynamic_slice(attn_block, (0, index * part), (rows, part))

    def feed_quarter(index):
        return jnp.concatenate(
            [
                lax.dynamic_slice(feed_block, (0, (kind * 4 + index) * units + start), (rows, size))
                for start, size in chunks
                for kind in range(2)
            ],
            1,
        )

    def chip_rows(mine, other):
        mine, other = order.after(mine, other)
        return order.mark(
            jnp.concatenate(
                [jnp.where(core == 0, mine, other), jnp.where(core == 0, other, mine)], 0
            )
        )

    order = Order(where)
    attn_mine = attn_quarter(core * 2 + rep)
    attn_other = hop(attn_quarter((1 - core) * 2 + rep), shards, core_move)
    attn_chip = chip_rows(attn_mine, attn_other)
    down_piece = pick(w_down.reshape(2, w_down.shape[0] // 2, width), rep)

    def outer_start(piece):
        return [piece] + [hop(piece, shards, outer_move(k, count)) for k in range(1, count)]

    def outer_stop(parts):
        return order.mark(jnp.stack(order.after(*parts)))

    def pair(held, came):
        return order.mark(jnp.stack(order.after(held, came)))

    tokens_t, cot_t = tokens.T, cotangent.T

    attn_way = outer_start(attn_chip)
    feed_block = (order.after(w_gate_up).astype(F32) * gain_mlp).astype(BF16)
    feed_mine = feed_quarter(core * 2 + rep)
    feed_other = hop(feed_quarter((1 - core) * 2 + rep), shards, core_move)
    cot_came = hop(cot_t, shards, core_move)
    half_dim = HD // 2
    freqs = ROPE_BASE ** (-2.0 * jnp.arange(half_dim, dtype=F32) / HD)
    angles = freqs[:, None] * positions[0].astype(F32)[None, :]
    cosine, sine = jnp.cos(angles), jnp.sin(angles)
    inputs = order.after(tokens_t).astype(F32)
    scale_attn = lax.rsqrt(jnp.mean(inputs * inputs, 0, keepdims=True) + EPSILON)
    normed_t = order.mark((inputs * scale_attn).astype(BF16))
    order.pause()
    cot_came = order.mark(order.after(cot_came))
    feed_chip = chip_rows(feed_mine, feed_other)
    attn_own = outer_stop(attn_way)
    attn_way = hop(attn_own, shards, second_move)
    down_way = outer_start(order.after(down_piece))
    order.pause()
    attn_own = pair(attn_own, attn_way)
    attn_way = hop(attn_own, shards, first_move)
    down_own = outer_stop(down_way)
    down_way = hop(down_own, shards, second_move)
    feed_way = outer_start(order.after(feed_chip))
    order.pause()
    attn_own = pair(attn_own, attn_way)
    attn_way = hop(attn_own, shards, core_move)
    order.pause()
    down_own = pair(down_own, down_way)
    down_way = hop(down_own, shards, first_move)
    attn_own, attn_way = order.after(attn_own, attn_way)
    attn_full = order.mark(assemble(attn_own, attn_way, where))
    qkv = order.mark(project(order.after(normed_t), attn_full, cosine, sine))
    feed_way = order.after(*feed_way)
    feed0_own = jnp.stack([piece[:, : 2 * big] for piece in feed_way])
    feed0_way = hop(order.mark(feed0_own), shards, second_move)
    feed1_own = jnp.stack(order.after(*[piece[:, 2 * big :] for piece in feed_way]))
    feed1_way = hop(order.mark(feed1_own), shards, second_move)
    prob, mixed = attend(order.after(qkv), segment_ids[0])
    order.mark(mixed)
    feed0_own = pair(feed0_own, feed0_way)
    feed0_way = hop(feed0_own, shards, first_move)
    after_attn, scale_mlp, mlp_low = branch(order.after(mixed), attn_full, tokens_t)
    order.mark(mlp_low)
    low_came = hop(mlp_low, shards, core_move)
    down_own = pair(down_own, down_way)
    down_way = hop(down_own, shards, core_move)
    feed1_own = pair(feed1_own, feed1_way)
    feed1_way = hop(feed1_own, shards, first_move)
    order.pause()

    def run_feed(chunk, pieces, down_grad, before):
        own, way, low, cot, down = order.after(*pieces, low_came, cot_came, down_way)
        return feed(
            where, chunks[chunk][0], (mlp_low, low), (cot_t, cot), (own, way), (down_own, down), down_grad, before
        )

    *before, keep0, send0, down_grad = run_feed(0, (feed0_own, feed0_way), None, ())
    order.mark(send0)
    feed0_sum = SlotReduction(keep0, send0, shards)

    sums, sums_other, back, back_other, keep1, send1, down_grad = run_feed(
        1, (feed1_own, feed1_way), down_grad, before
    )
    order.mark(send1)
    back_came = hop(back_other, shards, core_move)
    sums_came = hop(sums_other, shards, core_move)

    def down_piece_of(array, to_mid, to_rep):
        array = array.reshape(count // 2, 2, 2, 2, w_down.shape[0] // 2, width)
        return lax.dynamic_slice(
            array, (0, to_mid, 0, to_rep, 0, 0), (count // 2, 1, 2, 1) + array.shape[4:]
        )[:, 0, :, 0]

    feed1_sum = SlotReduction(keep1, send1, shards)
    down_sum = Reduction((down_grad,), down_piece_of, shards)
    feed0_sum.second(order)
    down_sum.first(order)
    order.pause()
    sums_came, back_came = order.after(sums_came, back_came)
    backs = (back, back_came)
    after_grad, mixed_grad, out_grad = return_branch(
        backs, after_attn, scale_mlp, cot_t, mixed, attn_full
    )
    order.mark(mixed_grad)
    dq, dk, dv = attend_back(prob, mixed, order.after(mixed_grad), qkv, cosine, sine)
    order.mark(dq)
    keep_attn, send_attn = finish_grads(order.tick, normed_t, order.after(dq), dk, dv, out_grad)
    order.mark(keep_attn)
    order.tick = gain_attn

    def attn_piece(array, to_mid, to_rep):
        array = array.reshape(count, 2, 2 * rows, 2 * part)
        return lax.dynamic_slice(
            array, (0, to_mid, 0, to_rep * part), (count, 1, 2 * rows, part)
        )[:, 0]

    attn_came = hop(send_attn, shards, core_move)
    feed1_sum.second(order)
    feed0_out = OuterReduction(feed0_sum.third(order), shards)
    feed0_out.send()
    down_sum.second(order)
    order.pause()
    attn_sum = Reduction((keep_attn, attn_came), attn_piece, shards)
    attn_sum.first(order)
    feed1_out = OuterReduction(feed1_sum.third(order), shards)
    feed1_out.send()
    feed0_out.receive(order)
    feed0_out.send()
    down_out = OuterReduction(down_sum.third(order), shards)
    down_out.send()
    input_grad, output = input_gradient(
        order.after(dq), dk, dv, attn_full, tokens_t, scale_attn, after_grad, after_attn, sums, sums_came
    )
    order.mark(output)
    attn_sum.second(order)
    feed1_out.receive(order)
    feed1_out.send()
    down_out.receive(order)
    down_mine = down_out.finish(order)
    down_way = give_down(down_mine, shards)
    feed0_out.receive(order)
    feed0_total = feed0_out.finish(order)
    order.pause()
    attn_out = OuterReduction(attn_sum.third(order), shards)
    attn_out.send()
    feed1_out.receive(order)
    feed1_total = feed1_out.finish(order)
    feed_total = order.mark(jnp.concatenate(order.after(feed0_total, feed1_total), -1))
    down_total = order.mark(add_low(*order.after(down_mine, down_way)))
    down_way = hop(pick(down_total, 1 - core), shards, core_move)
    feed_quarters = share_columns(order.after(feed_total), shards, rep, core)
    order.pause()
    attn_out.receive(order)
    attn_out.send()
    mine, came = order.after(pick(down_total, core), down_way)
    down_rows = order.mark(jnp.where(outer // (count // 2) == core, mine, came))
    down_way = hop(down_rows, shards, rep_move)
    feed_quarters = order.after(*feed_quarters)
    order.mark(feed_quarters[3])
    order.pause()
    attn_out.receive(order)
    down_rows = jnp.stack(order.after(down_rows, down_way))
    attn_quarters = share_columns(attn_out.finish(order), shards, rep, core)
    down_rows = jnp.concatenate([pick(down_rows, rep), pick(down_rows, 1 - rep)], 0)
    grad_down = down_rows.astype(F32)

    attn_rows = jnp.concatenate(attn_quarters, 1).astype(F32)
    feed_rows = jnp.concatenate(
        [
            q[:, 2 * start + kind * size : 2 * start + (kind + 1) * size]
            for kind in range(2)
            for q in feed_quarters
            for start, size in chunks
        ],
        1,
    ).astype(F32)
    qkv_rows = attn_rows[:, :kept]
    grad_norm_attn = jnp.sum(qkv_rows * w_qkv.astype(F32), 1)
    grad_norm_mlp = jnp.sum(feed_rows * w_gate_up.astype(F32), 1)
    grad_out = jnp.concatenate([attn_rows[:, kept + tail :], attn_rows[:, kept : kept + tail]], 1)
    return (
        output.T,
        input_grad.T,
        grad_norm_attn,
        qkv_rows * order.tick,
        grad_out,
        grad_norm_mlp,
        feed_rows * gain_mlp,
        grad_down,
    )


def solution(mesh):
    in_specs = (
        P(("rep", "shard"), None),
        P(("rep", "shard"), None),
        P(("rep", "shard"), None),
        P("shard"),
        P("shard", None),
        P("shard", None),
        P("shard"),
        P("shard", None),
        P("shard", None),
        P(("rep", "shard"), None),
    )
    out_specs = (
        P(("rep", "shard"), None),
        P(("rep", "shard"), None),
        P("shard"),
        P("shard", None),
        P("shard", None),
        P("shard"),
        P("shard", None),
        P("shard", None),
    )
    return jax.shard_map(
        functools.partial(per_device, mesh.shape["shard"]),
        mesh=mesh,
        in_specs=in_specs,
        out_specs=out_specs,
        check_vma=False,
    )
```

```python
import functools

import jax
import jax.numpy as jnp
from jax import lax
from jax.experimental import pallas as pl
from jax.experimental.pallas import tpu as pltpu
from jax.sharding import PartitionSpec as P

HEADS = 15
KV_HEADS = 5
HD = 64
GROUP = HEADS // KV_HEADS

EPSILON = 1e-05
ROPE_BASE = 100000.0
NEG_FILL = -1e30

AXES = ("rep", "shard")
F32 = jnp.float32
BF16 = jnp.bfloat16
LANES = 128
MIB = 1024 * 1024


def hop(values, shards, move):
    pairs = []
    for rep in range(2):
        for outer in range(shards // 4):
            for mid in range(2):
                for core in range(2):
                    to = move(rep, outer, mid, core)
                    pairs.append(
                        (
                            rep * shards + outer * 4 + mid * 2 + core,
                            to[0] * shards + to[1] * 4 + to[2] * 2 + to[3],
                        )
                    )
    return lax.ppermute(values, AXES, pairs)


def core_move(rep, outer, mid, core):
    return (rep, outer, mid, 1 - core)


def rep_move(rep, outer, mid, core):
    return (1 - rep, outer, mid, core)


def cross_move(rep, outer, mid, core):
    return (1 - rep, outer, mid, 1 - core)


def first_move(rep, outer, mid, core):
    return (rep, outer, 1 - mid, core) if core == 0 else (1 - rep, outer, mid, core)


def second_move(rep, outer, mid, core):
    return (1 - rep, outer, mid, core) if core == 0 else (rep, outer, 1 - mid, core)


def outer_move(step, count):
    return lambda rep, outer, mid, core: (rep, (outer + step) % count, mid, core)


class Order:
    def __init__(self, tick):
        self.done = None
        self.tick = tick

    def after(self, *values):
        if self.done is not None:
            values = lax.optimization_barrier(tuple(values) + (self.done,))[:-1]
        return values if len(values) > 1 else values[0]

    def mark(self, value):
        self.done = value
        return value

    def pause(self):
        self.tick = self.mark(anchor(self.after(self.tick)))


def pick(array, index):
    return lax.dynamic_index_in_dim(array, index, 0, keepdims=False)


def place():
    shard = lax.axis_index("shard")
    return lax.axis_index("rep"), shard // 4, (shard // 2) % 2, shard % 2


def arrival(half, first, second, step, rep, outer, mid, count):
    to_mid = jnp.where(half == 0, mid ^ second, mid ^ first)
    to_rep = jnp.where(half == 0, rep ^ first, rep ^ second)
    return to_mid, to_rep, lax.rem(outer + count - step, count)


def in_order(held, half):
    rep, outer, mid, _ = place()
    count = held.shape[2]
    flat = held.reshape((4,) + held.shape[2:])
    reps = []
    for want_rep in range(2):
        mids = []
        for want_mid in range(2):
            by_rep, by_mid = rep ^ want_rep, mid ^ want_mid
            second = jnp.where(half == 0, by_mid, by_rep)
            first = jnp.where(half == 0, by_rep, by_mid)
            piece = pick(flat, second * 2 + first)
            mids.append(
                jnp.concatenate([pick(piece, (outer - k) % count)[None] for k in range(count)], 0)
            )
        reps.append(jnp.stack(mids, 1))
    return jnp.stack(reps)


def assemble_kernel(where_ref, own_ref, came_ref, out_ref, sem):
    rep, outer, mid, core = (where_ref[k] for k in range(4))
    count, _, width = own_ref.shape[2:]
    for source, half in ((own_ref, core), (came_ref, 1 - core)):
        for second in range(2):
            for first in range(2):
                for step in range(count):
                    to_mid, to_rep, to_outer = arrival(
                        half, first, second, step, rep, outer, mid, count
                    )
                    column = pl.multiple_of((half * 2 + to_rep) * width, LANES)
                    pltpu.make_async_copy(
                        source.at[second, first, step],
                        out_ref.at[to_outer * 2 + to_mid, :, pl.ds(column, width)],
                        sem,
                    ).start()
    pltpu.make_async_copy(out_ref, out_ref, sem).wait()


def assemble(own, came, where):
    count, rows, width = own.shape[2:]
    core = where[3]
    shape = (2 * count * rows, 4 * width)
    if rows % 8 or width % LANES:
        halves = jnp.stack([in_order(own, core), in_order(came, 1 - core)])
        halves = jnp.stack([pick(halves, core), pick(halves, 1 - core)])
        return halves.transpose(2, 3, 4, 0, 1, 5).reshape(shape)
    out = pl.pallas_call(
        assemble_kernel,
        out_shape=jax.ShapeDtypeStruct((2 * count, rows, 4 * width), own.dtype),
        in_specs=[
            pl.BlockSpec(memory_space=pltpu.SMEM),
            pl.BlockSpec(memory_space=pl.ANY),
            pl.BlockSpec(memory_space=pl.ANY),
        ],
        out_specs=pl.BlockSpec(memory_space=pltpu.VMEM),
        scratch_shapes=[pltpu.SemaphoreType.DMA],
        compiler_params=pltpu.CompilerParams(vmem_limit_bytes=16 * MIB),
        cost_estimate=LONG,
        name="assemble",
    )(where, own, came)
    return out.reshape(shape)


def add_low(*terms):
    total = terms[0].astype(F32)
    for term in terms[1:]:
        total = total + term.astype(F32)
    return total.astype(BF16)


class Reduction:
    def __init__(self, terms, piece, shards):
        self.terms, self.piece, self.shards = terms, piece, shards

    def parts(self, where):
        return [self.piece(term, *where) for term in self.terms]

    def first(self, order, *way):
        rep, _, mid, core = place()
        got = order.after(*self.terms, *way)
        self.terms = got if isinstance(got, tuple) else (got,)
        away = [(1 - mid, 0), (1 - mid, 1)], [(0, 1 - rep), (1, 1 - rep)]
        sums = []
        for k in range(2):
            where = tuple(jnp.where(core == 0, away[0][k][d], away[1][k][d]) for d in range(2))
            sums.append(add_low(*self.parts(where)))
        self.way = hop(order.mark(jnp.stack(sums)), self.shards, first_move)

    def second(self, order):
        rep, _, mid, core = place()
        self.got = order.after(self.way)
        self.last = jnp.where(core == 0, rep, mid)
        k = 1 - self.last
        where = jnp.where(core == 0, mid, k), jnp.where(core == 0, k, rep)
        out = order.mark(add_low(*self.parts(where), pick(self.got, k)))
        self.way = hop(out, self.shards, second_move)

    def third(self, order):
        rep, _, mid, _ = place()
        came = order.after(self.way)
        return order.mark(add_low(*self.parts((mid, rep)), pick(self.got, self.last), came))


class SlotReduction:
    def __init__(self, keep, send, shards):
        rep, _, mid, core = place()
        self.last = jnp.where(core == 0, rep, mid)
        self.keep, self.shards = keep, shards
        self.way = hop(send, shards, first_move)

    def second(self, order):
        self.got = order.after(self.way)
        k = 1 - self.last
        out = order.mark(add_low(pick(self.keep, k), pick(self.got, k)))
        self.way = hop(out, self.shards, second_move)

    def third(self, order):
        came = order.after(self.way)
        return order.mark(add_low(pick(self.keep, self.last), pick(self.got, self.last), came))


class OuterReduction:
    def __init__(self, mine, shards):
        self.mine, self.shards, self.bit = mine, shards, 1

    def send(self):
        outer = place()[1]
        count = self.mine.shape[0]
        pairs = self.mine.reshape((count // 2, 2) + self.mine.shape[1:])
        side = (outer // self.bit) % 2
        split = lambda which: lax.dynamic_index_in_dim(pairs, which, 1, keepdims=False)
        self.keep = split(side)
        move = lambda rep, outer, mid, core: (rep, outer ^ self.bit, mid, core)
        self.way = hop(split(1 - side), self.shards, move)

    def receive(self, order):
        keep, way = order.after(self.keep, self.way)
        self.mine = order.mark(add_low(keep, way))
        self.bit *= 2

    def finish(self, order):
        while self.mine.shape[0] > 1:
            self.send()
            self.receive(order)
        return pick(self.mine, 0)


def give_down(mine, shards):
    count = shards // 4
    half = count // 2
    pairs = []
    for r in range(2):
        for o in range(count):
            for m in range(2):
                for c in range(2):
                    if o // half != c:
                        base = r * shards + m * 2 + c
                        pairs.append((base + o * 4, base + (o ^ half) * 4))
    return lax.ppermute(mine, AXES, pairs)


def share_columns(total, shards, rep, core):
    rows = total.shape[0] // 2
    halves = total.reshape(2, rows, total.shape[1])
    mine, other = pick(halves, core), pick(halves, 1 - core)
    stack = jnp.stack(
        [
            mine,
            hop(mine, shards, rep_move),
            hop(other, shards, core_move),
            hop(other, shards, cross_move),
        ]
    )
    return [pick(stack, q ^ (core * 2 + rep)) for q in range(4)]


LONG = pl.CostEstimate(flops=200 * 10**9, bytes_accessed=0, transcendentals=0)
SHORT = pl.CostEstimate(flops=10**6, bytes_accessed=0, transcendentals=0)


def dot(left, right, left_dim, right_dim):
    return lax.dot_general(
        left, right, (((left_dim,), (right_dim,)), ((), ())), preferred_element_type=F32
    )


def anchor_kernel(in_ref, out_ref):
    if len(in_ref.shape) == 1:
        for k in range(4):
            out_ref[k] = in_ref[k]
    else:
        out_ref[...] = in_ref[...]


def anchor(tick):
    space = pl.BlockSpec(memory_space=pltpu.SMEM if tick.ndim == 1 else pltpu.VMEM)
    return pl.pallas_call(
        anchor_kernel,
        out_shape=jax.ShapeDtypeStruct(tick.shape, tick.dtype),
        in_specs=[space],
        out_specs=space,
        cost_estimate=LONG,
        name="anchor",
    )(tick)


def join_kernel(count, *refs):
    for k, ref in enumerate(refs[:count]):
        start = 0
        for out_ref in refs[count:]:
            size = out_ref.shape[-1]
            out_ref[k] = ref[..., start : start + size]
            start += size


def join(arrays, sizes=None):
    shape, count = arrays[0].shape, len(arrays)
    outs = [
        jax.ShapeDtypeStruct((count,) + shape[:-1] + (size,), arrays[0].dtype)
        for size in sizes or (shape[-1],)
    ]
    out = pl.pallas_call(
        functools.partial(join_kernel, count),
        out_shape=outs,
        compiler_params=pltpu.CompilerParams(vmem_limit_bytes=16 * MIB),
        cost_estimate=SHORT,
        name="join",
    )(*arrays)
    return out if sizes else out[0]


def project_kernel(normed_ref, weight_ref, cos_ref, sin_ref, out_ref):
    half = HD // 2
    turned = (HEADS + KV_HEADS) * HD
    cosine, sine = cos_ref[...], sin_ref[...]
    normed = normed_ref[...]
    for start in range(0, turned, 2 * LANES):
        raw = dot(weight_ref[:, start : start + 2 * LANES], normed, 0, 0)
        for at in range(0, 2 * LANES, HD):
            row = start + at
            scale = 0.125 if row < HEADS * HD else 1.0
            upper, lower = raw[at : at + half], raw[at + half : at + HD]
            out_ref[row : row + half] = ((upper * cosine - lower * sine) * scale).astype(BF16)
            out_ref[row + half : row + HD] = ((lower * cosine + upper * sine) * scale).astype(BF16)
    out_ref[turned:] = dot(
        weight_ref[:, turned : turned + KV_HEADS * HD], normed, 0, 0
    ).astype(BF16)


def project(normed_t, weight, cosine, sine):
    return pl.pallas_call(
        project_kernel,
        out_shape=jax.ShapeDtypeStruct(((HEADS + 2 * KV_HEADS) * HD, normed_t.shape[1]), BF16),
        compiler_params=pltpu.CompilerParams(vmem_limit_bytes=24 * MIB),
        cost_estimate=SHORT,
        name="project",
    )(normed_t, weight, cosine, sine)


def split_tokens(tokens):
    block = 256 if tokens % 256 == 0 else tokens
    return [(start, start + block) for start in range(0, tokens, block)]


def attend_kernel(seg_row_ref, seg_col_ref, q_ref, k_ref, v_ref, prob_ref, mixed_ref, bias_ref):
    tokens = q_ref.shape[1]

    @pl.when(pl.program_id(0) == 0)
    def _():
        keys = lax.broadcasted_iota(jnp.int32, (tokens, tokens), 0)
        queries = lax.broadcasted_iota(jnp.int32, (tokens, tokens), 1)
        allowed = (seg_col_ref[...] == seg_row_ref[...]) & (keys <= queries)
        bias_ref[...] = jnp.where(allowed, 0.0, NEG_FILL)

    for head in range(GROUP):
        rows = slice(head * HD, (head + 1) * HD)
        for start, stop in split_tokens(tokens):
            scores = dot(k_ref[:, :stop], q_ref[rows, start:stop], 0, 0)
            scores = scores + bias_ref[:stop, start:stop]
            expo = jnp.exp(scores - jnp.max(scores, 0, keepdims=True))
            prob = (expo * (1.0 / jnp.sum(expo, 0, keepdims=True))).astype(BF16)
            prob_ref[head, :stop, start:stop] = prob
            mixed_ref[rows, start:stop] = dot(v_ref[:, :stop], prob, 1, 0).astype(BF16)


def attend(qkv, seg_row):
    tokens = qkv.shape[1]
    return pl.pallas_call(
        attend_kernel,
        grid=(KV_HEADS,),
        out_shape=(
            jax.ShapeDtypeStruct((HEADS, tokens, tokens), BF16),
            jax.ShapeDtypeStruct((HEADS * HD, tokens), BF16),
        ),
        in_specs=[
            pl.BlockSpec((1, tokens), lambda i: (0, 0)),
            pl.BlockSpec((tokens, 1), lambda i: (0, 0)),
            pl.BlockSpec((GROUP * HD, tokens), lambda i: (i, 0)),
            pl.BlockSpec((HD, tokens), lambda i: (HEADS + i, 0)),
            pl.BlockSpec((HD, tokens), lambda i: (HEADS + KV_HEADS + i, 0)),
        ],
        out_specs=(
            pl.BlockSpec((GROUP, tokens, tokens), lambda i: (i, 0, 0)),
            pl.BlockSpec((GROUP * HD, tokens), lambda i: (i, 0)),
        ),
        scratch_shapes=[pltpu.VMEM((tokens, tokens), F32)],
        compiler_params=pltpu.CompilerParams(vmem_limit_bytes=32 * MIB),
        cost_estimate=LONG,
        name="attend",
    )(seg_row.reshape(1, tokens), seg_row.reshape(tokens, 1), qkv, qkv, qkv)


def out_columns(width):
    kept = (HEADS + 2 * KV_HEADS) * HD
    tail = -kept % LANES
    return kept + tail - LANES, LANES - tail, kept + tail


def branch_kernel(mixed_ref, weight_ref, tokens_ref, after_ref, scale_ref, normed_ref):
    mixed = mixed_ref[...]
    tile, skip, rest = out_columns(weight_ref.shape[1])
    wide = weight_ref.shape[1] - rest
    last = dot(weight_ref[:, tile : tile + LANES], mixed, 0, 0)
    after_ref[:wide] = tokens_ref[:wide].astype(F32) + dot(weight_ref[:, rest:], mixed, 0, 0)
    after_ref[wide:] = tokens_ref[wide:].astype(F32) + last[skip:]
    after = after_ref[...]
    scale = lax.rsqrt(jnp.mean(after * after, 0, keepdims=True) + EPSILON)
    scale_ref[...] = scale
    normed_ref[...] = (after * scale).astype(BF16)


def branch(mixed, weight, tokens):
    width, count = tokens.shape
    return pl.pallas_call(
        branch_kernel,
        out_shape=(
            jax.ShapeDtypeStruct((width, count), F32),
            jax.ShapeDtypeStruct((1, count), F32),
            jax.ShapeDtypeStruct((width, count), BF16),
        ),
        compiler_params=pltpu.CompilerParams(vmem_limit_bytes=24 * MIB),
        cost_estimate=SHORT,
        name="branch",
    )(mixed, weight, tokens)


def feed_kernel(
    ordered,
    offset,
    where_ref,
    normed_refs,
    cot_refs,
    pieces_refs,
    down_refs,
    down_grad_in_ref,
    before_refs,
    sum_refs,
    back_refs,
    grad_refs,
    down_grad_ref,
    normed,
    cot,
    weight,
    down_all,
    down,
    inner,
    pull,
    grad,
    down_grad,
    results,
    results_low,
    sems,
    out_sems,
):
    rep, outer, mid, core = (where_ref[k] for k in range(4))
    tokens = normed_refs[0].shape[1]
    units = down.shape[0]
    size = units // 2
    quarter = down_all.shape[0] // 2

    def load(index, copies):
        for source, to in copies:
            pltpu.make_async_copy(source, to, sems.at[index]).start()

    def ready(index, ref):
        pltpu.make_async_copy(ref, ref, sems.at[index]).wait()

    load(0, [(normed_refs[k], normed.at[:, pl.ds(k * tokens, tokens)]) for k in range(2)])
    for kind in range(2):
        if ordered:
            load(
                1 + kind,
                [
                    (
                        pieces_refs[0].at[k, :, pl.ds(kind * size, size)],
                        weight.at[0, :, pl.ds(kind * units + k * size, size)],
                    )
                    for k in range(2)
                ],
            )
            continue
        for second, source in enumerate(pieces_refs):
            for first in range(2):
                steps = source.shape[1]
                for step in range(steps):
                    to_mid, to_rep, to_outer = arrival(
                        core, first, second, step, rep, outer, mid, steps
                    )
                    column = pl.multiple_of(kind * units + to_rep * size, LANES)
                    load(
                        1 + kind,
                        [
                            (
                                source.at[first, step, :, pl.ds(kind * size, size)],
                                weight.at[to_outer * 2 + to_mid, :, pl.ds(column, size)],
                            )
                        ],
                    )
    load(3, [(cot_refs[k], cot.at[:, pl.ds(k * tokens, tokens)]) for k in range(2)])
    if ordered:
        load(4, [(down_refs[0], down_all)])
    else:
        steps, block = down_refs[0].shape[2:4]
        half = steps // 2
        for source, owner in ((down_refs[0], core), (down_refs[1], 1 - core)):
            for at in range(half):
                step = lax.rem(outer + steps - (core * half + at), steps)
                for second in range(2):
                    for first in range(2):
                        to_mid, to_rep, _ = arrival(owner, first, second, 0, rep, outer, mid, steps)
                        row = (((at * 2 + to_mid) * 2 + owner) * 2 + to_rep) * block
                        to = down_all.at[pl.ds(pl.multiple_of(row, 16), block)]
                        load(4, [(source.at[second, first, step], to)])

    if before_refs:
        load(5, [(before_refs[2 - 2 * k], results.at[k]) for k in range(2)])
        load(6, [(before_refs[3 - 2 * k], results_low.at[k]) for k in range(2)])

    ready(0, normed)
    ready(1, weight.at[:, :, pl.ds(0, units)])
    tile = 2 * LANES if units % (2 * LANES) == 0 else LANES

    def columns(start, count=tile):
        return weight[:, :, pl.ds(start, count)].reshape(normed.shape[0], count)

    for start in range(0, units, tile):
        at = pl.ds(start, tile)
        gate = dot(columns(start), normed[...], 0, 0)
        if start == 0:
            ready(2, weight.at[:, :, pl.ds(units, units)])
        up = dot(columns(units + start), normed[...], 0, 0)
        if start == 0:
            ready(3, cot)
            ready(4, down_all)
            down[:size] = down_all[offset : offset + size]
            down[size:] = down_all[quarter + offset : quarter + offset + size]
        inner_grad = dot(down[at], cot[...], 1, 0)
        sigma = 1.0 / (1.0 + jnp.exp(-gate))
        activ = gate * sigma
        inner[at] = (activ * up).astype(BF16)
        pull[at] = (inner_grad * up * (sigma + activ * (1.0 - sigma))).astype(BF16)
        pull[pl.ds(units + start, tile)] = (inner_grad * activ).astype(BF16)
        down_grad[at] = dot(inner[at], cot[...], 1, 1).astype(BF16)
    for k in range(2):
        pltpu.make_async_copy(
            down_grad.at[pl.ds(k * size, size)],
            down_grad_ref.at[k, pl.ds(offset, size)],
            out_sems.at[0],
        ).start()
    for kind in range(2):
        for start in range(0, units, tile):
            at = pl.ds(kind * units + start, tile)
            part = dot(normed[...], pull[at], 1, 1)
            if ordered:
                grad[0, :, at] = part.astype(BF16)
            else:
                grad[:, :, at] = part.reshape(*grad.shape[:2], tile).astype(BF16)
        for to_rep in range(2):
            source_at = pl.ds(kind * units + to_rep * size, size)
            target_at = pl.ds(kind * size, size)
            if ordered:
                pltpu.make_async_copy(
                    grad.at[0, :, source_at], grad_refs[0].at[to_rep, :, target_at], out_sems.at[1]
                ).start()
                continue
            for at in range(grad.shape[0]):
                to_outer, to_mid = at // 2, at % 2
                for which in range(2):
                    slot, mine = (to_mid, rep == to_rep) if which else (to_rep, mid == to_mid)
                    for ref, wanted in zip(grad_refs, (mine, jnp.logical_not(mine))):

                        @pl.when(jnp.logical_and(core == which, wanted))
                        def _():
                            pltpu.make_async_copy(
                                grad.at[at, :, source_at],
                                ref.at[slot, to_outer, :, target_at],
                                out_sems.at[1],
                            ).start()
    for index, (out_refs, left, right, dim) in enumerate(
        ((back_refs, columns(0, 2 * units), pull, 1), (sum_refs, down[...], inner, 0))
    ):
        if before_refs and index == 0:
            ready(5, results)
            ready(6, results_low)
        low = dot(left, right[:, pl.ds(tokens, tokens)], dim, 0)
        if before_refs:
            low = low + results_low[index].astype(F32)
        results_low[index] = low.astype(BF16)
        pltpu.make_async_copy(results_low.at[index], out_refs[1], out_sems.at[2 + index]).start()
        total = dot(left, right[:, pl.ds(0, tokens)], dim, 0)
        results[index] = total + results[index] if before_refs else total
        pltpu.make_async_copy(results.at[index], out_refs[0], out_sems.at[4 + index]).start()
    pltpu.make_async_copy(down_grad, down_grad, out_sems.at[0]).wait()
    pltpu.make_async_copy(grad, grad, out_sems.at[1]).wait()
    for index in range(2):
        pltpu.make_async_copy(
            results_low.at[index], results_low.at[index], out_sems.at[2 + index]
        ).wait()
        pltpu.make_async_copy(results.at[index], results.at[index], out_sems.at[4 + index]).wait()


def feed(where, offset, normed, cot, pieces, down, down_grad, before):
    width, tokens = normed[0].shape
    size = pieces[0].shape[-1] // 2
    units = 2 * size
    count, block = down[0].shape[2:4]
    half_units = count * 4 * block
    rows = pieces[0].shape[2]
    ordered = rows % 8 != 0 or block % 16 != 0
    if ordered:
        core = where[3]
        pieces = (in_order(jnp.stack(pieces), core).reshape(2, width, units),)
        blocks = [in_order(array, half) for array, half in zip(down, (core, 1 - core))]
        blocks = jnp.stack([jnp.where(core == k, *blocks) for k in range(2)])
        blocks = blocks.transpose(2, 3, 0, 1, 4, 5).reshape(2, half_units, width)
        down = (pick(blocks, core),)
        rows = width
    first_call = down_grad is None
    operands = [*normed, *cot, *pieces, *down] + ([] if first_call else [down_grad, *before])
    split_before = len(before)
    split = len(down)

    def body(where_ref, *refs):
        refs = list(refs)
        take = lambda count: [refs.pop(0) for _ in range(count)]
        ins = take(2), take(2), take(len(pieces)), take(split)
        down_grad_in = None if first_call else take(1)[0]
        feed_kernel(
            ordered, offset, where_ref, *ins, down_grad_in, take(split_before), take(2), take(2), take(len(grads)), *refs
        )

    wide = jax.ShapeDtypeStruct((width, tokens), F32)
    low = jax.ShapeDtypeStruct((width, tokens), BF16)
    if ordered:
        grads = [jax.ShapeDtypeStruct((2, width, units), BF16)]
    else:
        grads = [jax.ShapeDtypeStruct((2, count, rows, units), BF16)] * 2
    out_shape = (
        wide,
        low,
        wide,
        low,
        *grads,
        jax.ShapeDtypeStruct((2, half_units // 2, width), BF16),
    )
    any_space = pl.BlockSpec(memory_space=pl.ANY)
    *sums, down_grad = pl.pallas_call(
        body,
        in_specs=[pl.BlockSpec(memory_space=pltpu.SMEM)] + [any_space] * len(operands),
        out_specs=(any_space,) * len(out_shape),
        out_shape=out_shape,
        scratch_shapes=[
            pltpu.VMEM((width, 2 * tokens), BF16),
            pltpu.VMEM((width, 2 * tokens), BF16),
            pltpu.VMEM((width // rows, rows, 2 * units), BF16),
            pltpu.VMEM((half_units, width), BF16),
            pltpu.VMEM((units, width), BF16),
            pltpu.VMEM((units, 2 * tokens), BF16),
            pltpu.VMEM((2 * units, 2 * tokens), BF16),
            pltpu.VMEM((width // rows, rows, 2 * units), BF16),
            pltpu.VMEM((units, width), BF16),
            pltpu.VMEM((2, width, tokens), F32),
            pltpu.VMEM((2, width, tokens), BF16),
            pltpu.SemaphoreType.DMA((7,)),
            pltpu.SemaphoreType.DMA((6,)),
        ],
        input_output_aliases={} if first_call else {len(operands) - split_before: 4 + len(grads)},
        compiler_params=pltpu.CompilerParams(vmem_limit_bytes=52 * MIB),
        cost_estimate=LONG,
        name="feed",
    )(where, *operands)
    if ordered:
        sums = (*sums[:4], *slots(sums[4], where, count))
    return (*sums, down_grad)


def slots(grad, where, count):
    rep, _, mid, core = (where[k] for k in range(4))
    blocks = grad.reshape(2, count, 2, -1, grad.shape[-1])

    def piece(to_mid, to_rep):
        return lax.dynamic_slice(
            blocks, (to_rep, 0, to_mid, 0, 0), (1, count, 1) + blocks.shape[3:]
        )[0, :, 0]

    keep = [piece(jnp.where(core == 0, mid, k), jnp.where(core == 0, k, rep)) for k in range(2)]
    send = [
        piece(jnp.where(core == 0, 1 - mid, k), jnp.where(core == 0, k, 1 - rep)) for k in range(2)
    ]
    return jnp.stack(keep), jnp.stack(send)


def return_kernel(
    back_refs, after_ref, scale_ref, cot_ref, mixed_ref, weight_ref, grad_ref, mixed_grad_ref, out_grad_ref
):
    back = back_refs[0][...]
    for ref in back_refs[1:]:
        back = back + ref[...].astype(F32)
    after, scale = after_ref[...], scale_ref[...]
    mean = jnp.mean(back * after, 0, keepdims=True)
    grad = cot_ref[...].astype(F32) + scale * back - after * (scale * scale * scale * mean)
    grad_ref[...] = grad
    low = grad.astype(BF16)
    tile, skip, rest = out_columns(weight_ref.shape[1])
    wide = weight_ref.shape[1] - rest
    last = low[wide:]
    mixed_grad_ref[...] = (
        dot(weight_ref[:, rest:], low[:wide], 1, 0)
        + dot(weight_ref[:, tile + skip : rest], last, 1, 0)
    ).astype(BF16)
    mixed = mixed_ref[...]
    out_grad_ref[:, : LANES - skip] = dot(mixed, last, 1, 1).astype(BF16)
    out_grad_ref[:, LANES - skip :] = dot(mixed, low[:wide], 1, 1).astype(BF16)


def return_branch(backs, after, scale, cot, mixed, weight):
    width, count = after.shape

    def body(*refs):
        return_kernel(refs[: len(backs)], *refs[len(backs) :])

    return pl.pallas_call(
        body,
        out_shape=(
            jax.ShapeDtypeStruct((width, count), F32),
            jax.ShapeDtypeStruct((width, count), BF16),
            jax.ShapeDtypeStruct((width, width), BF16),
        ),
        compiler_params=pltpu.CompilerParams(vmem_limit_bytes=32 * MIB),
        cost_estimate=SHORT,
        name="return_branch",
    )(*backs, after, scale, cot, mixed, weight)


def attend_back_kernel(
    prob_ref, mixed_ref, grad_ref, q_ref, k_ref, v_ref, cos_ref, sin_ref, dq_ref, dk_ref, dv_ref
):
    half = HD // 2
    tokens = q_ref.shape[1]
    cosine, sine = cos_ref[...], sin_ref[...]
    key_grad = [None] * len(split_tokens(tokens))
    value_grad = [None] * len(split_tokens(tokens))

    def unturn(to_ref, row, grads, columns):
        upper, lower = grads[:half], grads[half:]
        c, s = cosine[:, columns], sine[:, columns]
        to_ref[row : row + half, columns] = (upper * c + lower * s).astype(BF16)
        to_ref[row + half : row + HD, columns] = (lower * c - upper * s).astype(BF16)

    for head in range(GROUP):
        rows = slice(head * HD, (head + 1) * HD)
        for block, (start, stop) in enumerate(split_tokens(tokens)):
            grad = grad_ref[rows, start:stop]
            mixed = mixed_ref[rows, start:stop]
            row_dot = jnp.sum(grad.astype(F32) * mixed.astype(F32), 0, keepdims=True)
            prob = prob_ref[head, :stop, start:stop]
            prob_grad = dot(v_ref[:, :stop], grad, 0, 0)
            score_grad = (prob.astype(F32) * (prob_grad - row_dot)).astype(BF16)
            unturn(
                dq_ref,
                head * HD,
                dot(k_ref[:, :stop], score_grad, 1, 0) * 0.125,
                slice(start, stop),
            )
            dk = dot(q_ref[rows, start:stop], score_grad, 1, 1)
            dv = dot(grad, prob, 1, 1)
            for part in range(block + 1):
                a, b = split_tokens(tokens)[part]
                if key_grad[part] is None:
                    key_grad[part], value_grad[part] = dk[:, a:b], dv[:, a:b]
                else:
                    key_grad[part] = key_grad[part] + dk[:, a:b]
                    value_grad[part] = value_grad[part] + dv[:, a:b]
    for part, (a, b) in enumerate(split_tokens(tokens)):
        unturn(dk_ref, 0, key_grad[part], slice(a, b))
        dv_ref[:, a:b] = value_grad[part].astype(BF16)


def attend_back(prob, mixed, grad, qkv, cosine, sine):
    tokens = qkv.shape[1]
    heads = pl.BlockSpec((GROUP * HD, tokens), lambda i: (i, 0))
    one = pl.BlockSpec((HD, tokens), lambda i: (i, 0))
    table = pl.BlockSpec((HD // 2, tokens), lambda i: (0, 0))
    return pl.pallas_call(
        attend_back_kernel,
        grid=(KV_HEADS,),
        out_shape=(
            jax.ShapeDtypeStruct((HEADS * HD, tokens), BF16),
            jax.ShapeDtypeStruct((KV_HEADS * HD, tokens), BF16),
            jax.ShapeDtypeStruct((KV_HEADS * HD, tokens), BF16),
        ),
        in_specs=[
            pl.BlockSpec((GROUP, tokens, tokens), lambda i: (i, 0, 0)),
            heads,
            heads,
            heads,
            pl.BlockSpec((HD, tokens), lambda i: (HEADS + i, 0)),
            pl.BlockSpec((HD, tokens), lambda i: (HEADS + KV_HEADS + i, 0)),
            table,
            table,
        ],
        out_specs=(heads, one, one),
        compiler_params=pltpu.CompilerParams(vmem_limit_bytes=32 * MIB),
        cost_estimate=SHORT,
        name="attend_back",
    )(prob, mixed, grad, qkv, qkv, qkv, cosine, sine)


def finish_grads_kernel(
    where_ref, normed_t_ref, dq_ref, dk_ref, dv_ref, out_grad_ref, keep_ref, send_ref, halves_ref
):
    normed_t = normed_t_ref[...]
    queries = dq_ref.shape[0]
    values = dv_ref.shape[0]
    halves_ref[0, :, :queries] = dot(normed_t, dq_ref[...], 1, 1).astype(BF16)
    halves_ref[0, :, queries:] = dot(normed_t, dk_ref[...], 1, 1).astype(BF16)
    halves_ref[1, :, :values] = dot(normed_t, dv_ref[...], 1, 1).astype(BF16)
    halves_ref[1, :, values:] = out_grad_ref[...]
    core = where_ref[3]
    keep_ref[...] = halves_ref[core]
    send_ref[...] = halves_ref[1 - core]


def finish_grads(where, normed_t, dq, dk, dv, out_grad):
    width = normed_t.shape[0]
    half = dq.shape[0] + dk.shape[0]
    shape = jax.ShapeDtypeStruct((width, half), BF16)
    vmem = pl.BlockSpec(memory_space=pltpu.VMEM)
    return pl.pallas_call(
        finish_grads_kernel,
        out_shape=(shape, shape),
        in_specs=[pl.BlockSpec(memory_space=pltpu.SMEM)] + [vmem] * 5,
        out_specs=(vmem, vmem),
        scratch_shapes=[pltpu.VMEM((2, width, half), BF16)],
        compiler_params=pltpu.CompilerParams(vmem_limit_bytes=24 * MIB),
        cost_estimate=SHORT,
        name="finish_grads",
    )(where, normed_t, dq, dk, dv, out_grad)


def input_grad_kernel(
    dq_ref, dk_ref, dv_ref, weight_ref, tokens_ref, scale_ref, grad_ref, after_ref, sum_ref, came_ref,
    out_ref, output_ref,
):
    output_ref[...] = (after_ref[...] + sum_ref[...] + came_ref[...].astype(F32)).astype(BF16)
    queries, keys = dq_ref.shape[0], dk_ref.shape[0]
    end = queries + keys + dv_ref.shape[0]
    pull = dot(weight_ref[:, :queries], dq_ref[...], 1, 0)
    pull = pull + dot(weight_ref[:, queries : queries + keys], dk_ref[...], 1, 0)
    pull = pull + dot(weight_ref[:, queries + keys : end], dv_ref[...], 1, 0)
    values, scale = tokens_ref[...].astype(F32), scale_ref[...]
    mean = jnp.mean(pull * values, 0, keepdims=True)
    out_ref[...] = grad_ref[...] + scale * pull - values * (scale * scale * scale * mean)


def input_gradient(dq, dk, dv, weight, tokens, scale, grad, after, own, came):
    return pl.pallas_call(
        input_grad_kernel,
        out_shape=(
            jax.ShapeDtypeStruct(grad.shape, F32),
            jax.ShapeDtypeStruct(grad.shape, BF16),
        ),
        compiler_params=pltpu.CompilerParams(vmem_limit_bytes=24 * MIB),
        cost_estimate=LONG,
        name="input_gradient",
    )(dq, dk, dv, weight, tokens, scale, grad, after, own, came)


def per_device(
    shards,
    tokens,
    segment_ids,
    positions,
    norm_attn,
    w_qkv,
    w_out,
    norm_mlp,
    w_gate_up,
    w_down,
    cotangent,
):
    rep, outer, mid, core = place()
    where = jnp.stack([rep, outer, mid, core]).astype(jnp.int32)
    count = shards // 4
    width = tokens.shape[1]
    rows = w_qkv.shape[0]
    kept = w_qkv.shape[1]
    units = w_gate_up.shape[1] // 8
    gain_attn, gain_mlp = norm_attn.astype(F32)[:, None], norm_mlp.astype(F32)[:, None]

    qkv_block = (w_qkv.astype(F32) * gain_attn).astype(BF16)
    tail = -kept % LANES
    attn_block = jnp.concatenate([qkv_block, w_out[:, width - tail :], w_out[:, : width - tail]], 1)
    part = attn_block.shape[1] // 4

    big = -(-units // (2 * LANES)) * LANES
    chunks = ((0, big), (big, units - big))

    def attn_quarter(index):
        return lax.dynamic_slice(attn_block, (0, index * part), (rows, part))

    def feed_quarter(index):
        return jnp.concatenate(
            [
                lax.dynamic_slice(feed_block, (0, (kind * 4 + index) * units + start), (rows, size))
                for start, size in chunks
                for kind in range(2)
            ],
            1,
        )

    def chip_rows(mine, other):
        mine, other = order.after(mine, other)
        return order.mark(
            jnp.concatenate(
                [jnp.where(core == 0, mine, other), jnp.where(core == 0, other, mine)], 0
            )
        )

    order = Order(where)
    attn_mine = attn_quarter(core * 2 + rep)
    attn_other = hop(attn_quarter((1 - core) * 2 + rep), shards, core_move)
    attn_chip = chip_rows(attn_mine, attn_other)
    down_piece = pick(w_down.reshape(2, w_down.shape[0] // 2, width), rep)

    def outer_start(piece):
        return [piece] + [hop(piece, shards, outer_move(k, count)) for k in range(1, count)]

    def outer_stop(parts):
        return order.mark(join(order.after(*parts)))

    def pair(held, came):
        return order.mark(join(order.after(held, came)))

    tokens_t, cot_t = tokens.T, cotangent.T

    attn_way = outer_start(attn_chip)
    feed_block = (order.after(w_gate_up).astype(F32) * gain_mlp).astype(BF16)
    feed_mine = feed_quarter(core * 2 + rep)
    feed_other = hop(feed_quarter((1 - core) * 2 + rep), shards, core_move)
    cot_came = hop(cot_t, shards, core_move)
    half_dim = HD // 2
    freqs = ROPE_BASE ** (-2.0 * jnp.arange(half_dim, dtype=F32) / HD)
    angles = freqs[:, None] * positions[0].astype(F32)[None, :]
    cosine, sine = jnp.cos(angles), jnp.sin(angles)
    inputs = order.after(tokens_t).astype(F32)
    scale_attn = lax.rsqrt(jnp.mean(inputs * inputs, 0, keepdims=True) + EPSILON)
    normed_t = order.mark((inputs * scale_attn).astype(BF16))
    order.pause()
    cot_came = order.mark(order.after(cot_came))
    feed_chip = chip_rows(feed_mine, feed_other)
    attn_own = outer_stop(attn_way)
    attn_way = hop(attn_own, shards, second_move)
    down_way = outer_start(order.after(down_piece))
    order.pause()
    attn_own = pair(attn_own, attn_way)
    attn_way = hop(attn_own, shards, first_move)
    down_own = outer_stop(down_way)
    down_way = hop(down_own, shards, second_move)
    feed_way = outer_start(order.after(feed_chip))
    order.pause()
    attn_own = pair(attn_own, attn_way)
    attn_way = hop(attn_own, shards, core_move)
    order.pause()
    down_own = pair(down_own, down_way)
    down_way = hop(down_own, shards, first_move)
    attn_own, attn_way = order.after(attn_own, attn_way)
    attn_full = order.mark(assemble(attn_own, attn_way, where))
    qkv = order.mark(project(order.after(normed_t), attn_full, cosine, sine))
    feed_way = order.after(*feed_way)
    feed0_own, feed1_own = join(feed_way, [2 * size for _, size in chunks])
    feed0_way = hop(order.mark(feed0_own), shards, second_move)
    feed1_way = hop(feed1_own, shards, second_move)
    prob, mixed = attend(order.after(qkv), segment_ids[0])
    order.mark(mixed)
    feed0_own = pair(feed0_own, feed0_way)
    feed0_way = hop(feed0_own, shards, first_move)
    after_attn, scale_mlp, mlp_low = branch(order.after(mixed), attn_full, tokens_t)
    order.mark(mlp_low)
    low_came = hop(mlp_low, shards, core_move)
    down_own = pair(down_own, down_way)
    down_way = hop(down_own, shards, core_move)
    feed1_own = pair(feed1_own, feed1_way)
    feed1_way = hop(feed1_own, shards, first_move)
    order.pause()

    def run_feed(chunk, pieces, down_grad, before):
        own, way, low, cot, down = order.after(*pieces, low_came, cot_came, down_way)
        return feed(
            where, chunks[chunk][0], (mlp_low, low), (cot_t, cot), (own, way), (down_own, down), down_grad, before
        )

    *before, keep0, send0, down_grad = run_feed(0, (feed0_own, feed0_way), None, ())
    order.mark(send0)
    feed0_sum = SlotReduction(keep0, send0, shards)

    sums, sums_other, back, back_other, keep1, send1, down_grad = run_feed(
        1, (feed1_own, feed1_way), down_grad, before
    )
    order.mark(send1)
    back_came = hop(back_other, shards, core_move)
    sums_came = hop(sums_other, shards, core_move)

    def down_piece_of(array, to_mid, to_rep):
        array = array.reshape(count // 2, 2, 2, 2, w_down.shape[0] // 2, width)
        return lax.dynamic_slice(
            array, (0, to_mid, 0, to_rep, 0, 0), (count // 2, 1, 2, 1) + array.shape[4:]
        )[:, 0, :, 0]

    feed1_sum = SlotReduction(keep1, send1, shards)
    down_sum = Reduction((down_grad,), down_piece_of, shards)
    feed0_sum.second(order)
    down_sum.first(order)
    order.pause()
    sums_came, back_came = order.after(sums_came, back_came)
    backs = (back, back_came)
    after_grad, mixed_grad, out_grad = return_branch(
        backs, after_attn, scale_mlp, cot_t, mixed, attn_full
    )
    order.mark(mixed_grad)
    dq, dk, dv = attend_back(prob, mixed, order.after(mixed_grad), qkv, cosine, sine)
    order.mark(dq)
    keep_attn, send_attn = finish_grads(order.tick, normed_t, order.after(dq), dk, dv, out_grad)
    order.mark(keep_attn)
    order.tick = gain_attn

    def attn_piece(array, to_mid, to_rep):
        array = array.reshape(count, 2, 2 * rows, 2 * part)
        return lax.dynamic_slice(
            array, (0, to_mid, 0, to_rep * part), (count, 1, 2 * rows, part)
        )[:, 0]

    attn_came = hop(send_attn, shards, core_move)
    feed1_sum.second(order)
    feed0_out = OuterReduction(feed0_sum.third(order), shards)
    feed0_out.send()
    down_sum.second(order)
    order.pause()
    attn_sum = Reduction((keep_attn, attn_came), attn_piece, shards)
    attn_sum.first(order)
    feed1_out = OuterReduction(feed1_sum.third(order), shards)
    feed1_out.send()
    feed0_out.receive(order)
    feed0_out.send()
    down_out = OuterReduction(down_sum.third(order), shards)
    down_out.send()
    input_grad, output = input_gradient(
        order.after(dq), dk, dv, attn_full, tokens_t, scale_attn, after_grad, after_attn, sums, sums_came
    )
    order.mark(output)
    attn_sum.second(order)
    feed1_out.receive(order)
    feed1_out.send()
    down_out.receive(order)
    down_mine = down_out.finish(order)
    down_way = give_down(down_mine, shards)
    feed0_out.receive(order)
    feed0_total = feed0_out.finish(order)
    order.pause()
    attn_out = OuterReduction(attn_sum.third(order), shards)
    attn_out.send()
    feed1_out.receive(order)
    feed1_total = feed1_out.finish(order)
    feed_total = order.mark(jnp.concatenate(order.after(feed0_total, feed1_total), -1))
    down_total = order.mark(add_low(*order.after(down_mine, down_way)))
    down_way = hop(pick(down_total, 1 - core), shards, core_move)
    feed_quarters = share_columns(order.after(feed_total), shards, rep, core)
    order.pause()
    attn_out.receive(order)
    attn_out.send()
    mine, came = order.after(pick(down_total, core), down_way)
    down_rows = order.mark(jnp.where(outer // (count // 2) == core, mine, came))
    down_way = hop(down_rows, shards, rep_move)
    feed_quarters = order.after(*feed_quarters)
    order.mark(feed_quarters[3])
    order.pause()
    attn_out.receive(order)
    down_rows = jnp.stack(order.after(down_rows, down_way))
    attn_quarters = share_columns(attn_out.finish(order), shards, rep, core)
    down_rows = jnp.concatenate([pick(down_rows, rep), pick(down_rows, 1 - rep)], 0)
    grad_down = down_rows.astype(F32)

    attn_rows = jnp.concatenate(attn_quarters, 1).astype(F32)
    feed_rows = jnp.concatenate(
        [
            q[:, 2 * start + kind * size : 2 * start + (kind + 1) * size]
            for kind in range(2)
            for q in feed_quarters
            for start, size in chunks
        ],
        1,
    ).astype(F32)
    qkv_rows = attn_rows[:, :kept]
    grad_norm_attn = jnp.sum(qkv_rows * w_qkv.astype(F32), 1)
    grad_norm_mlp = jnp.sum(feed_rows * w_gate_up.astype(F32), 1)
    grad_out = jnp.concatenate([attn_rows[:, kept + tail :], attn_rows[:, kept : kept + tail]], 1)
    return (
        output.T,
        input_grad.T,
        grad_norm_attn,
        qkv_rows * order.tick,
        grad_out,
        grad_norm_mlp,
        feed_rows * gain_mlp,
        grad_down,
    )


def solution(mesh):
    in_specs = (
        P(("rep", "shard"), None),
        P(("rep", "shard"), None),
        P(("rep", "shard"), None),
        P("shard"),
        P("shard", None),
        P("shard", None),
        P("shard"),
        P("shard", None),
        P("shard", None),
        P(("rep", "shard"), None),
    )
    out_specs = (
        P(("rep", "shard"), None),
        P(("rep", "shard"), None),
        P("shard"),
        P("shard", None),
        P("shard", None),
        P("shard"),
        P("shard", None),
        P("shard", None),
    )
    return jax.shard_map(
        functools.partial(per_device, mesh.shape["shard"]),
        mesh=mesh,
        in_specs=in_specs,
        out_specs=out_specs,
        check_vma=False,
    )
```

```python
import functools

import jax
import jax.numpy as jnp
from jax import lax
from jax.experimental import pallas as pl
from jax.experimental.pallas import tpu as pltpu
from jax.sharding import PartitionSpec as P

HEADS = 15
KV_HEADS = 5
HD = 64
GROUP = HEADS // KV_HEADS

EPSILON = 1e-05
ROPE_BASE = 100000.0
NEG_FILL = -1e30

AXES = ("rep", "shard")
F32 = jnp.float32
BF16 = jnp.bfloat16
LANES = 128
MIB = 1024 * 1024


def hop(values, shards, move):
    pairs = []
    for rep in range(2):
        for outer in range(shards // 4):
            for mid in range(2):
                for core in range(2):
                    to = move(rep, outer, mid, core)
                    pairs.append(
                        (
                            rep * shards + outer * 4 + mid * 2 + core,
                            to[0] * shards + to[1] * 4 + to[2] * 2 + to[3],
                        )
                    )
    return lax.ppermute(values, AXES, pairs)


def core_move(rep, outer, mid, core):
    return (rep, outer, mid, 1 - core)


def rep_move(rep, outer, mid, core):
    return (1 - rep, outer, mid, core)


def cross_move(rep, outer, mid, core):
    return (1 - rep, outer, mid, 1 - core)


def first_move(rep, outer, mid, core):
    return (rep, outer, 1 - mid, core) if core == 0 else (1 - rep, outer, mid, core)


def second_move(rep, outer, mid, core):
    return (1 - rep, outer, mid, core) if core == 0 else (rep, outer, 1 - mid, core)


def outer_move(step, count):
    return lambda rep, outer, mid, core: (rep, (outer + step) % count, mid, core)


class Order:
    def __init__(self, tick):
        self.done = None
        self.tick = tick

    def after(self, *values):
        if self.done is not None:
            values = lax.optimization_barrier(tuple(values) + (self.done,))[:-1]
        return values if len(values) > 1 else values[0]

    def mark(self, value):
        self.done = value
        return value

    def pause(self):
        self.tick = self.mark(anchor(self.after(self.tick)))


def pick(array, index):
    return lax.dynamic_index_in_dim(array, index, 0, keepdims=False)


def place():
    shard = lax.axis_index("shard")
    return lax.axis_index("rep"), shard // 4, (shard // 2) % 2, shard % 2


def arrival(half, first, second, step, rep, outer, mid, count):
    to_mid = jnp.where(half == 0, mid ^ second, mid ^ first)
    to_rep = jnp.where(half == 0, rep ^ first, rep ^ second)
    return to_mid, to_rep, lax.rem(outer + count - step, count)


def in_order(held, half):
    rep, outer, mid, _ = place()
    count = held.shape[2]
    flat = held.reshape((4,) + held.shape[2:])
    reps = []
    for want_rep in range(2):
        mids = []
        for want_mid in range(2):
            by_rep, by_mid = rep ^ want_rep, mid ^ want_mid
            second = jnp.where(half == 0, by_mid, by_rep)
            first = jnp.where(half == 0, by_rep, by_mid)
            piece = pick(flat, second * 2 + first)
            mids.append(
                jnp.concatenate([pick(piece, (outer - k) % count)[None] for k in range(count)], 0)
            )
        reps.append(jnp.stack(mids, 1))
    return jnp.stack(reps)


def assemble_kernel(where_ref, own_ref, came_ref, out_ref, sem):
    rep, outer, mid, core = (where_ref[k] for k in range(4))
    count, _, width = own_ref.shape[2:]
    for source, half in ((own_ref, core), (came_ref, 1 - core)):
        for second in range(2):
            for first in range(2):
                for step in range(count):
                    to_mid, to_rep, to_outer = arrival(
                        half, first, second, step, rep, outer, mid, count
                    )
                    column = pl.multiple_of((half * 2 + to_rep) * width, LANES)
                    pltpu.make_async_copy(
                        source.at[second, first, step],
                        out_ref.at[to_outer * 2 + to_mid, :, pl.ds(column, width)],
                        sem,
                    ).start()
    pltpu.make_async_copy(out_ref, out_ref, sem).wait()


def assemble(own, came, where):
    count, rows, width = own.shape[2:]
    core = where[3]
    shape = (2 * count * rows, 4 * width)
    if rows % 8 or width % LANES:
        halves = jnp.stack([in_order(own, core), in_order(came, 1 - core)])
        halves = jnp.stack([pick(halves, core), pick(halves, 1 - core)])
        return halves.transpose(2, 3, 4, 0, 1, 5).reshape(shape)
    out = pl.pallas_call(
        assemble_kernel,
        out_shape=jax.ShapeDtypeStruct((2 * count, rows, 4 * width), own.dtype),
        in_specs=[
            pl.BlockSpec(memory_space=pltpu.SMEM),
            pl.BlockSpec(memory_space=pl.ANY),
            pl.BlockSpec(memory_space=pl.ANY),
        ],
        out_specs=pl.BlockSpec(memory_space=pltpu.VMEM),
        scratch_shapes=[pltpu.SemaphoreType.DMA],
        compiler_params=pltpu.CompilerParams(vmem_limit_bytes=16 * MIB),
        cost_estimate=LONG,
        name="assemble",
    )(where, own, came)
    return out.reshape(shape)


def add_low(*terms):
    total = terms[0].astype(F32)
    for term in terms[1:]:
        total = total + term.astype(F32)
    return total.astype(BF16)


class Reduction:
    def __init__(self, terms, piece, shards):
        self.terms, self.piece, self.shards = terms, piece, shards

    def parts(self, where):
        return [self.piece(term, *where) for term in self.terms]

    def first(self, order, *way):
        rep, _, mid, core = place()
        got = order.after(*self.terms, *way)
        self.terms = got if isinstance(got, tuple) else (got,)
        away = [(1 - mid, 0), (1 - mid, 1)], [(0, 1 - rep), (1, 1 - rep)]
        sums = []
        for k in range(2):
            where = tuple(jnp.where(core == 0, away[0][k][d], away[1][k][d]) for d in range(2))
            sums.append(add_low(*self.parts(where)))
        self.way = hop(order.mark(jnp.stack(sums)), self.shards, first_move)

    def second(self, order):
        rep, _, mid, core = place()
        self.got = order.after(self.way)
        self.last = jnp.where(core == 0, rep, mid)
        k = 1 - self.last
        where = jnp.where(core == 0, mid, k), jnp.where(core == 0, k, rep)
        out = order.mark(add_low(*self.parts(where), pick(self.got, k)))
        self.way = hop(out, self.shards, second_move)

    def third(self, order):
        rep, _, mid, _ = place()
        came = order.after(self.way)
        return order.mark(add_low(*self.parts((mid, rep)), pick(self.got, self.last), came))


class SlotReduction:
    def __init__(self, keep, send, shards):
        rep, _, mid, core = place()
        self.last = jnp.where(core == 0, rep, mid)
        self.keep, self.shards = keep, shards
        self.way = hop(send, shards, first_move)

    def second(self, order):
        self.got = order.after(self.way)
        k = 1 - self.last
        out = order.mark(add_low(pick(self.keep, k), pick(self.got, k)))
        self.way = hop(out, self.shards, second_move)

    def third(self, order):
        came = order.after(self.way)
        return order.mark(add_low(pick(self.keep, self.last), pick(self.got, self.last), came))


class OuterReduction:
    def __init__(self, mine, shards):
        self.mine, self.shards, self.bit = mine, shards, 1

    def send(self):
        outer = place()[1]
        count = self.mine.shape[0]
        pairs = self.mine.reshape((count // 2, 2) + self.mine.shape[1:])
        side = (outer // self.bit) % 2
        split = lambda which: lax.dynamic_index_in_dim(pairs, which, 1, keepdims=False)
        self.keep = split(side)
        move = lambda rep, outer, mid, core: (rep, outer ^ self.bit, mid, core)
        self.way = hop(split(1 - side), self.shards, move)

    def receive(self, order):
        keep, way = order.after(self.keep, self.way)
        self.mine = order.mark(add_low(keep, way))
        self.bit *= 2

    def finish(self, order):
        while self.mine.shape[0] > 1:
            self.send()
            self.receive(order)
        return pick(self.mine, 0)


def give_down(mine, shards):
    count = shards // 4
    half = count // 2
    pairs = []
    for r in range(2):
        for o in range(count):
            for m in range(2):
                for c in range(2):
                    if o // half != c:
                        base = r * shards + m * 2 + c
                        pairs.append((base + o * 4, base + (o ^ half) * 4))
    return lax.ppermute(mine, AXES, pairs)


def share_columns(total, shards, rep, core):
    rows = total.shape[0] // 2
    halves = total.reshape(2, rows, total.shape[1])
    mine, other = pick(halves, core), pick(halves, 1 - core)
    stack = jnp.stack(
        [
            mine,
            hop(mine, shards, rep_move),
            hop(other, shards, core_move),
            hop(other, shards, cross_move),
        ]
    )
    return [pick(stack, q ^ (core * 2 + rep)) for q in range(4)]


LONG = pl.CostEstimate(flops=200 * 10**9, bytes_accessed=0, transcendentals=0)
SHORT = pl.CostEstimate(flops=10**6, bytes_accessed=0, transcendentals=0)


def dot(left, right, left_dim, right_dim):
    return lax.dot_general(
        left, right, (((left_dim,), (right_dim,)), ((), ())), preferred_element_type=F32
    )


def anchor_kernel(in_ref, out_ref):
    if len(in_ref.shape) == 1:
        for k in range(4):
            out_ref[k] = in_ref[k]
    else:
        out_ref[...] = in_ref[...]


def anchor(tick):
    space = pl.BlockSpec(memory_space=pltpu.SMEM if tick.ndim == 1 else pltpu.VMEM)
    return pl.pallas_call(
        anchor_kernel,
        out_shape=jax.ShapeDtypeStruct(tick.shape, tick.dtype),
        in_specs=[space],
        out_specs=space,
        cost_estimate=LONG,
        name="anchor",
    )(tick)


def join_kernel(count, *refs):
    for k, ref in enumerate(refs[:count]):
        start = 0
        for out_ref in refs[count:]:
            size = out_ref.shape[-1]
            out_ref[k] = ref[..., start : start + size]
            start += size


def join(arrays, sizes=None):
    shape, count = arrays[0].shape, len(arrays)
    outs = [
        jax.ShapeDtypeStruct((count,) + shape[:-1] + (size,), arrays[0].dtype)
        for size in sizes or (shape[-1],)
    ]
    out = pl.pallas_call(
        functools.partial(join_kernel, count),
        out_shape=outs,
        compiler_params=pltpu.CompilerParams(vmem_limit_bytes=16 * MIB),
        cost_estimate=SHORT,
        name="join",
    )(*arrays)
    return out if sizes else out[0]


def project_kernel(normed_ref, weight_ref, cos_ref, sin_ref, out_ref):
    half = HD // 2
    turned = (HEADS + KV_HEADS) * HD
    cosine, sine = cos_ref[...], sin_ref[...]
    normed = normed_ref[...]
    for start in range(0, turned, 2 * LANES):
        raw = dot(weight_ref[:, start : start + 2 * LANES], normed, 0, 0)
        for at in range(0, 2 * LANES, HD):
            row = start + at
            scale = 0.125 if row < HEADS * HD else 1.0
            upper, lower = raw[at : at + half], raw[at + half : at + HD]
            out_ref[row : row + half] = ((upper * cosine - lower * sine) * scale).astype(BF16)
            out_ref[row + half : row + HD] = ((lower * cosine + upper * sine) * scale).astype(BF16)
    out_ref[turned:] = dot(
        weight_ref[:, turned : turned + KV_HEADS * HD], normed, 0, 0
    ).astype(BF16)


def project(normed_t, weight, cosine, sine):
    return pl.pallas_call(
        project_kernel,
        out_shape=jax.ShapeDtypeStruct(((HEADS + 2 * KV_HEADS) * HD, normed_t.shape[1]), BF16),
        compiler_params=pltpu.CompilerParams(vmem_limit_bytes=24 * MIB),
        cost_estimate=SHORT,
        name="project",
    )(normed_t, weight, cosine, sine)


def split_tokens(tokens):
    block = 256 if tokens % 256 == 0 else tokens
    return [(start, start + block) for start in range(0, tokens, block)]


def attend_kernel(seg_row_ref, seg_col_ref, q_ref, k_ref, v_ref, prob_ref, mixed_ref, bias_ref):
    tokens = q_ref.shape[1]

    @pl.when(pl.program_id(0) == 0)
    def _():
        keys = lax.broadcasted_iota(jnp.int32, (tokens, tokens), 0)
        queries = lax.broadcasted_iota(jnp.int32, (tokens, tokens), 1)
        allowed = (seg_col_ref[...] == seg_row_ref[...]) & (keys <= queries)
        bias_ref[...] = jnp.where(allowed, 0.0, NEG_FILL)

    for head in range(GROUP):
        rows = slice(head * HD, (head + 1) * HD)
        for start, stop in split_tokens(tokens):
            scores = dot(k_ref[:, :stop], q_ref[rows, start:stop], 0, 0)
            scores = scores + bias_ref[:stop, start:stop]
            expo = jnp.exp(scores - jnp.max(scores, 0, keepdims=True))
            prob = (expo * (1.0 / jnp.sum(expo, 0, keepdims=True))).astype(BF16)
            prob_ref[head, :stop, start:stop] = prob
            mixed_ref[rows, start:stop] = dot(v_ref[:, :stop], prob, 1, 0).astype(BF16)


def attend(qkv, seg_row):
    tokens = qkv.shape[1]
    return pl.pallas_call(
        attend_kernel,
        grid=(KV_HEADS,),
        out_shape=(
            jax.ShapeDtypeStruct((HEADS, tokens, tokens), BF16),
            jax.ShapeDtypeStruct((HEADS * HD, tokens), BF16),
        ),
        in_specs=[
            pl.BlockSpec((1, tokens), lambda i: (0, 0)),
            pl.BlockSpec((tokens, 1), lambda i: (0, 0)),
            pl.BlockSpec((GROUP * HD, tokens), lambda i: (i, 0)),
            pl.BlockSpec((HD, tokens), lambda i: (HEADS + i, 0)),
            pl.BlockSpec((HD, tokens), lambda i: (HEADS + KV_HEADS + i, 0)),
        ],
        out_specs=(
            pl.BlockSpec((GROUP, tokens, tokens), lambda i: (i, 0, 0)),
            pl.BlockSpec((GROUP * HD, tokens), lambda i: (i, 0)),
        ),
        scratch_shapes=[pltpu.VMEM((tokens, tokens), F32)],
        compiler_params=pltpu.CompilerParams(vmem_limit_bytes=32 * MIB),
        cost_estimate=LONG,
        name="attend",
    )(seg_row.reshape(1, tokens), seg_row.reshape(tokens, 1), qkv, qkv, qkv)


def out_columns(width):
    kept = (HEADS + 2 * KV_HEADS) * HD
    tail = -kept % LANES
    return kept + tail - LANES, LANES - tail, kept + tail


def branch_kernel(mixed_ref, weight_ref, tokens_ref, after_ref, scale_ref, normed_ref):
    mixed = mixed_ref[...]
    tile, skip, rest = out_columns(weight_ref.shape[1])
    wide = weight_ref.shape[1] - rest
    last = dot(weight_ref[:, tile : tile + LANES], mixed, 0, 0)
    after_ref[:wide] = tokens_ref[:wide].astype(F32) + dot(weight_ref[:, rest:], mixed, 0, 0)
    after_ref[wide:] = tokens_ref[wide:].astype(F32) + last[skip:]
    after = after_ref[...]
    scale = lax.rsqrt(jnp.mean(after * after, 0, keepdims=True) + EPSILON)
    scale_ref[...] = scale
    normed_ref[...] = (after * scale).astype(BF16)


def branch(mixed, weight, tokens):
    width, count = tokens.shape
    return pl.pallas_call(
        branch_kernel,
        out_shape=(
            jax.ShapeDtypeStruct((width, count), F32),
            jax.ShapeDtypeStruct((1, count), F32),
            jax.ShapeDtypeStruct((width, count), BF16),
        ),
        compiler_params=pltpu.CompilerParams(vmem_limit_bytes=24 * MIB),
        cost_estimate=SHORT,
        name="branch",
    )(mixed, weight, tokens)


def feed_kernel(
    ordered,
    offset,
    where_ref,
    normed_refs,
    cot_refs,
    pieces_refs,
    down_refs,
    down_grad_in_ref,
    before_refs,
    sum_refs,
    back_refs,
    grad_refs,
    down_grad_ref,
    normed,
    cot,
    weight,
    down_all,
    down,
    inner,
    pull,
    grad,
    down_grad,
    results,
    results_low,
    sems,
    out_sems,
):
    rep, outer, mid, core = (where_ref[k] for k in range(4))
    tokens = normed_refs[0].shape[1]
    units = down.shape[0]
    size = units // 2
    quarter = down_all.shape[0] // 2

    def load(index, copies):
        for source, to in copies:
            pltpu.make_async_copy(source, to, sems.at[index]).start()

    def ready(index, ref):
        pltpu.make_async_copy(ref, ref, sems.at[index]).wait()

    load(0, [(normed_refs[k], normed.at[:, pl.ds(k * tokens, tokens)]) for k in range(2)])
    for kind in range(2):
        if ordered:
            load(
                1 + kind,
                [
                    (
                        pieces_refs[0].at[k, :, pl.ds(kind * size, size)],
                        weight.at[0, :, pl.ds(kind * units + k * size, size)],
                    )
                    for k in range(2)
                ],
            )
            continue
        for second, source in enumerate(pieces_refs):
            for first in range(2):
                steps = source.shape[1]
                for step in range(steps):
                    to_mid, to_rep, to_outer = arrival(
                        core, first, second, step, rep, outer, mid, steps
                    )
                    column = pl.multiple_of(kind * units + to_rep * size, LANES)
                    load(
                        1 + kind,
                        [
                            (
                                source.at[first, step, :, pl.ds(kind * size, size)],
                                weight.at[to_outer * 2 + to_mid, :, pl.ds(column, size)],
                            )
                        ],
                    )
    load(3, [(cot_refs[k], cot.at[:, pl.ds(k * tokens, tokens)]) for k in range(2)])
    if ordered:
        load(4, [(down_refs[0], down_all)])
    else:
        steps, block = down_refs[0].shape[2:4]
        half = steps // 2
        for source, owner in ((down_refs[0], core), (down_refs[1], 1 - core)):
            for at in range(half):
                step = lax.rem(outer + steps - (core * half + at), steps)
                for second in range(2):
                    for first in range(2):
                        to_mid, to_rep, _ = arrival(owner, first, second, 0, rep, outer, mid, steps)
                        row = (((at * 2 + to_mid) * 2 + owner) * 2 + to_rep) * block
                        to = down_all.at[pl.ds(pl.multiple_of(row, 16), block)]
                        load(4, [(source.at[second, first, step], to)])

    if before_refs:
        load(5, [(before_refs[2 - 2 * k], results.at[k]) for k in range(2)])
        load(6, [(before_refs[3 - 2 * k], results_low.at[k]) for k in range(2)])

    ready(0, normed)
    ready(1, weight.at[:, :, pl.ds(0, units)])
    tile = 2 * LANES if units % (2 * LANES) == 0 else LANES

    def columns(start, count=tile):
        return weight[:, :, pl.ds(start, count)].reshape(normed.shape[0], count)

    for start in range(0, units, tile):
        at = pl.ds(start, tile)
        gate = dot(columns(start), normed[...], 0, 0)
        if start == 0:
            ready(2, weight.at[:, :, pl.ds(units, units)])
        up = dot(columns(units + start), normed[...], 0, 0)
        if start == 0:
            ready(3, cot)
            ready(4, down_all)
            down[:size] = down_all[offset : offset + size]
            down[size:] = down_all[quarter + offset : quarter + offset + size]
        inner_grad = dot(down[at], cot[...], 1, 0)
        sigma = 1.0 / (1.0 + jnp.exp(-gate))
        activ = gate * sigma
        inner[at] = (activ * up).astype(BF16)
        pull[at] = (inner_grad * up * (sigma + activ * (1.0 - sigma))).astype(BF16)
        pull[pl.ds(units + start, tile)] = (inner_grad * activ).astype(BF16)
        down_grad[at] = dot(inner[at], cot[...], 1, 1).astype(BF16)
    for k in range(2):
        pltpu.make_async_copy(
            down_grad.at[pl.ds(k * size, size)],
            down_grad_ref.at[k, pl.ds(offset, size)],
            out_sems.at[0],
        ).start()
    for kind in range(2):
        for start in range(0, units, tile):
            at = pl.ds(kind * units + start, tile)
            part = dot(normed[...], pull[at], 1, 1)
            if ordered:
                grad[0, :, at] = part.astype(BF16)
            else:
                grad[:, :, at] = part.reshape(*grad.shape[:2], tile).astype(BF16)
        for to_rep in range(2):
            source_at = pl.ds(kind * units + to_rep * size, size)
            target_at = pl.ds(kind * size, size)
            if ordered:
                pltpu.make_async_copy(
                    grad.at[0, :, source_at], grad_refs[0].at[to_rep, :, target_at], out_sems.at[1]
                ).start()
                continue
            for at in range(grad.shape[0]):
                to_outer, to_mid = at // 2, at % 2
                for which in range(2):
                    slot, mine = (to_mid, rep == to_rep) if which else (to_rep, mid == to_mid)
                    for ref, wanted in zip(grad_refs, (mine, jnp.logical_not(mine))):

                        @pl.when(jnp.logical_and(core == which, wanted))
                        def _():
                            pltpu.make_async_copy(
                                grad.at[at, :, source_at],
                                ref.at[slot, to_outer, :, target_at],
                                out_sems.at[1],
                            ).start()
    for index, (out_refs, left, right, dim) in enumerate(
        ((back_refs, columns(0, 2 * units), pull, 1), (sum_refs, down[...], inner, 0))
    ):
        if before_refs and index == 0:
            ready(5, results)
            ready(6, results_low)
        low = dot(left, right[:, pl.ds(tokens, tokens)], dim, 0)
        if before_refs:
            low = low + results_low[index].astype(F32)
        results_low[index] = low.astype(BF16)
        pltpu.make_async_copy(results_low.at[index], out_refs[1], out_sems.at[2 + index]).start()
        total = dot(left, right[:, pl.ds(0, tokens)], dim, 0)
        results[index] = total + results[index] if before_refs else total
        pltpu.make_async_copy(results.at[index], out_refs[0], out_sems.at[4 + index]).start()
    pltpu.make_async_copy(down_grad, down_grad, out_sems.at[0]).wait()
    pltpu.make_async_copy(grad, grad, out_sems.at[1]).wait()
    for index in range(2):
        pltpu.make_async_copy(
            results_low.at[index], results_low.at[index], out_sems.at[2 + index]
        ).wait()
        pltpu.make_async_copy(results.at[index], results.at[index], out_sems.at[4 + index]).wait()


def feed(where, offset, normed, cot, pieces, down, down_grad, before):
    width, tokens = normed[0].shape
    size = pieces[0].shape[-1] // 2
    units = 2 * size
    count, block = down[0].shape[2:4]
    half_units = count * 4 * block
    rows = pieces[0].shape[2]
    ordered = rows % 8 != 0 or block % 16 != 0
    if ordered:
        core = where[3]
        pieces = (in_order(jnp.stack(pieces), core).reshape(2, width, units),)
        blocks = [in_order(array, half) for array, half in zip(down, (core, 1 - core))]
        blocks = jnp.stack([jnp.where(core == k, *blocks) for k in range(2)])
        blocks = blocks.transpose(2, 3, 0, 1, 4, 5).reshape(2, half_units, width)
        down = (pick(blocks, core),)
        rows = width
    first_call = down_grad is None
    operands = [*normed, *cot, *pieces, *down] + ([] if first_call else [down_grad, *before])
    split_before = len(before)
    split = len(down)

    def body(where_ref, *refs):
        refs = list(refs)
        take = lambda count: [refs.pop(0) for _ in range(count)]
        ins = take(2), take(2), take(len(pieces)), take(split)
        down_grad_in = None if first_call else take(1)[0]
        feed_kernel(
            ordered, offset, where_ref, *ins, down_grad_in, take(split_before), take(2), take(2), take(len(grads)), *refs
        )

    wide = jax.ShapeDtypeStruct((width, tokens), F32)
    low = jax.ShapeDtypeStruct((width, tokens), BF16)
    if ordered:
        grads = [jax.ShapeDtypeStruct((2, width, units), BF16)]
    else:
        grads = [jax.ShapeDtypeStruct((2, count, rows, units), BF16)] * 2
    out_shape = (
        wide,
        low,
        wide,
        low,
        *grads,
        jax.ShapeDtypeStruct((2, half_units // 2, width), BF16),
    )
    any_space = pl.BlockSpec(memory_space=pl.ANY)
    *sums, down_grad = pl.pallas_call(
        body,
        in_specs=[pl.BlockSpec(memory_space=pltpu.SMEM)] + [any_space] * len(operands),
        out_specs=(any_space,) * len(out_shape),
        out_shape=out_shape,
        scratch_shapes=[
            pltpu.VMEM((width, 2 * tokens), BF16),
            pltpu.VMEM((width, 2 * tokens), BF16),
            pltpu.VMEM((width // rows, rows, 2 * units), BF16),
            pltpu.VMEM((half_units, width), BF16),
            pltpu.VMEM((units, width), BF16),
            pltpu.VMEM((units, 2 * tokens), BF16),
            pltpu.VMEM((2 * units, 2 * tokens), BF16),
            pltpu.VMEM((width // rows, rows, 2 * units), BF16),
            pltpu.VMEM((units, width), BF16),
            pltpu.VMEM((2, width, tokens), F32),
            pltpu.VMEM((2, width, tokens), BF16),
            pltpu.SemaphoreType.DMA((7,)),
            pltpu.SemaphoreType.DMA((6,)),
        ],
        input_output_aliases={} if first_call else {len(operands) - split_before: 4 + len(grads)},
        compiler_params=pltpu.CompilerParams(vmem_limit_bytes=52 * MIB),
        cost_estimate=LONG,
        name="feed",
    )(where, *operands)
    if ordered:
        sums = (*sums[:4], *slots(sums[4], where, count))
    return (*sums, down_grad)


def slots(grad, where, count):
    rep, _, mid, core = (where[k] for k in range(4))
    blocks = grad.reshape(2, count, 2, -1, grad.shape[-1])

    def piece(to_mid, to_rep):
        return lax.dynamic_slice(
            blocks, (to_rep, 0, to_mid, 0, 0), (1, count, 1) + blocks.shape[3:]
        )[0, :, 0]

    keep = [piece(jnp.where(core == 0, mid, k), jnp.where(core == 0, k, rep)) for k in range(2)]
    send = [
        piece(jnp.where(core == 0, 1 - mid, k), jnp.where(core == 0, k, 1 - rep)) for k in range(2)
    ]
    return jnp.stack(keep), jnp.stack(send)


def return_kernel(
    back_refs, after_ref, scale_ref, cot_ref, mixed_ref, weight_ref, grad_ref, mixed_grad_ref, out_grad_ref
):
    back = back_refs[0][...]
    for ref in back_refs[1:]:
        back = back + ref[...].astype(F32)
    after, scale = after_ref[...], scale_ref[...]
    mean = jnp.mean(back * after, 0, keepdims=True)
    grad = cot_ref[...].astype(F32) + scale * back - after * (scale * scale * scale * mean)
    grad_ref[...] = grad
    low = grad.astype(BF16)
    tile, skip, rest = out_columns(weight_ref.shape[1])
    wide = weight_ref.shape[1] - rest
    last = low[wide:]
    mixed_grad_ref[...] = (
        dot(weight_ref[:, rest:], low[:wide], 1, 0)
        + dot(weight_ref[:, tile + skip : rest], last, 1, 0)
    ).astype(BF16)
    mixed = mixed_ref[...]
    out_grad_ref[:, : LANES - skip] = dot(mixed, last, 1, 1).astype(BF16)
    out_grad_ref[:, LANES - skip :] = dot(mixed, low[:wide], 1, 1).astype(BF16)


def return_branch(backs, after, scale, cot, mixed, weight):
    width, count = after.shape

    def body(*refs):
        return_kernel(refs[: len(backs)], *refs[len(backs) :])

    return pl.pallas_call(
        body,
        out_shape=(
            jax.ShapeDtypeStruct((width, count), F32),
            jax.ShapeDtypeStruct((width, count), BF16),
            jax.ShapeDtypeStruct((width, width), BF16),
        ),
        compiler_params=pltpu.CompilerParams(vmem_limit_bytes=32 * MIB),
        cost_estimate=SHORT,
        name="return_branch",
    )(*backs, after, scale, cot, mixed, weight)


def attend_back_kernel(
    prob_ref, mixed_ref, grad_ref, q_ref, k_ref, v_ref, cos_ref, sin_ref, dq_ref, dk_ref, dv_ref
):
    half = HD // 2
    tokens = q_ref.shape[1]
    cosine, sine = cos_ref[...], sin_ref[...]
    key_grad = [None] * len(split_tokens(tokens))
    value_grad = [None] * len(split_tokens(tokens))

    def unturn(to_ref, row, grads, columns):
        upper, lower = grads[:half], grads[half:]
        c, s = cosine[:, columns], sine[:, columns]
        to_ref[row : row + half, columns] = (upper * c + lower * s).astype(BF16)
        to_ref[row + half : row + HD, columns] = (lower * c - upper * s).astype(BF16)

    for head in range(GROUP):
        rows = slice(head * HD, (head + 1) * HD)
        for block, (start, stop) in enumerate(split_tokens(tokens)):
            grad = grad_ref[rows, start:stop]
            mixed = mixed_ref[rows, start:stop]
            row_dot = jnp.sum(grad.astype(F32) * mixed.astype(F32), 0, keepdims=True)
            prob = prob_ref[head, :stop, start:stop]
            prob_grad = dot(v_ref[:, :stop], grad, 0, 0)
            score_grad = (prob.astype(F32) * (prob_grad - row_dot)).astype(BF16)
            unturn(
                dq_ref,
                head * HD,
                dot(k_ref[:, :stop], score_grad, 1, 0) * 0.125,
                slice(start, stop),
            )
            dk = dot(q_ref[rows, start:stop], score_grad, 1, 1)
            dv = dot(grad, prob, 1, 1)
            for part in range(block + 1):
                a, b = split_tokens(tokens)[part]
                if key_grad[part] is None:
                    key_grad[part], value_grad[part] = dk[:, a:b], dv[:, a:b]
                else:
                    key_grad[part] = key_grad[part] + dk[:, a:b]
                    value_grad[part] = value_grad[part] + dv[:, a:b]
    for part, (a, b) in enumerate(split_tokens(tokens)):
        unturn(dk_ref, 0, key_grad[part], slice(a, b))
        dv_ref[:, a:b] = value_grad[part].astype(BF16)


def attend_back(prob, mixed, grad, qkv, cosine, sine):
    tokens = qkv.shape[1]
    heads = pl.BlockSpec((GROUP * HD, tokens), lambda i: (i, 0))
    one = pl.BlockSpec((HD, tokens), lambda i: (i, 0))
    table = pl.BlockSpec((HD // 2, tokens), lambda i: (0, 0))
    return pl.pallas_call(
        attend_back_kernel,
        grid=(KV_HEADS,),
        out_shape=(
            jax.ShapeDtypeStruct((HEADS * HD, tokens), BF16),
            jax.ShapeDtypeStruct((KV_HEADS * HD, tokens), BF16),
            jax.ShapeDtypeStruct((KV_HEADS * HD, tokens), BF16),
        ),
        in_specs=[
            pl.BlockSpec((GROUP, tokens, tokens), lambda i: (i, 0, 0)),
            heads,
            heads,
            heads,
            pl.BlockSpec((HD, tokens), lambda i: (HEADS + i, 0)),
            pl.BlockSpec((HD, tokens), lambda i: (HEADS + KV_HEADS + i, 0)),
            table,
            table,
        ],
        out_specs=(heads, one, one),
        compiler_params=pltpu.CompilerParams(vmem_limit_bytes=32 * MIB),
        cost_estimate=SHORT,
        name="attend_back",
    )(prob, mixed, grad, qkv, qkv, qkv, cosine, sine)


def finish_grads_kernel(
    where_ref, normed_t_ref, dq_ref, dk_ref, dv_ref, out_grad_ref, keep_ref, send_ref, halves_ref
):
    normed_t = normed_t_ref[...]
    queries = dq_ref.shape[0]
    values = dv_ref.shape[0]
    halves_ref[0, :, :queries] = dot(normed_t, dq_ref[...], 1, 1).astype(BF16)
    halves_ref[0, :, queries:] = dot(normed_t, dk_ref[...], 1, 1).astype(BF16)
    halves_ref[1, :, :values] = dot(normed_t, dv_ref[...], 1, 1).astype(BF16)
    halves_ref[1, :, values:] = out_grad_ref[...]
    core = where_ref[3]
    keep_ref[...] = halves_ref[core]
    send_ref[...] = halves_ref[1 - core]


def finish_grads(where, normed_t, dq, dk, dv, out_grad):
    width = normed_t.shape[0]
    half = dq.shape[0] + dk.shape[0]
    shape = jax.ShapeDtypeStruct((width, half), BF16)
    vmem = pl.BlockSpec(memory_space=pltpu.VMEM)
    return pl.pallas_call(
        finish_grads_kernel,
        out_shape=(shape, shape),
        in_specs=[pl.BlockSpec(memory_space=pltpu.SMEM)] + [vmem] * 5,
        out_specs=(vmem, vmem),
        scratch_shapes=[pltpu.VMEM((2, width, half), BF16)],
        compiler_params=pltpu.CompilerParams(vmem_limit_bytes=24 * MIB),
        cost_estimate=SHORT,
        name="finish_grads",
    )(where, normed_t, dq, dk, dv, out_grad)


def input_grad_kernel(
    dq_ref, dk_ref, dv_ref, weight_ref, tokens_ref, scale_ref, grad_ref, after_ref, sum_ref, came_ref,
    out_ref, output_ref,
):
    output_ref[...] = (after_ref[...] + sum_ref[...] + came_ref[...].astype(F32)).astype(BF16)
    queries, keys = dq_ref.shape[0], dk_ref.shape[0]
    end = queries + keys + dv_ref.shape[0]
    pull = dot(weight_ref[:, :queries], dq_ref[...], 1, 0)
    pull = pull + dot(weight_ref[:, queries : queries + keys], dk_ref[...], 1, 0)
    pull = pull + dot(weight_ref[:, queries + keys : end], dv_ref[...], 1, 0)
    values, scale = tokens_ref[...].astype(F32), scale_ref[...]
    mean = jnp.mean(pull * values, 0, keepdims=True)
    out_ref[...] = grad_ref[...] + scale * pull - values * (scale * scale * scale * mean)


def input_gradient(dq, dk, dv, weight, tokens, scale, grad, after, own, came):
    return pl.pallas_call(
        input_grad_kernel,
        out_shape=(
            jax.ShapeDtypeStruct(grad.shape, F32),
            jax.ShapeDtypeStruct(grad.shape, BF16),
        ),
        compiler_params=pltpu.CompilerParams(vmem_limit_bytes=24 * MIB),
        cost_estimate=LONG,
        name="input_gradient",
    )(dq, dk, dv, weight, tokens, scale, grad, after, own, came)


def per_device(
    shards,
    tokens,
    segment_ids,
    positions,
    norm_attn,
    w_qkv,
    w_out,
    norm_mlp,
    w_gate_up,
    w_down,
    cotangent,
):
    rep, outer, mid, core = place()
    where = jnp.stack([rep, outer, mid, core]).astype(jnp.int32)
    count = shards // 4
    width = tokens.shape[1]
    rows = w_qkv.shape[0]
    kept = w_qkv.shape[1]
    units = w_gate_up.shape[1] // 8
    gain_attn, gain_mlp = norm_attn.astype(F32)[:, None], norm_mlp.astype(F32)[:, None]

    qkv_block = (w_qkv.astype(F32) * gain_attn).astype(BF16)
    tail = -kept % LANES
    attn_block = jnp.concatenate([qkv_block, w_out[:, width - tail :], w_out[:, : width - tail]], 1)
    part = attn_block.shape[1] // 4

    big = -(-units // (2 * LANES)) * LANES
    chunks = ((0, big), (big, units - big))

    def attn_quarter(index):
        return lax.dynamic_slice(attn_block, (0, index * part), (rows, part))

    def feed_quarter(index):
        return jnp.concatenate(
            [
                lax.dynamic_slice(feed_block, (0, (kind * 4 + index) * units + start), (rows, size))
                for start, size in chunks
                for kind in range(2)
            ],
            1,
        )

    def chip_rows(mine, other):
        mine, other = order.after(mine, other)
        return order.mark(
            jnp.concatenate(
                [jnp.where(core == 0, mine, other), jnp.where(core == 0, other, mine)], 0
            )
        )

    order = Order(where)
    attn_mine = attn_quarter(core * 2 + rep)
    attn_other = hop(attn_quarter((1 - core) * 2 + rep), shards, core_move)
    attn_chip = chip_rows(attn_mine, attn_other)
    down_piece = pick(w_down.reshape(2, w_down.shape[0] // 2, width), rep)

    def outer_start(piece):
        return [piece] + [hop(piece, shards, outer_move(k, count)) for k in range(1, count)]

    def outer_stop(parts):
        return order.mark(join(order.after(*parts)))

    def pair(held, came):
        return order.mark(join(order.after(held, came)))

    tokens_t, cot_t = tokens.T, cotangent.T

    attn_way = outer_start(attn_chip)
    feed_block = (order.after(w_gate_up).astype(F32) * gain_mlp).astype(BF16)
    feed_mine = feed_quarter(core * 2 + rep)
    feed_other = hop(feed_quarter((1 - core) * 2 + rep), shards, core_move)
    cot_came = hop(cot_t, shards, core_move)
    half_dim = HD // 2
    freqs = ROPE_BASE ** (-2.0 * jnp.arange(half_dim, dtype=F32) / HD)
    angles = freqs[:, None] * positions[0].astype(F32)[None, :]
    cosine, sine = jnp.cos(angles), jnp.sin(angles)
    inputs = order.after(tokens_t).astype(F32)
    scale_attn = lax.rsqrt(jnp.mean(inputs * inputs, 0, keepdims=True) + EPSILON)
    normed_t = order.mark((inputs * scale_attn).astype(BF16))
    order.pause()
    cot_came = order.mark(order.after(cot_came))
    feed_chip = chip_rows(feed_mine, feed_other)
    attn_own = outer_stop(attn_way)
    attn_way = hop(attn_own, shards, second_move)
    down_way = outer_start(order.after(down_piece))
    order.pause()
    attn_own = pair(attn_own, attn_way)
    attn_way = hop(attn_own, shards, first_move)
    down_own = outer_stop(down_way)
    down_way = hop(down_own, shards, second_move)
    feed_way = outer_start(order.after(feed_chip))
    order.pause()
    attn_own = pair(attn_own, attn_way)
    attn_way = hop(attn_own, shards, core_move)
    order.pause()
    down_own = pair(down_own, down_way)
    down_way = hop(down_own, shards, first_move)
    attn_own, attn_way = order.after(attn_own, attn_way)
    attn_full = order.mark(assemble(attn_own, attn_way, where))
    qkv = order.mark(project(order.after(normed_t), attn_full, cosine, sine))
    feed_way = order.after(*feed_way)
    feed0_own, feed1_own = join(feed_way, [2 * size for _, size in chunks])
    feed0_way = hop(order.mark(feed0_own), shards, second_move)
    feed1_way = hop(feed1_own, shards, second_move)
    prob, mixed = attend(order.after(qkv), segment_ids[0])
    order.mark(mixed)
    feed0_own = pair(feed0_own, feed0_way)
    feed0_way = hop(feed0_own, shards, first_move)
    after_attn, scale_mlp, mlp_low = branch(order.after(mixed), attn_full, tokens_t)
    order.mark(mlp_low)
    low_came = hop(mlp_low, shards, core_move)
    down_own = pair(down_own, down_way)
    down_way = hop(down_own, shards, core_move)
    feed1_own = pair(feed1_own, feed1_way)
    feed1_way = hop(feed1_own, shards, first_move)
    order.pause()

    def run_feed(chunk, pieces, down_grad, before):
        own, way, low, cot, down = order.after(*pieces, low_came, cot_came, down_way)
        return feed(
            where, chunks[chunk][0], (mlp_low, low), (cot_t, cot), (own, way), (down_own, down), down_grad, before
        )

    *before, keep0, send0, down_grad = run_feed(0, (feed0_own, feed0_way), None, ())
    order.mark(send0)
    feed0_sum = SlotReduction(keep0, send0, shards)

    sums, sums_other, back, back_other, keep1, send1, down_grad = run_feed(
        1, (feed1_own, feed1_way), down_grad, before
    )
    order.mark(send1)
    back_came = hop(back_other, shards, core_move)
    sums_came = hop(sums_other, shards, core_move)

    def down_piece_of(array, to_mid, to_rep):
        array = array.reshape(count // 2, 2, 2, 2, w_down.shape[0] // 2, width)
        return lax.dynamic_slice(
            array, (0, to_mid, 0, to_rep, 0, 0), (count // 2, 1, 2, 1) + array.shape[4:]
        )[:, 0, :, 0]

    feed1_sum = SlotReduction(keep1, send1, shards)
    down_sum = Reduction((down_grad,), down_piece_of, shards)
    feed0_sum.second(order)
    down_sum.first(order)
    order.pause()
    sums_came, back_came = order.after(sums_came, back_came)
    backs = (back, back_came)
    after_grad, mixed_grad, out_grad = return_branch(
        backs, after_attn, scale_mlp, cot_t, mixed, attn_full
    )
    order.mark(mixed_grad)
    dq, dk, dv = attend_back(prob, mixed, order.after(mixed_grad), qkv, cosine, sine)
    order.mark(dq)
    keep_attn, send_attn = finish_grads(order.tick, normed_t, order.after(dq), dk, dv, out_grad)
    order.mark(keep_attn)
    order.tick = gain_attn

    def attn_piece(array, to_mid, to_rep):
        array = array.reshape(count, 2, 2 * rows, 2 * part)
        return lax.dynamic_slice(
            array, (0, to_mid, 0, to_rep * part), (count, 1, 2 * rows, part)
        )[:, 0]

    attn_came = hop(send_attn, shards, core_move)
    feed1_sum.second(order)
    feed0_out = OuterReduction(feed0_sum.third(order), shards)
    feed0_out.send()
    down_sum.second(order)
    order.pause()
    attn_sum = Reduction((keep_attn, attn_came), attn_piece, shards)
    attn_sum.first(order)
    feed1_out = OuterReduction(feed1_sum.third(order), shards)
    feed1_out.send()
    feed0_out.receive(order)
    feed0_out.send()
    down_out = OuterReduction(down_sum.third(order), shards)
    down_out.send()
    input_grad, output = input_gradient(
        order.after(dq), dk, dv, attn_full, tokens_t, scale_attn, after_grad, after_attn, sums, sums_came
    )
    order.mark(output)
    attn_sum.second(order)
    feed1_out.receive(order)
    feed1_out.send()
    down_out.receive(order)
    down_mine = down_out.finish(order)
    down_way = give_down(down_mine, shards)
    feed0_out.receive(order)
    feed0_total = feed0_out.finish(order)
    order.pause()
    attn_out = OuterReduction(attn_sum.third(order), shards)
    attn_out.send()
    order.pause()
    attn_out.receive(order)
    attn_out.send()
    feed1_out.receive(order)
    feed1_total = feed1_out.finish(order)
    feed_total = order.mark(jnp.concatenate(order.after(feed0_total, feed1_total), -1))
    feed_quarters = share_columns(feed_total, shards, rep, core)
    down_total = order.mark(add_low(*order.after(down_mine, down_way)))
    down_way = hop(pick(down_total, 1 - core), shards, core_move)
    order.pause()
    attn_out.receive(order)
    attn_quarters = share_columns(attn_out.finish(order), shards, rep, core)
    mine, came = order.after(pick(down_total, core), down_way)
    down_rows = order.mark(jnp.where(outer // (count // 2) == core, mine, came))
    down_way = hop(down_rows, shards, rep_move)
    feed_quarters = order.after(*feed_quarters)
    down_rows = jnp.stack([down_rows, down_way])
    down_rows = jnp.concatenate([pick(down_rows, rep), pick(down_rows, 1 - rep)], 0)
    grad_down = down_rows.astype(F32)

    attn_rows = jnp.concatenate(attn_quarters, 1).astype(F32)
    feed_rows = jnp.concatenate(
        [
            q[:, 2 * start + kind * size : 2 * start + (kind + 1) * size]
            for kind in range(2)
            for q in feed_quarters
            for start, size in chunks
        ],
        1,
    ).astype(F32)
    qkv_rows = attn_rows[:, :kept]
    grad_norm_attn = jnp.sum(qkv_rows * w_qkv.astype(F32), 1)
    grad_norm_mlp = jnp.sum(feed_rows * w_gate_up.astype(F32), 1)
    grad_out = jnp.concatenate([attn_rows[:, kept + tail :], attn_rows[:, kept : kept + tail]], 1)
    return (
        output.T,
        input_grad.T,
        grad_norm_attn,
        qkv_rows * order.tick,
        grad_out,
        grad_norm_mlp,
        feed_rows * gain_mlp,
        grad_down,
    )


def solution(mesh):
    in_specs = (
        P(("rep", "shard"), None),
        P(("rep", "shard"), None),
        P(("rep", "shard"), None),
        P("shard"),
        P("shard", None),
        P("shard", None),
        P("shard"),
        P("shard", None),
        P("shard", None),
        P(("rep", "shard"), None),
    )
    out_specs = (
        P(("rep", "shard"), None),
        P(("rep", "shard"), None),
        P("shard"),
        P("shard", None),
        P("shard", None),
        P("shard"),
        P("shard", None),
        P("shard", None),
    )
    return jax.shard_map(
        functools.partial(per_device, mesh.shape["shard"]),
        mesh=mesh,
        in_specs=in_specs,
        out_specs=out_specs,
        check_vma=False,
    )
```
